32 devices in a mesh: row: 8 (over z, x), col: 4 (over y, core).
Axes of the slice: x: 2, y: 2, z: 4, core: 2. Of those that a mesh axis runs over, the one named last changes fastest.
Arguments:
- leaf_mass: bfloat16 [32, 2048, 2048], P(('row', 'col')), as said below
- tile_mask: int32 [32, 16, 16], P(('row', 'col')), may hold values from 0 to 1, as said below
- constraint_modes: bfloat16 [32, 2048, 1024], P(('row', 'col')), may hold values from -0.125 to 0.125
- leaf_fixed_modes: bfloat16 [32, 2048, 128], P(('row', 'col')), may hold values from -6 to 6
- block_map: int32 [32, 2, 4], P(('row', 'col')), may hold values from 0 to 3, each once within a row
- group_mass: float32 [4, 512, 512], P('col', 'row'), as said below
- top_mass: float32 [512, 512], P(('row', 'col')), as said below
- group_basis: float32 [4, 512, 128], P('col', 'row'), may hold values from -6 to 6
- top_basis: float32 [512, 128], P('row'), may hold values from -6 to 6
Outputs:
- coupling: float32 [32, 128, 2, 128], P(('row', 'col'))
- group_modes: float32 [4, 512, 128], P('col', 'row')
- top_modes: float32 [512, 128], P('row')
- group_assembled: float32 [4, 512, 512], P('col', 'row')
- apex_gathered_mass: float32 [512, 512], P(('row', 'col'))
The draws below stay inside these ranges and needn't reach their ends.
Inputs may be any that keep to these rules, and one draw needn't show every extreme that they name: `tile_mask`: symmetric in its two tile indices, with ones on the diagonal tiles. block_map[l, k] is a permutation of the 4 separator blocks. `leaf_mass`: each leaf's matrix is symmetric and strictly diagonally dominant with a positive diagonal. `group_mass`: each group's matrix is symmetric and strictly diagonally dominant with a positive diagonal. `top_mass`: symmetric and strictly diagonally dominant with a positive diagonal.
All inputs are finite; a program needn't handle non-finite values.
Results may differ from the reference program's by a relative error of at most 0.0029.
Values sent between devices are 32-bit elements; how exact they have to be, the bound alone decides.
No kernel may reach another device: no remote copies, remote signals or barrier semaphores. Data moves between devices by JAX's collectives and lax.ppermute only.
A program may use at most 128 MiB of HBM per device.

```python
import jax
import jax.numpy as jnp
from jax import lax

SUBDOMAIN_DOFS = 2048
TILE = 128
SEP = 512
SEP_BLOCK = 128
MODES = 128
LEAVES = 32
GROUPS = 4
TILES = 16
SEPB = 4


def dominant(key, matrix_rows, destination):
    sampled = jax.random.normal(key, (matrix_rows, matrix_rows), jnp.float32)
    symmetric = 0.5 * (sampled + sampled.T)
    off_diagonal_part = symmetric * (1.0 - jnp.eye(matrix_rows, dtype=jnp.float32))
    margin = jax.random.uniform(jax.random.fold_in(key, 7), (matrix_rows,), jnp.float32, 1.2, 2.0)
    diagonal_part = jnp.sum(jnp.abs(off_diagonal_part), axis=1) * margin
    assembled = off_diagonal_part + jnp.diag(diagonal_part)
    return assembled * (destination / jnp.mean(diagonal_part))


def draw_leaf_mass(key, part):
    mass_unit = 1.0 / (LEAVES // GROUPS * SEP)

    def draw_one(leaf_index):
        subdomain_seed = jax.random.fold_in(key, leaf_index)
        rising = 1.0 + 2.0 * leaf_index.astype(jnp.float32) / max(LEAVES - 1, 1)
        scale_row = mass_unit * rising * jax.random.uniform(jax.random.fold_in(subdomain_seed, 1), (SUBDOMAIN_DOFS,), jnp.float32, 0.85, 1.15)
        root_row = jnp.sqrt(scale_row)
        narrow_spread = jnp.diag(scale_row)
        for position, offset in enumerate((1, TILE - 1, TILE, TILE + 1)):
            sub_key = jax.random.fold_in(subdomain_seed, 10 + position)
            weights = jax.random.uniform(sub_key, (SUBDOMAIN_DOFS - offset,), jnp.float32, 0.05, 0.09)
            upper_band = jnp.diag(weights * root_row[:-offset] * root_row[offset:], offset)
            narrow_spread = narrow_spread + upper_band + upper_band.T
        permute_degrees = jax.random.permutation(jax.random.fold_in(subdomain_seed, 2), SUBDOMAIN_DOFS)
        return narrow_spread[permute_degrees][:, permute_degrees].astype(jnp.bfloat16)
    return lax.map(draw_one, jnp.arange(LEAVES, dtype=jnp.int32))


def draw_tile_mask(key, part):
    patch_flags = jax.random.randint(jax.random.fold_in(key, 11), (LEAVES, TILES, TILES), 0, 2, dtype=jnp.int32)
    upper_part = jnp.triu(patch_flags, 1)
    identity_part = jnp.eye(TILES, dtype=jnp.int32)[None, :, :]
    return upper_part + jnp.swapaxes(upper_part, 1, 2) + identity_part


def draw_group_mass(key, part):

    def draw_one(group_index):
        return dominant(jax.random.fold_in(key, group_index + 101), SEP, 0.5 / SEP)
    return lax.map(draw_one, jnp.arange(GROUPS, dtype=jnp.int32))


def draw_top_mass(key, part):
    return dominant(jax.random.fold_in(key, 202), SEP, 0.5 * GROUPS / SEP)


def block_levels(rng, extent, shards, least, top_value):
    level = 1.0
    for dim, shards_of in shards:
        heights = jax.random.uniform(jax.random.fold_in(jax.random.fold_in(rng, 6), dim), (shards_of,), jnp.float32, least / len(shards), top_value / len(shards))
        level = level * jnp.repeat(jnp.exp(heights), extent[dim] // shards_of).reshape((-1,) + (1,) * (len(extent) - 1 - dim))
    return level


def scatter_about(key, dims, scale, most, split=(), held_as=jnp.bfloat16):
    array = jax.random.normal(key, dims, jnp.float32) * scale
    if len(split) > 0:
        array = block_levels(key, dims, split, -0.22, 0.18) * array
    return jnp.clip(array, min=-most, max=most).astype(held_as)


def setup_inputs(seed: int = 0) -> dict:
    streams_of = jax.random.split(jax.random.key(seed), 10)
    leaf_mass = draw_leaf_mass(jax.random.fold_in(streams_of[9], 71), 0)
    tile_mask = draw_tile_mask(jax.random.fold_in(streams_of[9], 71), 0)
    constraint_modes = scatter_about(streams_of[2], (LEAVES, SUBDOMAIN_DOFS, 2 * SEP), SUBDOMAIN_DOFS ** -0.5, 0.125, ((0, 32),))
    leaf_fixed_modes = scatter_about(streams_of[3], (LEAVES, SUBDOMAIN_DOFS, MODES), (((LEAVES // GROUPS) * SEP // SUBDOMAIN_DOFS) ** 0.5), 6.0, ((0, 32),))
    block_map = jax.vmap(lambda own: jax.random.permutation(own, SEPB))(jax.random.split(streams_of[4], LEAVES * 2)).reshape((LEAVES, 2, SEPB)).astype(jnp.int32)
    group_mass = draw_group_mass(jax.random.fold_in(streams_of[9], 71), 0)
    top_mass = draw_top_mass(jax.random.fold_in(streams_of[9], 71), 0)
    group_basis = scatter_about(streams_of[7], (GROUPS, SEP, MODES), 1.0, 6.0, ((0, 4), (1, 8)), jnp.float32)
    top_basis = scatter_about(streams_of[8], (SEP, MODES), 1.0, 6.0, ((0, 8),), jnp.float32)
    return {"leaf_mass": leaf_mass, "tile_mask": tile_mask, "constraint_modes": constraint_modes, "leaf_fixed_modes": leaf_fixed_modes, "block_map": block_map, "group_mass": group_mass, "top_mass": top_mass, "group_basis": group_basis, "top_basis": top_basis}


def expand_mask(leaf_matrix, tile_flags):
    tile_count = tile_flags.shape[0]
    leaf_rows = leaf_matrix.shape[0]
    chosen = tile_flags.astype(jnp.bfloat16)
    tiled = leaf_matrix.reshape(tile_count, TILE, tile_count, TILE) * chosen[:, None, :, None]
    return tiled.reshape(leaf_rows, leaf_rows)

def contract_product(left_side, right_side):
    return lax.dot_general(left_side.astype(jnp.float32), right_side.astype(jnp.float32), (((0,), (0,)), ((), ())), preferred_element_type=jnp.float32)

def to_separator(partial_value, ordering):
    block_count = SEP // SEP_BLOCK
    inverse = jnp.argsort(ordering)
    blocks = partial_value.reshape(block_count, SEP_BLOCK, block_count, SEP_BLOCK)
    blocks = blocks[inverse][:, :, inverse]
    return blocks.reshape(SEP, SEP)

def to_leaf(mode_rows, ordering):
    block_count = SEP // SEP_BLOCK
    blocks = mode_rows.reshape(block_count, SEP_BLOCK, mode_rows.shape[1])
    return blocks[ordering].reshape(SEP, mode_rows.shape[1])

def orthonormal(separator_matrix, basis_rows):
    applied = jnp.dot(separator_matrix, basis_rows, precision=lax.Precision.HIGHEST)
    gram_matrix = jnp.dot(basis_rows.T, applied, precision=lax.Precision.HIGHEST)
    gram_matrix = 0.5 * (gram_matrix + gram_matrix.T)
    lower_factor = jnp.linalg.cholesky(gram_matrix)
    return lax.linalg.triangular_solve(lower_factor, basis_rows, left_side=False, lower=True, transpose_a=True)

def reference(leaf_mass, tile_mask, constraint_modes, leaf_fixed_modes, block_map, group_mass, top_mass, group_basis, top_basis):

    def leaf_work(leaf_entries):
        leaf_matrix, tile_flags, modes_c, modes_l, ordering = leaf_entries
        masked = expand_mask(leaf_matrix, tile_flags)
        loaded = jnp.dot(masked.astype(jnp.float32), modes_c.astype(jnp.float32), preferred_element_type=jnp.float32).astype(jnp.bfloat16)
        partial_group = contract_product(modes_c[:, :SEP], loaded[:, :SEP])
        partial_top = contract_product(modes_c[:, SEP:], loaded[:, SEP:])
        projected = contract_product(modes_l, loaded)
        return (to_separator(partial_group, ordering[0]), to_separator(partial_top, ordering[1]), projected)
    sep_group, sep_top, projected = lax.map(leaf_work, (leaf_mass, tile_mask, constraint_modes, leaf_fixed_modes, block_map))
    group_matrix = group_mass + jnp.sum(sep_group.reshape(LEAVES // GROUPS, GROUPS, SEP, SEP), axis=0)
    top_matrix = top_mass + jnp.sum(sep_top, axis=0)
    group_assembled = SEP * group_matrix
    apex_gathered_mass = SEP * top_matrix
    group_modes = jax.vmap(orthonormal)(group_matrix, group_basis)
    top_modes = orthonormal(top_matrix, top_basis)
    group_index = (jnp.arange(LEAVES) % GROUPS).astype(jnp.int32)

    def couple(leaf_entries):
        leaf_projected, ordering, which_group = leaf_entries
        modes_group = to_leaf(group_modes[which_group], ordering[0])
        modes_top = to_leaf(top_modes, ordering[1])
        first = jnp.dot(leaf_projected[:, :SEP], modes_group, precision=lax.Precision.HIGHEST)
        second = jnp.dot(leaf_projected[:, SEP:], modes_top, precision=lax.Precision.HIGHEST)
        return jnp.stack([first, second], axis=1)
    coupling = lax.map(couple, (projected, block_map, group_index))
    return (coupling, group_modes, top_modes, group_assembled, apex_gathered_mass)
```

```python
import functools

import jax
import jax.numpy as jnp
from jax import lax
from jax.experimental import pallas as pl
from jax.experimental.pallas import tpu as pltpu
from jax.sharding import PartitionSpec as P

TILE = 128
LANES = 128
SUBLANES = 8
F32 = jnp.float32
BF16 = jnp.bfloat16
EXACT = lax.Precision.HIGHEST
VMEM = pl.BlockSpec(memory_space=pltpu.VMEM)
SMEM = pl.BlockSpec(memory_space=pltpu.SMEM)


def params(megabytes):
    return pltpu.CompilerParams(vmem_limit_bytes=megabytes * 2**20)


def turned(count, step):
    return [(i, (i + step) % count) for i in range(count)]


def crossed(count, bit):
    return [(i, i ^ bit) for i in range(count)]


def rows_first(left, right, precision=None):
    return lax.dot_general(
        left, right, (((0,), (0,)), ((), ())), precision=precision, preferred_element_type=F32
    )


def add_own(ref, own, place):
    share = own.shape[0]
    if share % SUBLANES == 0:
        window = pl.ds(pl.multiple_of(place * share, SUBLANES), share)
        ref[window, :] += own
        return
    fold = SUBLANES // share
    wide = jnp.concatenate([own] * fold, axis=0)
    line = lax.broadcasted_iota(jnp.int32, wide.shape, 0) // share
    window = pl.ds(pl.multiple_of(place // fold * SUBLANES, SUBLANES), SUBLANES)
    ref[window, :] += jnp.where(line == place % fold, wide, 0.0)


def copy_rows(target_ref, start, source_ref, place, share):
    if share % SUBLANES == 0:
        window = pl.ds(pl.multiple_of(place * share, SUBLANES), share)
        target_ref[start : start + share, :] = source_ref[window, :]
        return
    for i in range(share):
        target_ref[start + i : start + i + 1, :] = source_ref[pl.ds(place * share + i, 1), :]


def leaf_kernel(
    half, row_count, col_count, place_ref, mask_ref, map_ref, mass_ref, modes_ref, fixed_ref,
    own_ref, *refs,
):
    whole_ref, moved_ref, chunks = refs[0], refs[1], refs[2:-2]
    partial_ref, projected_ref = refs[-2:]
    step = pl.program_id(0)
    height, width = mass_ref.shape[1], mass_ref.shape[2]
    lines = []
    for a in range(height // TILE):
        pieces = []
        for b in range(width // TILE):
            kept = mask_ref[0, step * (height // TILE) + a, b]
            piece = mass_ref[0, a * TILE : (a + 1) * TILE, b * TILE : (b + 1) * TILE]
            pieces.append(jnp.where(kept != 0, piece, jnp.zeros_like(piece)))
        lines.append(jnp.concatenate(pieces, axis=1))
    masked = jnp.concatenate(lines, axis=0)
    loaded = jnp.dot(masked, modes_ref[0], preferred_element_type=F32).astype(BF16)
    window = pl.ds(pl.multiple_of(step * height, height), height)
    partial = rows_first(modes_ref[0, window, :], loaded)
    projected = rows_first(fixed_ref[0], loaded)

    @pl.when(step == 0)
    def _():
        partial_ref[...] = partial
        projected_ref[...] = projected

    @pl.when(step > 0)
    def _():
        partial_ref[...] += partial
        projected_ref[...] += projected

    @pl.when(step == pl.num_programs(0) - 1)
    def _():
        size = whole_ref.shape[0]
        blocks = map_ref.shape[2]
        block = size // blocks
        to = [pl.multiple_of(map_ref[0, half, a] * block, block) for a in range(blocks)]
        for b in range(blocks):
            source = slice(b * block, (b + 1) * block)
            moved_ref[:, pl.ds(to[b], block)] = projected_ref[:, source]
            for a in range(blocks):
                whole_ref[pl.ds(to[a], block), pl.ds(to[b], block)] = partial_ref[
                    a * block : (a + 1) * block, source
                ]
        row, col = place_ref[0], place_ref[1]
        if half == 0:
            own = own_ref[0]
            place = row
        else:
            own = own_ref[...]
            place = row * col_count + col
        add_own(whole_ref, own, place)
        share = own.shape[0]
        for k, chunk in enumerate(chunks):
            for r in range(chunk.shape[0] // share):
                if half == 0:
                    at = 2 * r + lax.rem(row + k, 2)
                else:
                    at = r * col_count + lax.rem(col + k, col_count)
                copy_rows(chunk, r * share, whole_ref, at, share)


def leaf_half(half, place, tile_mask, block_map, leaf_mass, constraint_modes, fixed, own, counts):
    row_count, col_count = counts
    rows, size = constraint_modes.shape[1], constraint_modes.shape[2] // 2
    modes = fixed.shape[2]
    height = 2 * TILE
    chunk_count = 2 if half == 0 else col_count
    chunk = jax.ShapeDtypeStruct((size // chunk_count, size), F32)
    own_block = (1,) + own.shape[1:] if own.ndim == 3 else own.shape
    outs = [jax.ShapeDtypeStruct((size, size), F32), jax.ShapeDtypeStruct((modes, size), F32)]
    outs += [chunk] * chunk_count
    return pl.pallas_call(
        functools.partial(leaf_kernel, half, row_count, col_count),
        grid=(rows // height,),
        in_specs=[
            SMEM,
            SMEM,
            SMEM,
            pl.BlockSpec((1, height, rows), lambda i: (0, i, 0)),
            pl.BlockSpec((1, rows, size), lambda i: (0, 0, half)),
            pl.BlockSpec((1, height, modes), lambda i: (0, i, 0)),
            pl.BlockSpec(own_block, lambda i: (0,) * len(own_block)),
        ],
        out_specs=[pl.BlockSpec(o.shape, lambda i: (0, 0)) for o in outs],
        out_shape=outs,
        scratch_shapes=[pltpu.VMEM((size, size), F32), pltpu.VMEM((modes, size), F32)],
        compiler_params=params(48),
        cost_estimate=pl.CostEstimate(
            flops=2 * rows * size * (rows + size + modes),
            bytes_accessed=2 * rows * (rows + size + modes) + 8 * size * size,
            transcendentals=0,
        ),
        name="leaf_group" if half == 0 else "leaf_top",
    )(place, tile_mask, block_map, leaf_mass, constraint_modes, fixed, own)


def prepare_kernel(count, place_ref, group_ref, top_ref, first_ref, second_ref, *refs):
    pieces, (packed_ref, terms_ref, basis_ref) = refs[:count], refs[count:]
    row = place_ref[0]
    line = pieces[0].shape[0]
    modes = terms_ref.shape[2]
    for k, piece in enumerate(pieces):
        at = pl.multiple_of(lax.rem(row + count - k, count) * line, line)
        basis_ref[pl.ds(at, line), :] = piece[...]
    grams = []
    for half, (matrix_ref, moved_ref) in enumerate(((group_ref, first_ref), (top_ref, second_ref))):
        basis = basis_ref[:, half * modes : (half + 1) * modes]
        applied = jnp.dot(matrix_ref[...], basis, precision=EXACT, preferred_element_type=F32)
        gram = rows_first(basis, applied, EXACT)
        grams.append(0.5 * (gram + gram.T))
        terms_ref[half] = jnp.dot(
            moved_ref[...], basis, precision=EXACT, preferred_element_type=F32
        )
    down = lax.broadcasted_iota(jnp.int32, (modes, modes), 0)
    across = lax.broadcasted_iota(jnp.int32, (modes, modes), 1)
    packed_ref[:modes, :] = jnp.where(down >= across, grams[0], grams[1])
    diagonal = jnp.sum(jnp.where(down == across, grams[1], 0.0), axis=0, keepdims=True)
    packed_ref[modes:, :] = jnp.broadcast_to(diagonal, (SUBLANES, modes))


def prepare(place, group, top, first, second, pieces):
    modes = first.shape[0]
    size = group.shape[0]
    return pl.pallas_call(
        functools.partial(prepare_kernel, len(pieces)),
        in_specs=[SMEM] + [VMEM] * (4 + len(pieces)),
        out_specs=[VMEM, VMEM],
        out_shape=[
            jax.ShapeDtypeStruct((modes + SUBLANES, modes), F32),
            jax.ShapeDtypeStruct((2, modes, modes), F32),
        ],
        scratch_shapes=[pltpu.VMEM((size, 2 * modes), F32)],
        compiler_params=params(32),
        cost_estimate=pl.CostEstimate(
            flops=24 * size * size * modes, bytes_accessed=12 * size * size, transcendentals=0
        ),
        name="prepare",
    )(place, group, top, first, second, *pieces)


def factor(matrices):
    size = matrices[0].shape[0]
    width = SUBLANES
    down = lax.broadcasted_iota(jnp.int32, (size, size), 0)
    across = lax.broadcasted_iota(jnp.int32, (size, size), 1)
    line = lax.broadcasted_iota(jnp.int32, (width, size), 0)
    lane = lax.broadcasted_iota(jnp.int32, (width, size), 1)
    states = list(matrices)
    diagonals = [[] for _ in matrices]
    for start in range(0, size, width):
        stop = start + width
        for m, state in enumerate(states):
            spread = [
                jnp.broadcast_to(state[:, start + q : start + q + 1], (size, size))
                for q in range(width)
            ]
            strip = state[start:stop, :]
            small = [s[start:stop, :] for s in spread]
            scaled = []
            rest = strip
            for q in range(width):
                scale = lax.rsqrt(small[q][q : q + 1, :])
                tail = [small[t][q : q + 1, :] * scale for t in range(q + 1, width)]
                level = rest[q : q + 1, :] * scale
                rest = rest - small[q] * (scale * level)
                small[q] = jnp.where(line == q, 1.0, small[q]) * scale
                for t in range(q + 1, width):
                    small[t] = jnp.where(line == q, 0.0, small[t]) - small[q] * tail[t - q - 1]
                scaled.append(level)
            small = [jnp.where(line <= q, s, 0.0) for q, s in enumerate(small)]
            solved = small[0] * scaled[0]
            for q in range(1, width):
                solved = solved + small[q] * scaled[q]
            solved = jnp.where(lane >= stop, solved, 0.0)
            update = spread[0] * solved[0:1, :]
            for q in range(1, width):
                update = update + spread[q] * solved[q : q + 1, :]
            block = jnp.where(lane == line + start, 1.0, 0.0)
            kept = jnp.where(lane < start, strip, block) - solved
            parts = []
            if start > 0:
                parts.append(state[:start] - update[:start])
            parts.append(kept)
            if stop < size:
                parts.append(state[stop:] - update[stop:])
            states[m] = jnp.concatenate(parts, axis=0)
            diagonal = jnp.zeros((width, size), F32)
            for q in range(width):
                diagonal = jnp.where(lane == start + q, small[q], diagonal)
            diagonals[m].append(diagonal)
    uppers = [jnp.where(across >= down, state, 0.0) for state in states]
    return uppers, [jnp.concatenate(d, axis=0) for d in diagonals]


def finish_kernel(near_ref, far_ref, terms_ref, basis_ref, coupling_ref, group_ref, top_ref):
    modes = near_ref.shape[1]
    down = lax.broadcasted_iota(jnp.int32, (modes, modes), 0)
    across = lax.broadcasted_iota(jnp.int32, (modes, modes), 1)
    near, far = near_ref[:modes, :], far_ref[:modes, :]
    group = jnp.where(down >= across, near, near.T)
    top = jnp.where(down > across, far.T, far)
    top = jnp.where(down == across, jnp.broadcast_to(far_ref[modes : modes + 1, :], top.shape), top)
    uppers, diagonals = factor([group, top])
    for half in range(2):
        inverse = jnp.dot(
            uppers[half], diagonals[half], precision=EXACT, preferred_element_type=F32
        )
        lane = slice(half * modes, (half + 1) * modes)
        coupling_ref[0, :, half, :] = jnp.dot(
            terms_ref[half], inverse, precision=EXACT, preferred_element_type=F32
        )
        rows = jnp.dot(basis_ref[:, lane], inverse, precision=EXACT, preferred_element_type=F32)
        if half == 0:
            group_ref[0] = rows
        else:
            top_ref[...] = rows


def finish(near, far, terms, basis):
    modes = near.shape[1]
    line = basis.shape[0]
    return pl.pallas_call(
        finish_kernel,
        in_specs=[VMEM] * 4,
        out_specs=[VMEM] * 3,
        out_shape=[
            jax.ShapeDtypeStruct((1, modes, 2, modes), F32),
            jax.ShapeDtypeStruct((1, line, modes), F32),
            jax.ShapeDtypeStruct((line, modes), F32),
        ],
        compiler_params=params(32),
        cost_estimate=pl.CostEstimate(
            flops=20 * modes**3, bytes_accessed=24 * modes * modes, transcendentals=2 * modes
        ),
        name="finish",
    )(near, far, terms, basis)


def merge_kernel(count, part, place_ref, *refs):
    pieces, chunks = refs[:count], refs[count:-1]
    total_ref = refs[-1]
    total = pieces[0][...]
    for piece in pieces[1:]:
        total = total + piece[...]
    total_ref[...] = total
    share = chunks[0].shape[0]
    for k, chunk in enumerate(chunks):
        at = lax.rem(place_ref[0] // part + k, len(chunks))
        copy_rows(chunk, 0, total_ref, at, share)


def merge(place, pieces, chunk_count, part):
    rows, size = pieces[0].shape
    chunk = jax.ShapeDtypeStruct((rows // chunk_count, size), F32)
    return pl.pallas_call(
        functools.partial(merge_kernel, len(pieces), part),
        in_specs=[SMEM] + [VMEM] * len(pieces),
        out_specs=[VMEM] * chunk_count,
        out_shape=[chunk] * chunk_count,
        scratch_shapes=[pltpu.VMEM((rows, size), F32)],
        compiler_params=params(32),
        cost_estimate=pl.CostEstimate(
            flops=len(pieces) * rows * size,
            bytes_accessed=4 * (len(pieces) + 1) * rows * size,
            transcendentals=0,
        ),
        name="merge",
    )(place, *pieces)


def body(
    leaf_mass, tile_mask, constraint_modes, leaf_fixed_modes, block_map, group_mass, top_mass,
    group_basis, top_basis,
):
    row_count, col_count = lax.axis_size("row"), lax.axis_size("col")
    place = jnp.stack([lax.axis_index("row"), lax.axis_index("col")]).astype(jnp.int32)
    counts = (row_count, col_count)
    size = group_mass.shape[2]
    basis = jnp.concatenate([group_basis[0], top_basis], axis=1)
    pieces = [basis] + [
        lax.ppermute(basis, "row", turned(row_count, k)) for k in range(1, row_count)
    ]

    def half_of(half, own):
        return leaf_half(
            half, place, tile_mask, block_map, leaf_mass, constraint_modes, leaf_fixed_modes, own,
            counts,
        )

    group_whole, first, group_keep, group_send = half_of(0, group_mass)
    group_other = lax.ppermute(group_send, "row", crossed(row_count, 1))
    top_whole, second, *top_chunks = half_of(1, top_mass)
    packed, terms = prepare(place, group_whole, top_whole, first, second, pieces)

    near = packed
    bit = 1
    while bit < row_count:
        near = near + lax.ppermute(near, "row", crossed(row_count, bit))
        bit *= 2
    far = near
    bit = 1
    while bit < col_count:
        far = far + lax.ppermute(far, "col", crossed(col_count, bit))
        bit *= 2
    coupling, group_modes, top_modes = finish(near, far, terms, basis)

    lines = row_count // 2
    group_chunks = merge(place, [group_keep, group_other], lines, 2)
    group_total = group_chunks[0]
    for k in range(1, lines):
        group_total = group_total + lax.ppermute(
            group_chunks[k], "row", turned(row_count, 2 * k)
        )
    top_other = [
        lax.ppermute(top_chunks[k], "col", turned(col_count, k)) for k in range(1, col_count)
    ]
    top_chunks = merge(place, [top_chunks[0]] + top_other, row_count, 1)
    top_total = top_chunks[0]
    for k in range(1, row_count):
        top_total = top_total + lax.ppermute(top_chunks[k], "row", turned(row_count, k))
    return coupling, group_modes, top_modes, (size * group_total)[None], size * top_total


def solution(mesh):
    leaf = P(("row", "col"), None, None)
    group = P("col", "row", None)
    in_specs = (
        leaf, leaf, leaf, leaf, leaf, group, P(("row", "col"), None), group, P("row", None),
    )
    out_specs = (
        P(("row", "col"), None, None, None), group, P("row", None), group, P(("row", "col"), None),
    )
    return jax.shard_map(body, mesh=mesh, in_specs=in_specs, out_specs=out_specs, check_vma=False)
```

```python
import functools

import jax
import jax.numpy as jnp
from jax import lax
from jax.experimental import pallas as pl
from jax.experimental.pallas import tpu as pltpu
from jax.sharding import PartitionSpec as P

TILE = 128
SUBLANES = 8
F32 = jnp.float32
BF16 = jnp.bfloat16
VMEM = pl.BlockSpec(memory_space=pltpu.VMEM)
SMEM = pl.BlockSpec(memory_space=pltpu.SMEM)
HBM = pl.BlockSpec(memory_space=pltpu.HBM)
MASS_PARTS = 4


def params(megabytes):
    return pltpu.CompilerParams(vmem_limit_bytes=megabytes * 2**20)


def crossed(count, bit):
    return [(i, i ^ bit) for i in range(count)]


def rows_first(left, right):
    return lax.dot_general(left, right, (((0,), (0,)), ((), ())), preferred_element_type=F32)


def add_own(ref, own, place):
    share = own.shape[0]
    if share % SUBLANES == 0:
        window = pl.ds(pl.multiple_of(place * share, SUBLANES), share)
        ref[window, :] += own
        return
    fold = SUBLANES // share
    wide = jnp.concatenate([own] * fold, axis=0)
    line = lax.broadcasted_iota(jnp.int32, wide.shape, 0) // share
    window = pl.ds(pl.multiple_of(place // fold * SUBLANES, SUBLANES), SUBLANES)
    ref[window, :] += jnp.where(line == place % fold, wide, 0.0)


def copy_rows(target_ref, start, source_ref, place, share):
    if share % SUBLANES == 0:
        window = pl.ds(pl.multiple_of(place * share, SUBLANES), share)
        target_ref[start : start + share, :] = source_ref[window, :]
        return
    for i in range(share):
        target_ref[start + i : start + i + 1, :] = source_ref[pl.ds(place * share + i, 1), :]


def leaf_kernel(
    half, tiles, table_ref, mass_hbm, modes_hbm, fixed_hbm, own_hbm, moved_ref, *refs
):
    chunks = refs[:-8]
    mass_ref, modes_ref, fixed_ref, own_ref, whole_ref, partial_ref, projected_ref, sems = refs[-8:]
    row, col = lax.axis_index("row"), lax.axis_index("col")
    row_count, col_count = lax.axis_size("row"), lax.axis_size("col")
    rows, size = modes_ref.shape
    height = rows // MASS_PARTS

    def mass_copy(i):
        window = pl.ds(pl.multiple_of(i * height, height), height)
        return pltpu.make_async_copy(
            mass_hbm.at[0, window], mass_ref.at[window], sems.at[3 + i]
        )

    half_modes = modes_hbm.at[0, :, pl.ds(half * size, size)]
    modes_copy = pltpu.make_async_copy(half_modes, modes_ref, sems.at[0])
    fixed_copy = pltpu.make_async_copy(fixed_hbm.at[0], fixed_ref, sems.at[1])
    own_source = own_hbm.at[0] if half == 0 else own_hbm
    own_copy = pltpu.make_async_copy(own_source, own_ref, sems.at[2])
    modes_copy.start()
    mass_copy(0).start()
    fixed_copy.start()
    for i in range(1, MASS_PARTS):
        mass_copy(i).start()
    own_copy.start()
    modes_copy.wait()

    def part(i, first):
        mass_copy(i).wait()
        lines = []
        for a in range(height // TILE):
            pieces = []
            for b in range(tiles):
                kept = table_ref[(i * (height // TILE) + a) * tiles + b]
                window = pl.ds(pl.multiple_of(i * height + a * TILE, TILE), TILE)
                piece = mass_ref[window, b * TILE : (b + 1) * TILE]
                pieces.append(jnp.where(kept != 0, piece, jnp.zeros_like(piece)))
            lines.append(jnp.concatenate(pieces, axis=1))
        masked = jnp.concatenate(lines, axis=0)
        loaded = jnp.dot(masked, modes_ref[...], preferred_element_type=F32).astype(BF16)
        if first:
            fixed_copy.wait()
        window = pl.ds(pl.multiple_of(i * height, height), height)
        partial = rows_first(modes_ref[window, :], loaded)
        projected = rows_first(fixed_ref[window, :], loaded)
        if first:
            partial_ref[...] = partial
            projected_ref[...] = projected
        else:
            partial_ref[...] += partial
            projected_ref[...] += projected

    part(0, True)
    lax.fori_loop(1, MASS_PARTS, lambda i, _: part(i, False), None)

    blocks = size // TILE
    base = tiles * tiles + half * blocks
    to = [pl.multiple_of(table_ref[base + a] * TILE, TILE) for a in range(blocks)]
    for b in range(blocks):
        source = slice(b * TILE, (b + 1) * TILE)
        moved_ref[:, pl.ds(to[b], TILE)] = projected_ref[:, source]
        for a in range(blocks):
            whole_ref[pl.ds(to[a], TILE), pl.ds(to[b], TILE)] = partial_ref[
                a * TILE : (a + 1) * TILE, source
            ]
    own_copy.wait()
    share = own_ref.shape[0]
    if half == 0:
        add_own(whole_ref, own_ref[...], row)
        for k, chunk in enumerate(chunks):
            for r in range(row_count // 2):
                copy_rows(chunk, r * share, whole_ref, 2 * r + lax.rem(row + k, 2), share)
    else:
        add_own(whole_ref, own_ref[...], row * col_count + col)
        for r in range(row_count):
            for c in range(col_count):
                start, place = (c * row_count + r) * share, (r * col_count + c) * share
                chunks[0][start : start + share, :] = whole_ref[place : place + share, :]


def leaf_half(half, tiles, table, leaf_mass, constraint_modes, fixed, own):
    rows, size = constraint_modes.shape[1], constraint_modes.shape[2] // 2
    modes = fixed.shape[2]
    chunk_count = 2 if half == 0 else 1
    outs = [jax.ShapeDtypeStruct((modes, size), F32)]
    outs += [jax.ShapeDtypeStruct((size // chunk_count, size), F32)] * chunk_count
    return pl.pallas_call(
        functools.partial(leaf_kernel, half, tiles),
        in_specs=[SMEM] + [HBM] * 4,
        out_specs=[VMEM] * len(outs),
        out_shape=outs,
        scratch_shapes=[
            pltpu.VMEM((rows, rows), BF16),
            pltpu.VMEM((rows, size), BF16),
            pltpu.VMEM((rows, modes), BF16),
            pltpu.VMEM(own.shape[-2:], F32),
            pltpu.VMEM((size, size), F32),
            pltpu.VMEM((size, size), F32),
            pltpu.VMEM((modes, size), F32),
            pltpu.SemaphoreType.DMA((3 + MASS_PARTS,)),
        ],
        compiler_params=params(48),
        cost_estimate=pl.CostEstimate(
            flops=2 * rows * size * (rows + size + modes),
            bytes_accessed=2 * rows * (rows + size + modes) + 8 * size * size,
            transcendentals=0,
        ),
        name="leaf_group" if half == 0 else "leaf_top",
    )(table, leaf_mass, constraint_modes, fixed, own)


def split(value):
    high = value.astype(BF16)
    return high, (value - high.astype(F32)).astype(BF16)


def three_pass(left, right, turn=False):
    (left_high, left_low), (right_high, right_low) = left, right
    multiply = rows_first if turn else functools.partial(jnp.dot, preferred_element_type=F32)
    width = right_high.shape[1]
    both = multiply(left_high, jnp.concatenate([right_high, right_low], axis=1))
    return both[:, :width] + both[:, width:] + multiply(left_low, right_high)


def prepare_kernel(keep_ref, send_ref, top_ref, first_ref, second_ref, bases_ref, out_ref, terms_ref):
    modes = terms_ref.shape[2]
    size = bases_ref.shape[0]
    row, col = lax.axis_index("row"), lax.axis_index("col")
    row_count, col_count = lax.axis_size("row"), lax.axis_size("col")
    grams = []
    for half in range(2):
        lanes = slice(half * modes, (half + 1) * modes)
        basis = split(bases_ref[:, lanes])
        if half == 0:
            line = size // row_count
            matrix, order = [], []
            for k, ref in enumerate((keep_ref, send_ref)):
                matrix.append(ref[...])
                for r in range(row_count // 2):
                    at = (2 * r + lax.rem(row + k, 2)) * line
                    order.append(bases_ref[pl.ds(pl.multiple_of(at, line), line), lanes])
            matrix = jnp.concatenate(matrix, axis=0)
            ordered = split(jnp.concatenate(order, axis=0))
        else:
            line = size // (row_count * col_count)
            order = [
                bases_ref[(r * col_count + c) * line : (r * col_count + c + 1) * line, lanes]
                for c in range(col_count)
                for r in range(row_count)
            ]
            matrix = top_ref[...]
            ordered = split(jnp.concatenate(order, axis=0))
        applied = three_pass(split(matrix), basis)
        gram = three_pass(ordered, split(applied), turn=True)
        grams.append(0.5 * (gram + gram.T))
        moved = (first_ref, second_ref)[half]
        terms_ref[half] = three_pass(split(moved[...]), basis)
    down = lax.broadcasted_iota(jnp.int32, (modes, modes), 0)
    across = lax.broadcasted_iota(jnp.int32, (modes, modes), 1)
    packed = jnp.where(down >= across, grams[0], grams[1])
    diagonal = jnp.sum(jnp.where(down == across, grams[1], 0.0), axis=0, keepdims=True)
    devices = row_count * col_count
    share, line = modes // devices, out_ref.shape[0] // devices
    diagonal = jnp.broadcast_to(diagonal, (line - share, modes))
    for d in range(devices):
        out_ref[d * line : d * line + share, :] = packed[d * share : (d + 1) * share]
        out_ref[d * line + share : (d + 1) * line, :] = diagonal


def packed_lines(modes, devices):
    share = modes // devices
    return (share + SUBLANES) // SUBLANES * SUBLANES


def prepare(keep, send, top, first, second, bases, devices):
    modes, size = first.shape
    return pl.pallas_call(
        prepare_kernel,
        in_specs=[VMEM] * 6,
        out_specs=[VMEM, VMEM],
        out_shape=[
            jax.ShapeDtypeStruct((devices * packed_lines(modes, devices), modes), F32),
            jax.ShapeDtypeStruct((2, modes, modes), F32),
        ],
        compiler_params=params(32),
        cost_estimate=pl.CostEstimate(
            flops=12 * size * size * modes, bytes_accessed=12 * size * size, transcendentals=0
        ),
        name="prepare",
    )(keep, send, top, first, second, bases)


def total_kernel(in_ref, out_ref):
    row, col = lax.axis_index("row"), lax.axis_index("col")
    row_count, col_count = lax.axis_size("row"), lax.axis_size("col")
    devices = row_count * col_count
    modes = in_ref.shape[1]
    line = in_ref.shape[0] // devices
    share = modes // devices
    groups = []
    for c in range(col_count):
        value = in_ref[c * line : (c + 1) * line, :]
        for r in range(1, row_count):
            at = (r * col_count + c) * line
            value = value + in_ref[at : at + line, :]
        groups.append(value)
    top = functools.reduce(jnp.add, groups)
    down = lax.broadcasted_iota(jnp.int32, (line, modes), 0)
    across = lax.broadcasted_iota(jnp.int32, (line, modes), 1)
    lower = (down < share) & (across <= down + (row * col_count + col) * share)
    for c in range(col_count):
        value = jnp.where(lower, groups[c], top)
        for r in range(row_count):
            at = (r * col_count + c) * line
            out_ref[at : at + line, :] = value


def total(pieces):
    return pl.pallas_call(
        total_kernel,
        in_specs=[VMEM],
        out_specs=VMEM,
        out_shape=jax.ShapeDtypeStruct(pieces.shape, F32),
        cost_estimate=pl.CostEstimate(
            flops=2 * pieces.size, bytes_accessed=8 * pieces.size, transcendentals=0
        ),
        name="total",
    )(pieces)


def factor(matrices):
    size = matrices[0].shape[0]
    width = SUBLANES
    down = lax.broadcasted_iota(jnp.int32, (size, size), 0)
    across = lax.broadcasted_iota(jnp.int32, (size, size), 1)
    line = lax.broadcasted_iota(jnp.int32, (width, size), 0)
    lane = lax.broadcasted_iota(jnp.int32, (width, size), 1)
    states = list(matrices)
    diagonals = [[] for _ in matrices]
    for start in range(0, size, width):
        stop = start + width
        for m, state in enumerate(states):
            spread = [
                jnp.broadcast_to(state[:, start + q : start + q + 1], (size, size))
                for q in range(width)
            ]
            strip = state[start:stop, :]
            small = [s[start:stop, :] for s in spread]
            scaled = []
            rest = strip
            for q in range(width):
                scale = lax.rsqrt(small[q][q : q + 1, :])
                tail = [small[t][q : q + 1, :] * scale for t in range(q + 1, width)]
                level = rest[q : q + 1, :] * scale
                rest = rest - small[q] * (scale * level)
                small[q] = jnp.where(line == q, 1.0, small[q]) * scale
                for t in range(q + 1, width):
                    small[t] = jnp.where(line == q, 0.0, small[t]) - small[q] * tail[t - q - 1]
                scaled.append(level)
            small = [jnp.where(line <= q, s, 0.0) for q, s in enumerate(small)]
            solved = small[0] * scaled[0]
            for q in range(1, width):
                solved = solved + small[q] * scaled[q]
            solved = jnp.where(lane >= stop, solved, 0.0)
            update = spread[0] * solved[0:1, :]
            for q in range(1, width):
                update = update + spread[q] * solved[q : q + 1, :]
            block = jnp.where(lane == line + start, 1.0, 0.0)
            kept = jnp.where(lane < start, strip, block) - solved
            parts = []
            if start > 0:
                parts.append(state[:start] - update[:start])
            parts.append(kept)
            if stop < size:
                parts.append(state[stop:] - update[stop:])
            states[m] = jnp.concatenate(parts, axis=0)
            diagonal = jnp.zeros((width, size), F32)
            for q in range(width):
                diagonal = jnp.where(lane == start + q, small[q], diagonal)
            diagonals[m].append(diagonal)
    uppers = [jnp.where(across >= down, state, 0.0) for state in states]
    return uppers, [jnp.concatenate(d, axis=0) for d in diagonals]


def finish_kernel(packed_ref, terms_ref, group_basis_ref, top_basis_ref, coupling_ref, group_ref, top_ref):
    modes = packed_ref.shape[1]
    devices = lax.axis_size("row") * lax.axis_size("col")
    line, share = packed_ref.shape[0] // devices, modes // devices
    packed = jnp.concatenate(
        [packed_ref[d * line : d * line + share, :] for d in range(devices)], axis=0
    )
    down = lax.broadcasted_iota(jnp.int32, (modes, modes), 0)
    across = lax.broadcasted_iota(jnp.int32, (modes, modes), 1)
    turned = packed.T
    group = jnp.where(down >= across, packed, turned)
    top = jnp.where(down > across, turned, packed)
    diagonal = jnp.broadcast_to(packed_ref[share : share + 1, :], top.shape)
    top = jnp.where(down == across, diagonal, top)
    uppers, diagonals = factor([group, top])
    for half in range(2):
        inverse = split(three_pass(split(uppers[half]), split(diagonals[half])))
        basis = (group_basis_ref[0], top_basis_ref[...])[half]
        left = jnp.concatenate([terms_ref[half], basis], axis=0)
        result = three_pass(split(left), inverse)
        coupling_ref[0, :, half, :] = result[:modes]
        if half == 0:
            group_ref[0] = result[modes:]
        else:
            top_ref[...] = result[modes:]


def finish(packed, terms, group_basis, top_basis):
    modes = packed.shape[1]
    return pl.pallas_call(
        finish_kernel,
        in_specs=[VMEM] * 4,
        out_specs=[VMEM] * 3,
        out_shape=[
            jax.ShapeDtypeStruct((1, modes, 2, modes), F32),
            jax.ShapeDtypeStruct(group_basis.shape, F32),
            jax.ShapeDtypeStruct(top_basis.shape, F32),
        ],
        compiler_params=params(32),
        cost_estimate=pl.CostEstimate(
            flops=20 * modes**3, bytes_accessed=24 * modes * modes, transcendentals=2 * modes
        ),
        name="finish",
    )(packed, terms, group_basis, top_basis)


def body(
    leaf_mass, tile_mask, constraint_modes, leaf_fixed_modes, block_map, group_mass, top_mass,
    group_basis, top_basis,
):
    row_count, col_count = lax.axis_size("row"), lax.axis_size("col")
    both = ("row", "col")
    size = group_mass.shape[2]
    tiles = tile_mask.shape[1]
    table = jnp.concatenate([tile_mask.reshape(-1), block_map.reshape(-1)])
    bases = lax.all_gather(
        jnp.concatenate([group_basis[0], top_basis], axis=1), "row", axis=0, tiled=True
    )

    def half_of(half, own):
        return leaf_half(half, tiles, table, leaf_mass, constraint_modes, leaf_fixed_modes, own)

    first, keep, send = half_of(0, group_mass)
    other = lax.ppermute(send, "row", crossed(row_count, 1))
    second, top = half_of(1, top_mass)
    packed, terms = prepare(keep, send, top, first, second, bases, row_count * col_count)
    packed = lax.all_to_all(packed, both, 0, 0, tiled=True)
    packed = lax.all_to_all(total(packed), both, 0, 0, tiled=True)
    coupling, group_modes, top_modes = finish(packed, terms, group_basis, top_basis)

    parities = [list(range(p, row_count, 2)) for p in range(2)]
    group_rows = lax.all_to_all(
        keep + other, "row", 0, 0, axis_index_groups=parities, tiled=True
    )
    group_rows = group_rows.reshape(row_count // 2, -1, size).sum(axis=0)
    top_rows = lax.all_to_all(top, "col", 0, 0, tiled=True)
    top_rows = top_rows.reshape(col_count, -1, size).sum(axis=0)
    top_rows = lax.all_to_all(top_rows, "row", 0, 0, tiled=True)
    top_rows = top_rows.reshape(row_count, -1, size).sum(axis=0)
    return coupling, group_modes, top_modes, (size * group_rows)[None], size * top_rows


def solution(mesh):
    leaf = P(("row", "col"), None, None)
    group = P("col", "row", None)
    in_specs = (
        leaf, leaf, leaf, leaf, leaf, group, P(("row", "col"), None), group, P("row", None),
    )
    out_specs = (
        P(("row", "col"), None, None, None), group, P("row", None), group, P(("row", "col"), None),
    )
    return jax.shard_map(body, mesh=mesh, in_specs=in_specs, out_specs=out_specs, check_vma=False)
```

```python
import functools

import jax
import jax.numpy as jnp
from jax import lax
from jax.experimental import pallas as pl
from jax.experimental.pallas import tpu as pltpu
from jax.sharding import PartitionSpec as P

TILE = 128
SUBLANES = 8
F32 = jnp.float32
BF16 = jnp.bfloat16
VMEM = pl.BlockSpec(memory_space=pltpu.VMEM)
SMEM = pl.BlockSpec(memory_space=pltpu.SMEM)
HBM = pl.BlockSpec(memory_space=pltpu.HBM)
MASS_PARTS = 4
LEAF_MEGABYTES = 48


def params(megabytes):
    return pltpu.CompilerParams(vmem_limit_bytes=int(megabytes * 2**20))


def crossed(count, bit):
    return [(i, i ^ bit) for i in range(count)]


def rows_first(left, right):
    return lax.dot_general(left, right, (((0,), (0,)), ((), ())), preferred_element_type=F32)


def add_own(ref, own, place):
    share = own.shape[0]
    if share % SUBLANES == 0:
        window = pl.ds(pl.multiple_of(place * share, SUBLANES), share)
        ref[window, :] += own
        return
    fold = SUBLANES // share
    wide = jnp.concatenate([own] * fold, axis=0)
    line = lax.broadcasted_iota(jnp.int32, wide.shape, 0) // share
    window = pl.ds(pl.multiple_of(place // fold * SUBLANES, SUBLANES), SUBLANES)
    ref[window, :] += jnp.where(line == place % fold, wide, 0.0)


def copy_rows(target_ref, start, source_ref, place, share):
    if share % SUBLANES == 0:
        window = pl.ds(pl.multiple_of(place * share, SUBLANES), share)
        target_ref[start : start + share, :] = source_ref[window, :]
        return
    for i in range(share):
        target_ref[start + i : start + i + 1, :] = source_ref[pl.ds(place * share + i, 1), :]


def bits_of(count):
    return count.bit_length() - 1


def exchanges(half, row_count, col_count):
    row = [("row", 1)] + [("row", 1 << b) for b in range(bits_of(row_count) - 1, 0, -1)]
    col = [("col", 1 << b) for b in range(bits_of(col_count))]
    return row if half == 0 else col + row


def cut_order(half, row_count, col_count):
    steps = exchanges(half, row_count, col_count)
    order = [0]
    for axis, bit in reversed(steps):
        stride = 1 if half == 0 or axis == "col" else col_count
        order = order + [place + bit * stride for place in order]
    return order


def leaf_kernel(
    half, mask_ref, map_ref, mass_hbm, modes_hbm, fixed_hbm, own_hbm, after_ref, moved_ref, *refs
):
    chunks = refs[:-8]
    mass_ref, modes_ref, fixed_ref, own_ref, whole_ref, partial_ref, projected_ref, sems = refs[-8:]
    row, col = lax.axis_index("row"), lax.axis_index("col")
    row_count, col_count = lax.axis_size("row"), lax.axis_size("col")
    rows, size = modes_ref.shape
    tiles = rows // TILE
    height = rows // MASS_PARTS

    def mass_copy(i):
        window = pl.ds(pl.multiple_of(i * height, height), height)
        return pltpu.make_async_copy(
            mass_hbm.at[0, window], mass_ref.at[window], sems.at[3 + i]
        )

    half_modes = modes_hbm.at[0, :, pl.ds(half * size, size)]
    modes_copy = pltpu.make_async_copy(half_modes, modes_ref, sems.at[0])
    fixed_copy = pltpu.make_async_copy(fixed_hbm.at[0], fixed_ref, sems.at[1])
    own_source = own_hbm.at[0] if half == 0 else own_hbm
    own_copy = pltpu.make_async_copy(own_source, own_ref, sems.at[2])
    modes_copy.start()
    mass_copy(0).start()
    fixed_copy.start()
    for i in range(1, MASS_PARTS):
        mass_copy(i).start()
    own_copy.start()
    modes_copy.wait()

    def part(i, first):
        mass_copy(i).wait()
        lines = []
        for a in range(height // TILE):
            pieces = []
            for b in range(tiles):
                kept = mask_ref[0, i * (height // TILE) + a, b]
                window = pl.ds(pl.multiple_of(i * height + a * TILE, TILE), TILE)
                piece = mass_ref[window, b * TILE : (b + 1) * TILE]
                pieces.append(jnp.where(kept != 0, piece, jnp.zeros_like(piece)))
            lines.append(jnp.concatenate(pieces, axis=1))
        masked = jnp.concatenate(lines, axis=0)
        loaded = jnp.dot(masked, modes_ref[...], preferred_element_type=F32).astype(BF16)
        if first:
            fixed_copy.wait()
        window = pl.ds(pl.multiple_of(i * height, height), height)
        partial = rows_first(modes_ref[window, :], loaded)
        projected = rows_first(fixed_ref[window, :], loaded)
        if first:
            partial_ref[...] = partial
            projected_ref[...] = projected
        else:
            partial_ref[...] += partial
            projected_ref[...] += projected

    part(0, True)
    lax.fori_loop(1, MASS_PARTS, lambda i, _: part(i, False), None)

    blocks = size // TILE
    to = [pl.multiple_of(map_ref[0, half, a] * TILE, TILE) for a in range(blocks)]
    for b in range(blocks):
        source = slice(b * TILE, (b + 1) * TILE)
        moved_ref[:, pl.ds(to[b], TILE)] = projected_ref[:, source]
        for a in range(blocks):
            whole_ref[pl.ds(to[a], TILE), pl.ds(to[b], TILE)] = partial_ref[
                a * TILE : (a + 1) * TILE, source
            ]
    own_copy.wait()
    share = own_ref.shape[0]
    order = cut_order(half, row_count, col_count)
    add_own(whole_ref, own_ref[...], row if half == 0 else row * col_count + col)
    bit = lax.rem(row if half == 0 else col, 2)
    for k, chunk in enumerate(chunks):
        for i, place in enumerate(order):
            if i < len(order) // 2:
                step = order[i + len(order) // 2] - place
                copy_rows(chunk, i * share, whole_ref, place + step * lax.rem(bit + k, 2), share)


def leaf_half(half, tile_mask, block_map, leaf_mass, constraint_modes, fixed, own, after):
    rows, size = constraint_modes.shape[1], constraint_modes.shape[2] // 2
    modes = fixed.shape[2]
    outs = [jax.ShapeDtypeStruct((modes, size), F32)]
    outs += [jax.ShapeDtypeStruct((size // 2, size), F32)] * 2
    return pl.pallas_call(
        functools.partial(leaf_kernel, half),
        in_specs=[SMEM] * 2 + [HBM] * 4 + [pl.BlockSpec(memory_space=pl.ANY)],
        out_specs=[VMEM] * len(outs),
        out_shape=outs,
        scratch_shapes=[
            pltpu.VMEM((rows, rows), BF16),
            pltpu.VMEM((rows, size), BF16),
            pltpu.VMEM((rows, modes), BF16),
            pltpu.VMEM(own.shape[-2:], F32),
            pltpu.VMEM((size, size), F32),
            pltpu.VMEM((size, size), F32),
            pltpu.VMEM((modes, size), F32),
            pltpu.SemaphoreType.DMA((3 + MASS_PARTS,)),
        ],
        compiler_params=params(LEAF_MEGABYTES),
        cost_estimate=pl.CostEstimate(
            flops=2 * rows * size * (rows + size + modes),
            bytes_accessed=2 * rows * (rows + size + modes) + 8 * size * size,
            transcendentals=0,
        ),
        name="leaf_group" if half == 0 else "leaf_top",
    )(tile_mask, block_map, leaf_mass, constraint_modes, fixed, own, after)


def split(value):
    high = value.astype(BF16)
    return high, (value - high.astype(F32)).astype(BF16)


def three_pass(left, right, turn=False):
    (left_high, left_low), (right_high, right_low) = left, right
    multiply = rows_first if turn else functools.partial(jnp.dot, preferred_element_type=F32)
    width = right_high.shape[1]
    both = multiply(left_high, jnp.concatenate([right_high, right_low], axis=1))
    return both[:, :width] + both[:, width:] + multiply(left_low, right_high)


def halve(step, keep_ref, other_ref, next_ref, send_ref):
    axis, bit = step
    height = next_ref.shape[0]
    mine = lax.rem(lax.axis_index(axis) // bit, 2) == 1
    low = keep_ref[:height, :] + other_ref[:height, :]
    high = keep_ref[height:, :] + other_ref[height:, :]
    next_ref[...] = jnp.where(mine, high, low)
    send_ref[...] = jnp.where(mine, low, high)


def prepare_kernel(
    count, step, keep_ref, send_ref, other_ref, top_keep_ref, top_send_ref, first_ref, second_ref, *refs
):
    pieces = refs[:count]
    packed_ref, terms_ref, next_ref, next_send_ref, bases_ref = refs[count:]
    halve(step, keep_ref, other_ref, next_ref, next_send_ref)
    modes = terms_ref.shape[2]
    size = bases_ref.shape[0]
    row, col = lax.axis_index("row"), lax.axis_index("col")
    row_count, col_count = lax.axis_size("row"), lax.axis_size("col")
    line = size // row_count
    for k, piece in enumerate(pieces):
        pair = lax.bitwise_xor(row // 2, k)
        for i in range(2):
            at = (2 * pair + lax.rem(row + i, 2)) * line
            bases_ref[pl.ds(pl.multiple_of(at, line), line), :] = piece[i * line : (i + 1) * line, :]
    grams = []
    for half in range(2):
        lanes = slice(half * modes, (half + 1) * modes)
        basis = split(bases_ref[:, lanes])
        order = cut_order(half, row_count, col_count)
        share = size // len(order)
        lower = jnp.concatenate(
            [bases_ref[at * share : (at + 1) * share, lanes] for at in order[: len(order) // 2]], axis=0
        )
        upper = jnp.concatenate(
            [bases_ref[at * share : (at + 1) * share, lanes] for at in order[len(order) // 2 :]], axis=0
        )
        swap = lax.rem((row, col)[half], 2) == 1
        ordered = jnp.concatenate(
            [jnp.where(swap, upper, lower), jnp.where(swap, lower, upper)], axis=0
        )
        parts = ((keep_ref, send_ref), (top_keep_ref, top_send_ref))[half]
        matrix = jnp.concatenate([part[...] for part in parts], axis=0)
        applied = three_pass(split(matrix), basis)
        gram = three_pass(split(ordered), split(applied), turn=True)
        grams.append(0.5 * (gram + gram.T))
        moved = (first_ref, second_ref)[half]
        terms_ref[half] = three_pass(split(moved[...]), basis)
    down = lax.broadcasted_iota(jnp.int32, (modes, modes), 0)
    across = lax.broadcasted_iota(jnp.int32, (modes, modes), 1)
    packed_ref[:modes, :] = jnp.where(down >= across, grams[0], grams[1])
    diagonal = jnp.sum(jnp.where(down == across, grams[1], 0.0), axis=0, keepdims=True)
    packed_ref[modes:, :] = jnp.broadcast_to(diagonal, (SUBLANES, modes))


def prepare(step, keep, send, other, top_keep, top_send, first, second, pieces):
    modes, size = first.shape
    part = jax.ShapeDtypeStruct((keep.shape[0] // 2, size), F32)
    return pl.pallas_call(
        functools.partial(prepare_kernel, len(pieces), step),
        in_specs=[VMEM] * (7 + len(pieces)),
        out_specs=[VMEM] * 4,
        out_shape=[
            jax.ShapeDtypeStruct((modes + SUBLANES, modes), F32),
            jax.ShapeDtypeStruct((2, modes, modes), F32),
            part,
            part,
        ],
        scratch_shapes=[pltpu.VMEM((size, 2 * modes), F32)],
        compiler_params=params(32),
        cost_estimate=pl.CostEstimate(
            flops=12 * size * size * modes, bytes_accessed=12 * size * size, transcendentals=0
        ),
        name="prepare",
    )(keep, send, other, top_keep, top_send, first, second, *pieces)


def fold_kernel(step, keep_ref, other_ref, after_ref, next_ref, send_ref):
    halve(step, keep_ref, other_ref, next_ref, send_ref)


def fold(step, keep, other, after):
    part = jax.ShapeDtypeStruct((keep.shape[0] // 2, keep.shape[1]), F32)
    return pl.pallas_call(
        functools.partial(fold_kernel, step),
        in_specs=[VMEM] * 2 + [pl.BlockSpec(memory_space=pl.ANY)],
        out_specs=[VMEM] * 2,
        out_shape=[part, part],
        compiler_params=params(16),
        cost_estimate=pl.CostEstimate(flops=1, bytes_accessed=1, transcendentals=0),
        name="fold",
    )(keep, other, after)


def factor(matrices):
    size = matrices[0].shape[0]
    width = SUBLANES
    down = lax.broadcasted_iota(jnp.int32, (size, size), 0)
    across = lax.broadcasted_iota(jnp.int32, (size, size), 1)
    line = lax.broadcasted_iota(jnp.int32, (width, size), 0)
    lane = lax.broadcasted_iota(jnp.int32, (width, size), 1)
    states = list(matrices)
    diagonals = [[] for _ in matrices]
    for start in range(0, size, width):
        stop = start + width
        for m, state in enumerate(states):
            spread = [
                jnp.broadcast_to(state[:, start + q : start + q + 1], (size, size))
                for q in range(width)
            ]
            strip = state[start:stop, :]
            small = [s[start:stop, :] for s in spread]
            scaled = []
            rest = strip
            for q in range(width):
                scale = lax.rsqrt(small[q][q : q + 1, :])
                tail = [small[t][q : q + 1, :] * scale for t in range(q + 1, width)]
                level = rest[q : q + 1, :] * scale
                rest = rest - small[q] * (scale * level)
                small[q] = jnp.where(line == q, 1.0, small[q]) * scale
                for t in range(q + 1, width):
                    small[t] = jnp.where(line == q, 0.0, small[t]) - small[q] * tail[t - q - 1]
                scaled.append(level)
            small = [jnp.where(line <= q, s, 0.0) for q, s in enumerate(small)]
            solved = small[0] * scaled[0]
            for q in range(1, width):
                solved = solved + small[q] * scaled[q]
            solved = jnp.where(lane >= stop, solved, 0.0)
            update = spread[0] * solved[0:1, :]
            for q in range(1, width):
                update = update + spread[q] * solved[q : q + 1, :]
            block = jnp.where(lane == line + start, 1.0, 0.0)
            kept = jnp.where(lane < start, strip, block) - solved
            parts = []
            if start > 0:
                parts.append(state[:start] - update[:start])
            parts.append(kept)
            if stop < size:
                parts.append(state[stop:] - update[stop:])
            states[m] = jnp.concatenate(parts, axis=0)
            diagonal = jnp.zeros((width, size), F32)
            for q in range(width):
                diagonal = jnp.where(lane == start + q, small[q], diagonal)
            diagonals[m].append(diagonal)
    uppers = [jnp.where(across >= down, state, 0.0) for state in states]
    return uppers, [jnp.concatenate(d, axis=0) for d in diagonals]


def finish_kernel(near_ref, far_ref, terms_ref, group_basis_ref, top_basis_ref, coupling_ref, group_ref, top_ref):
    modes = near_ref.shape[1]
    down = lax.broadcasted_iota(jnp.int32, (modes, modes), 0)
    across = lax.broadcasted_iota(jnp.int32, (modes, modes), 1)
    near, far = near_ref[:modes, :], far_ref[:modes, :]
    group = jnp.where(down >= across, near, near.T)
    top = jnp.where(down > across, far.T, far)
    diagonal = jnp.broadcast_to(far_ref[modes : modes + 1, :], top.shape)
    top = jnp.where(down == across, diagonal, top)
    uppers, diagonals = factor([group, top])
    for half in range(2):
        inverse = split(three_pass(split(uppers[half]), split(diagonals[half])))
        basis = (group_basis_ref[0], top_basis_ref[...])[half]
        left = jnp.concatenate([terms_ref[half], basis], axis=0)
        result = three_pass(split(left), inverse)
        coupling_ref[0, :, half, :] = result[:modes]
        if half == 0:
            group_ref[0] = result[modes:]
        else:
            top_ref[...] = result[modes:]


def finish(near, far, terms, group_basis, top_basis):
    modes = near.shape[1]
    return pl.pallas_call(
        finish_kernel,
        in_specs=[VMEM] * 5,
        out_specs=[VMEM] * 3,
        out_shape=[
            jax.ShapeDtypeStruct((1, modes, 2, modes), F32),
            jax.ShapeDtypeStruct(group_basis.shape, F32),
            jax.ShapeDtypeStruct(top_basis.shape, F32),
        ],
        compiler_params=params(32),
        cost_estimate=pl.CostEstimate(
            flops=20 * modes**3, bytes_accessed=24 * modes * modes, transcendentals=2 * modes
        ),
        name="finish",
    )(near, far, terms, group_basis, top_basis)


def body(
    leaf_mass, tile_mask, constraint_modes, leaf_fixed_modes, block_map, group_mass, top_mass,
    group_basis, top_basis,
):
    row_count, col_count = lax.axis_size("row"), lax.axis_size("col")
    sizes = {"row": row_count, "col": col_count}
    size = group_mass.shape[2]

    def swap(value, axis, bit):
        return lax.ppermute(value, axis, crossed(sizes[axis], bit))

    def half_of(half, own, after):
        return leaf_half(
            half, tile_mask, block_map, leaf_mass, constraint_modes, leaf_fixed_modes, own, after
        )

    basis = jnp.concatenate([group_basis[0], top_basis], axis=1)
    beside = swap(basis, "row", 1)
    first, keep, send = half_of(0, group_mass, basis)
    pair = jnp.concatenate([basis, beside], axis=0)
    pieces = [pair] + [swap(pair, "row", 2 * k) for k in range(1, row_count // 2)]
    second, top_keep, top_send = half_of(1, top_mass, pair)
    group_steps = exchanges(0, row_count, col_count)
    packed, terms, keep, send = prepare(
        group_steps[1], keep, send, swap(send, *group_steps[0]), top_keep, top_send, first, second,
        pieces,
    )

    def summed(value, axis):
        for b in range(bits_of(sizes[axis])):
            value = value + swap(value, axis, 1 << b)
        return value

    near = summed(packed, "row")
    far = summed(near, "col")
    coupling, group_modes, top_modes = finish(near, far, terms, group_basis, top_basis)

    def scattered(keep, send, steps):
        for i, step in enumerate(steps):
            other = swap(send, *step)
            if i == len(steps) - 1:
                return size * (keep + other)
            keep, send = fold(steps[i + 1], keep, other, packed)

    group_assembled = scattered(keep, send, group_steps[1:])[None]
    assembled = scattered(top_keep, top_send, exchanges(1, row_count, col_count))
    return coupling, group_modes, top_modes, group_assembled, assembled


def solution(mesh):
    leaf = P(("row", "col"), None, None)
    group = P("col", "row", None)
    in_specs = (
        leaf, leaf, leaf, leaf, leaf, group, P(("row", "col"), None), group, P("row", None),
    )
    out_specs = (
        P(("row", "col"), None, None, None), group, P("row", None), group, P(("row", "col"), None),
    )
    return jax.shard_map(body, mesh=mesh, in_specs=in_specs, out_specs=out_specs, check_vma=False)
```

```python
import functools

import jax
import jax.numpy as jnp
from jax import lax
from jax.experimental import pallas as pl
from jax.experimental.pallas import tpu as pltpu
from jax.sharding import PartitionSpec as P

TILE = 128
SUBLANES = 8
F32 = jnp.float32
BF16 = jnp.bfloat16
VMEM = pl.BlockSpec(memory_space=pltpu.VMEM)
SMEM = pl.BlockSpec(memory_space=pltpu.SMEM)
HBM = pl.BlockSpec(memory_space=pltpu.HBM)
MASS_PARTS = 4
LEAF_MEGABYTES = 48


def params(megabytes):
    return pltpu.CompilerParams(vmem_limit_bytes=int(megabytes * 2**20))


def crossed(count, bit):
    return [(i, i ^ bit) for i in range(count)]


def rows_first(left, right):
    return lax.dot_general(left, right, (((0,), (0,)), ((), ())), preferred_element_type=F32)


def add_own(ref, own, place):
    share = own.shape[0]
    if share % SUBLANES == 0:
        window = pl.ds(pl.multiple_of(place * share, SUBLANES), share)
        ref[window, :] += own
        return
    fold = SUBLANES // share
    wide = jnp.concatenate([own] * fold, axis=0)
    line = lax.broadcasted_iota(jnp.int32, wide.shape, 0) // share
    window = pl.ds(pl.multiple_of(place // fold * SUBLANES, SUBLANES), SUBLANES)
    ref[window, :] += jnp.where(line == place % fold, wide, 0.0)


def copy_rows(target_ref, start, source_ref, place, share):
    if share % SUBLANES == 0:
        window = pl.ds(pl.multiple_of(place * share, SUBLANES), share)
        target_ref[start : start + share, :] = source_ref[window, :]
        return
    for i in range(share):
        target_ref[start + i : start + i + 1, :] = source_ref[pl.ds(place * share + i, 1), :]


def bits_of(count):
    return count.bit_length() - 1


def exchanges(half, row_count, col_count):
    row = [("row", 1)] + [("row", 1 << b) for b in range(bits_of(row_count) - 1, 0, -1)]
    col = [("col", 1 << b) for b in range(bits_of(col_count))]
    return row if half == 0 else col + row


def cut_order(half, row_count, col_count):
    steps = exchanges(half, row_count, col_count)
    order = [0]
    for axis, bit in reversed(steps):
        stride = 1 if half == 0 or axis == "col" else col_count
        order = order + [place + bit * stride for place in order]
    return order


def share_place(steps):
    place = 0
    for axis, bit in steps:
        place = 2 * place + lax.rem(lax.axis_index(axis) // bit, 2)
    return place


def leaf_kernel(half, mask_ref, map_ref, mass_hbm, modes_hbm, *refs):
    if half == 0:
        after_ref, keep_ref, send_ref, loaded_ref = refs[:4]
    else:
        fixed_hbm, first_ref, after_ref, keep_ref, send_ref, moved_ref = refs[:6]
        fixed_ref, loaded_ref = refs[-2:]
        refs = refs[:-2]
    mass_ref, modes_ref, whole_ref, partial_ref, sems = refs[-5:]
    row, col = lax.axis_index("row"), lax.axis_index("col")
    row_count, col_count = lax.axis_size("row"), lax.axis_size("col")
    rows, size = modes_ref.shape
    tiles = rows // TILE
    height = rows // MASS_PARTS

    def mass_copy(i):
        window = pl.ds(pl.multiple_of(i * height, height), height)
        return pltpu.make_async_copy(
            mass_hbm.at[0, window], mass_ref.at[window], sems.at[2 + i]
        )

    half_modes = modes_hbm.at[0, :, pl.ds(half * size, size)]
    modes_copy = pltpu.make_async_copy(half_modes, modes_ref, sems.at[0])
    modes_copy.start()
    for i in range(MASS_PARTS):
        mass_copy(i).start()
    if half == 1:
        fixed_copy = pltpu.make_async_copy(fixed_hbm.at[0], fixed_ref, sems.at[1])
        fixed_copy.start()
    modes_copy.wait()

    def part(i, first):
        mass_copy(i).wait()
        lines = []
        for a in range(height // TILE):
            pieces = []
            for b in range(tiles):
                kept = mask_ref[0, i * (height // TILE) + a, b]
                window = pl.ds(pl.multiple_of(i * height + a * TILE, TILE), TILE)
                piece = mass_ref[window, b * TILE : (b + 1) * TILE]
                pieces.append(jnp.where(kept != 0, piece, jnp.zeros_like(piece)))
            lines.append(jnp.concatenate(pieces, axis=1))
        masked = jnp.concatenate(lines, axis=0)
        loaded = jnp.dot(masked, modes_ref[...], preferred_element_type=F32).astype(BF16)
        window = pl.ds(pl.multiple_of(i * height, height), height)
        loaded_ref[window, :] = loaded
        partial = rows_first(modes_ref[window, :], loaded)
        if first:
            partial_ref[...] = partial
        else:
            partial_ref[...] += partial

    part(0, True)
    lax.fori_loop(1, MASS_PARTS, lambda i, _: part(i, False), None)

    blocks = size // TILE
    to = [pl.multiple_of(map_ref[0, half, a] * TILE, TILE) for a in range(blocks)]
    for b in range(blocks):
        for a in range(blocks):
            whole_ref[pl.ds(to[a], TILE), pl.ds(to[b], TILE)] = partial_ref[
                a * TILE : (a + 1) * TILE, b * TILE : (b + 1) * TILE
            ]
    order = cut_order(half, row_count, col_count)
    share = size // len(order)
    bit = lax.rem(row if half == 0 else col, 2)
    for k, chunk in enumerate((keep_ref, send_ref)):
        for i in range(len(order) // 2):
            step = order[i + len(order) // 2] - order[i]
            copy_rows(chunk, i * share, whole_ref, order[i] + step * lax.rem(bit + k, 2), share)
    if half == 1:
        fixed_copy.wait()
        for k, ref in enumerate((first_ref, loaded_ref)):
            projected = rows_first(fixed_ref[...], ref[...])
            for b in range(blocks):
                at = pl.multiple_of(map_ref[0, k, b] * TILE, TILE)
                moved_ref[k, :, pl.ds(at, TILE)] = projected[:, b * TILE : (b + 1) * TILE]


def leaf_half(half, tile_mask, block_map, leaf_mass, constraint_modes, more, after):
    rows, size = constraint_modes.shape[1], constraint_modes.shape[2] // 2
    outs = [jax.ShapeDtypeStruct((size // 2, size), F32)] * 2
    scratch = [
        pltpu.VMEM((rows, rows), BF16),
        pltpu.VMEM((rows, size), BF16),
        pltpu.VMEM((size, size), F32),
        pltpu.VMEM((size, size), F32),
        pltpu.SemaphoreType.DMA((2 + MASS_PARTS,)),
    ]
    if half == 0:
        outs.append(jax.ShapeDtypeStruct((rows, size), BF16))
        specs = []
    else:
        modes = more[0].shape[2]
        outs.append(jax.ShapeDtypeStruct((2, modes, size), F32))
        scratch += [pltpu.VMEM((rows, modes), BF16), pltpu.VMEM((rows, size), BF16)]
        specs = [HBM, VMEM]
    return pl.pallas_call(
        functools.partial(leaf_kernel, half),
        in_specs=[SMEM] * 2 + [HBM] * 2 + specs + [pl.BlockSpec(memory_space=pl.ANY)],
        out_specs=[VMEM] * len(outs),
        out_shape=outs,
        scratch_shapes=scratch,
        compiler_params=params(LEAF_MEGABYTES),
        cost_estimate=pl.CostEstimate(
            flops=2 * rows * size * (rows + size),
            bytes_accessed=2 * rows * (rows + size) + 8 * size * size,
            transcendentals=0,
        ),
        name="leaf_group" if half == 0 else "leaf_top",
    )(tile_mask, block_map, leaf_mass, constraint_modes, *more, after)


def split(value):
    high = value.astype(BF16)
    return high, (value - high.astype(F32)).astype(BF16)


def three_pass(left, right, turn=False):
    (left_high, left_low), (right_high, right_low) = left, right
    multiply = rows_first if turn else functools.partial(jnp.dot, preferred_element_type=F32)
    width = right_high.shape[1]
    both = multiply(left_high, jnp.concatenate([right_high, right_low], axis=1))
    return both[:, :width] + both[:, width:] + multiply(left_low, right_high)


def halve(step, keep_ref, other_ref, next_ref, send_ref):
    axis, bit = step
    height = next_ref.shape[0]
    mine = lax.rem(lax.axis_index(axis) // bit, 2) == 1
    low = keep_ref[:height, :] + other_ref[:height, :]
    high = keep_ref[height:, :] + other_ref[height:, :]
    next_ref[...] = jnp.where(mine, high, low)
    send_ref[...] = jnp.where(mine, low, high)


def prepare_kernel(
    count, keep_in, send_ref, other_ref, top_keep_in, top_send_ref, moved_ref, group_own_ref,
    top_own_ref, *refs,
):
    pieces = refs[:count]
    (
        packed_ref, terms_ref, next_ref, next_send_ref, top_keep_ref, top_next_ref, bases_ref, keep_ref
    ) = refs[count:]
    modes = terms_ref.shape[2]
    size = bases_ref.shape[0]
    row, col = lax.axis_index("row"), lax.axis_index("col")
    row_count, col_count = lax.axis_size("row"), lax.axis_size("col")
    group_steps = exchanges(0, row_count, col_count)
    top_steps = exchanges(1, row_count, col_count)
    keep_ref[...] = keep_in[...]
    add_own(keep_ref, group_own_ref[0], share_place(group_steps[1:]))
    halve(group_steps[1], keep_ref, other_ref, next_ref, next_send_ref)
    top_keep_ref[...] = top_keep_in[...]
    add_own(top_keep_ref, top_own_ref[...], share_place(top_steps[1:]))
    top_next_ref[...] = top_send_ref[...]
    line = size // row_count
    for k, piece in enumerate(pieces):
        pair = lax.bitwise_xor(row // 2, k)
        for i in range(2):
            at = (2 * pair + lax.rem(row + i, 2)) * line
            bases_ref[pl.ds(pl.multiple_of(at, line), line), :] = piece[i * line : (i + 1) * line, :]
    grams = []
    for half in range(2):
        lanes = slice(half * modes, (half + 1) * modes)
        basis = split(bases_ref[:, lanes])
        order = cut_order(half, row_count, col_count)
        share = size // len(order)
        lower = jnp.concatenate(
            [bases_ref[at * share : (at + 1) * share, lanes] for at in order[: len(order) // 2]], axis=0
        )
        upper = jnp.concatenate(
            [bases_ref[at * share : (at + 1) * share, lanes] for at in order[len(order) // 2 :]], axis=0
        )
        swap = lax.rem((row, col)[half], 2) == 1
        ordered = jnp.concatenate(
            [jnp.where(swap, upper, lower), jnp.where(swap, lower, upper)], axis=0
        )
        parts = ((keep_ref, send_ref), (top_keep_ref, top_send_ref))[half]
        matrix = jnp.concatenate([part[...] for part in parts], axis=0)
        applied = three_pass(split(matrix), basis)
        gram = three_pass(split(ordered), split(applied), turn=True)
        grams.append(0.5 * (gram + gram.T))
        terms_ref[half] = three_pass(split(moved_ref[half]), basis)
    down = lax.broadcasted_iota(jnp.int32, (modes, modes), 0)
    across = lax.broadcasted_iota(jnp.int32, (modes, modes), 1)
    packed_ref[:modes, :] = jnp.where(down >= across, grams[0], grams[1])
    diagonal = jnp.sum(jnp.where(down == across, grams[1], 0.0), axis=0, keepdims=True)
    packed_ref[modes:, :] = jnp.broadcast_to(diagonal, (SUBLANES, modes))


def prepare(keep, send, other, top_keep, top_send, moved, group_own, top_own, pieces):
    _, modes, size = moved.shape
    part = jax.ShapeDtypeStruct((keep.shape[0] // 2, size), F32)
    half = jax.ShapeDtypeStruct(keep.shape, F32)
    return pl.pallas_call(
        functools.partial(prepare_kernel, len(pieces)),
        in_specs=[VMEM] * (8 + len(pieces)),
        out_specs=[VMEM] * 6,
        out_shape=[
            jax.ShapeDtypeStruct((modes + SUBLANES, modes), F32),
            jax.ShapeDtypeStruct((2, modes, modes), F32),
            part,
            part,
            half,
            half,
        ],
        scratch_shapes=[pltpu.VMEM((size, 2 * modes), F32), pltpu.VMEM(keep.shape, F32)],
        compiler_params=params(32),
        cost_estimate=pl.CostEstimate(
            flops=12 * size * size * modes, bytes_accessed=12 * size * size, transcendentals=0
        ),
        name="prepare",
    )(keep, send, other, top_keep, top_send, moved, group_own, top_own, *pieces)


def fold_kernel(step, keep_ref, other_ref, after_ref, next_ref, send_ref):
    halve(step, keep_ref, other_ref, next_ref, send_ref)


def fold(step, keep, other, after):
    part = jax.ShapeDtypeStruct((keep.shape[0] // 2, keep.shape[1]), F32)
    return pl.pallas_call(
        functools.partial(fold_kernel, step),
        in_specs=[VMEM] * 2 + [pl.BlockSpec(memory_space=pl.ANY)],
        out_specs=[VMEM] * 2,
        out_shape=[part, part],
        compiler_params=params(16),
        cost_estimate=pl.CostEstimate(flops=1, bytes_accessed=1, transcendentals=0),
        name="fold",
    )(keep, other, after)


def factor(matrices):
    size = matrices[0].shape[0]
    width = SUBLANES
    down = lax.broadcasted_iota(jnp.int32, (size, size), 0)
    across = lax.broadcasted_iota(jnp.int32, (size, size), 1)
    line = lax.broadcasted_iota(jnp.int32, (width, size), 0)
    lane = lax.broadcasted_iota(jnp.int32, (width, size), 1)
    states = list(matrices)
    diagonals = [[] for _ in matrices]
    for start in range(0, size, width):
        stop = start + width
        for m, state in enumerate(states):
            spread = [
                jnp.broadcast_to(state[:, start + q : start + q + 1], (size, size))
                for q in range(width)
            ]
            strip = state[start:stop, :]
            small = [s[start:stop, :] for s in spread]
            scaled = []
            rest = strip
            for q in range(width):
                scale = lax.rsqrt(small[q][q : q + 1, :])
                tail = [small[t][q : q + 1, :] * scale for t in range(q + 1, width)]
                level = rest[q : q + 1, :] * scale
                rest = rest - small[q] * (scale * level)
                small[q] = jnp.where(line == q, 1.0, small[q]) * scale
                for t in range(q + 1, width):
                    small[t] = jnp.where(line == q, 0.0, small[t]) - small[q] * tail[t - q - 1]
                scaled.append(level)
            small = [jnp.where(line <= q, s, 0.0) for q, s in enumerate(small)]
            solved = small[0] * scaled[0]
            for q in range(1, width):
                solved = solved + small[q] * scaled[q]
            solved = jnp.where(lane >= stop, solved, 0.0)
            update = spread[0] * solved[0:1, :]
            for q in range(1, width):
                update = update + spread[q] * solved[q : q + 1, :]
            block = jnp.where(lane == line + start, 1.0, 0.0)
            kept = jnp.where(lane < start, strip, block) - solved
            parts = []
            if start > 0:
                parts.append(state[:start] - update[:start])
            parts.append(kept)
            if stop < size:
                parts.append(state[stop:] - update[stop:])
            states[m] = jnp.concatenate(parts, axis=0)
            diagonal = jnp.zeros((width, size), F32)
            for q in range(width):
                diagonal = jnp.where(lane == start + q, small[q], diagonal)
            diagonals[m].append(diagonal)
    uppers = [jnp.where(across >= down, state, 0.0) for state in states]
    return uppers, [jnp.concatenate(d, axis=0) for d in diagonals]


def finish_kernel(
    near_ref, far_ref, terms_ref, group_basis_ref, top_basis_ref, keep_ref, other_ref, top_keep_ref,
    top_other_ref, coupling_ref, group_ref, top_ref, assembled_ref, top_assembled_ref,
):
    size = assembled_ref.shape[2]
    assembled_ref[0] = size * (keep_ref[...] + other_ref[...])
    top_assembled_ref[...] = size * (top_keep_ref[...] + top_other_ref[...])
    modes = near_ref.shape[1]
    down = lax.broadcasted_iota(jnp.int32, (modes, modes), 0)
    across = lax.broadcasted_iota(jnp.int32, (modes, modes), 1)
    near, far = near_ref[:modes, :], far_ref[:modes, :]
    group = jnp.where(down >= across, near, near.T)
    top = jnp.where(down > across, far.T, far)
    diagonal = jnp.broadcast_to(far_ref[modes : modes + 1, :], top.shape)
    top = jnp.where(down == across, diagonal, top)
    uppers, diagonals = factor([group, top])
    for half in range(2):
        inverse = split(three_pass(split(uppers[half]), split(diagonals[half])))
        basis = (group_basis_ref[0], top_basis_ref[...])[half]
        left = jnp.concatenate([terms_ref[half], basis], axis=0)
        result = three_pass(split(left), inverse)
        coupling_ref[0, :, half, :] = result[:modes]
        if half == 0:
            group_ref[0] = result[modes:]
        else:
            top_ref[...] = result[modes:]


def finish(near, far, terms, group_basis, top_basis, group_parts, top_parts):
    modes = near.shape[1]
    return pl.pallas_call(
        finish_kernel,
        in_specs=[VMEM] * 9,
        out_specs=[VMEM] * 5,
        out_shape=[
            jax.ShapeDtypeStruct((1, modes, 2, modes), F32),
            jax.ShapeDtypeStruct(group_basis.shape, F32),
            jax.ShapeDtypeStruct(top_basis.shape, F32),
            jax.ShapeDtypeStruct((1,) + group_parts[0].shape, F32),
            jax.ShapeDtypeStruct(top_parts[0].shape, F32),
        ],
        compiler_params=params(32),
        cost_estimate=pl.CostEstimate(
            flops=20 * modes**3, bytes_accessed=24 * modes * modes, transcendentals=2 * modes
        ),
        name="finish",
    )(near, far, terms, group_basis, top_basis, *group_parts, *top_parts)


def body(
    leaf_mass, tile_mask, constraint_modes, leaf_fixed_modes, block_map, group_mass, top_mass,
    group_basis, top_basis,
):
    row_count, col_count = lax.axis_size("row"), lax.axis_size("col")
    sizes = {"row": row_count, "col": col_count}

    def swap(value, axis, bit):
        return lax.ppermute(value, axis, crossed(sizes[axis], bit))

    def half_of(half, more, after):
        return leaf_half(half, tile_mask, block_map, leaf_mass, constraint_modes, more, after)

    def summed(value, axis):
        for b in range(bits_of(sizes[axis])):
            value = value + swap(value, axis, 1 << b)
        return value

    def scattered(keep, send, steps, after):
        other = swap(send, *steps[0])
        for step, later in zip(steps[:-1], steps[1:]):
            keep, send = fold(later, keep, other, after)
            other = swap(send, *later)
        return keep, other

    group_steps = exchanges(0, row_count, col_count)
    basis = jnp.concatenate([group_basis[0], top_basis], axis=1)
    beside = swap(basis, "row", 1)
    keep, send, loaded = half_of(0, [], basis)
    pair = jnp.concatenate([basis, beside], axis=0)
    pieces = [pair] + [swap(pair, "row", 2 * k) for k in range(1, row_count // 2)]
    other = swap(send, *group_steps[0])
    top_keep, top_send, moved = half_of(1, [leaf_fixed_modes, loaded], pair)
    packed, terms, keep, send, top_keep, top_send = prepare(
        keep, send, other, top_keep, top_send, moved, group_mass, top_mass, pieces
    )
    near = summed(packed, "row")
    far = summed(near, "col")
    group_parts = scattered(keep, send, group_steps[1:], packed)
    top_parts = scattered(top_keep, top_send, exchanges(1, row_count, col_count), packed)
    return finish(near, far, terms, group_basis, top_basis, group_parts, top_parts)


def solution(mesh):
    leaf = P(("row", "col"), None, None)
    group = P("col", "row", None)
    in_specs = (
        leaf, leaf, leaf, leaf, leaf, group, P(("row", "col"), None), group, P("row", None),
    )
    out_specs = (
        P(("row", "col"), None, None, None), group, P("row", None), group, P(("row", "col"), None),
    )
    return jax.shard_map(body, mesh=mesh, in_specs=in_specs, out_specs=out_specs, check_vma=False)
```

```python
import functools

import jax
import jax.numpy as jnp
from jax import lax
from jax.experimental import pallas as pl
from jax.experimental.pallas import tpu as pltpu
from jax.sharding import PartitionSpec as P

TILE = 128
SUBLANES = 8
F32 = jnp.float32
BF16 = jnp.bfloat16
VMEM = pl.BlockSpec(memory_space=pltpu.VMEM)
SMEM = pl.BlockSpec(memory_space=pltpu.SMEM)
HBM = pl.BlockSpec(memory_space=pltpu.HBM)
MASS_PARTS = 4
LEAF_MEGABYTES = 48


def params(megabytes):
    return pltpu.CompilerParams(vmem_limit_bytes=int(megabytes * 2**20))


def crossed(count, bit):
    return [(i, i ^ bit) for i in range(count)]


def rows_first(left, right):
    return lax.dot_general(left, right, (((0,), (0,)), ((), ())), preferred_element_type=F32)


def add_own(ref, own, place):
    share = own.shape[0]
    if share % SUBLANES == 0:
        window = pl.ds(pl.multiple_of(place * share, SUBLANES), share)
        ref[window, :] += own
        return
    fold = SUBLANES // share
    wide = jnp.concatenate([own] * fold, axis=0)
    line = lax.broadcasted_iota(jnp.int32, wide.shape, 0) // share
    window = pl.ds(pl.multiple_of(place // fold * SUBLANES, SUBLANES), SUBLANES)
    ref[window, :] += jnp.where(line == place % fold, wide, 0.0)


def copy_rows(target_ref, start, source_ref, place, share):
    if share % SUBLANES == 0:
        window = pl.ds(pl.multiple_of(place * share, SUBLANES), share)
        target_ref[start : start + share, :] = source_ref[window, :]
        return
    for i in range(share):
        target_ref[start + i : start + i + 1, :] = source_ref[pl.ds(place * share + i, 1), :]


def bits_of(count):
    return count.bit_length() - 1


def exchanges(half, row_count, col_count):
    row = [("row", 1)] + [("row", 1 << b) for b in range(bits_of(row_count) - 1, 0, -1)]
    col = [("col", 1 << b) for b in range(bits_of(col_count))]
    return row if half == 0 else col + row


def cut_order(half, row_count, col_count):
    steps = exchanges(half, row_count, col_count)
    order = [0]
    for axis, bit in reversed(steps):
        stride = 1 if half == 0 or axis == "col" else col_count
        order = order + [place + bit * stride for place in order]
    return order


def share_place(steps):
    place = 0
    for axis, bit in steps:
        place = 2 * place + lax.rem(lax.axis_index(axis) // bit, 2)
    return place


def leaf_kernel(half, mask_ref, map_ref, mass_hbm, modes_hbm, *refs):
    if half == 0:
        after_ref, keep_ref, send_ref, loaded_ref = refs[:4]
    else:
        fixed_hbm, first_ref, after_ref, keep_ref, send_ref, moved_ref = refs[:6]
        fixed_ref, loaded_ref = refs[-2:]
        refs = refs[:-2]
    mass_ref, modes_ref, whole_ref, partial_ref, sems = refs[-5:]
    row, col = lax.axis_index("row"), lax.axis_index("col")
    row_count, col_count = lax.axis_size("row"), lax.axis_size("col")
    rows, size = modes_ref.shape
    tiles = rows // TILE
    height = rows // MASS_PARTS

    def mass_copy(i):
        window = pl.ds(pl.multiple_of(i * height, height), height)
        return pltpu.make_async_copy(
            mass_hbm.at[0, window], mass_ref.at[window], sems.at[2 + i]
        )

    half_modes = modes_hbm.at[0, :, pl.ds(half * size, size)]
    modes_copy = pltpu.make_async_copy(half_modes, modes_ref, sems.at[0])
    modes_copy.start()
    for i in range(MASS_PARTS):
        mass_copy(i).start()
    if half == 1:
        fixed_copy = pltpu.make_async_copy(fixed_hbm.at[0], fixed_ref, sems.at[1])
        fixed_copy.start()
    modes_copy.wait()

    def part(i, first):
        mass_copy(i).wait()
        lines = []
        for a in range(height // TILE):
            pieces = []
            for b in range(tiles):
                kept = mask_ref[0, i * (height // TILE) + a, b]
                window = pl.ds(pl.multiple_of(i * height + a * TILE, TILE), TILE)
                piece = mass_ref[window, b * TILE : (b + 1) * TILE]
                pieces.append(jnp.where(kept != 0, piece, jnp.zeros_like(piece)))
            lines.append(jnp.concatenate(pieces, axis=1))
        masked = jnp.concatenate(lines, axis=0)
        loaded = jnp.dot(masked, modes_ref[...], preferred_element_type=F32).astype(BF16)
        window = pl.ds(pl.multiple_of(i * height, height), height)
        loaded_ref[window, :] = loaded
        if not first:
            add_partial(i - 1)

    def add_partial(i):
        window = pl.ds(pl.multiple_of(i * height, height), height)
        partial_ref[...] += rows_first(modes_ref[window, :], loaded_ref[window, :])

    partial_ref[...] = jnp.zeros_like(partial_ref)
    part(0, True)
    lax.fori_loop(1, MASS_PARTS, lambda i, _: part(i, False), None)
    add_partial(MASS_PARTS - 1)

    blocks = size // TILE
    to = [pl.multiple_of(map_ref[0, half, a] * TILE, TILE) for a in range(blocks)]
    for b in range(blocks):
        for a in range(blocks):
            whole_ref[pl.ds(to[a], TILE), pl.ds(to[b], TILE)] = partial_ref[
                a * TILE : (a + 1) * TILE, b * TILE : (b + 1) * TILE
            ]
    order = cut_order(half, row_count, col_count)
    share = size // len(order)
    bit = lax.rem(row if half == 0 else col, 2)
    for k, chunk in enumerate((keep_ref, send_ref)):
        for i in range(len(order) // 2):
            step = order[i + len(order) // 2] - order[i]
            copy_rows(chunk, i * share, whole_ref, order[i] + step * lax.rem(bit + k, 2), share)
    if half == 1:
        fixed_copy.wait()
        for k, ref in enumerate((first_ref, loaded_ref)):
            projected = rows_first(fixed_ref[...], ref[...])
            for b in range(blocks):
                at = pl.multiple_of(map_ref[0, k, b] * TILE, TILE)
                moved_ref[k, :, pl.ds(at, TILE)] = projected[:, b * TILE : (b + 1) * TILE]


def leaf_half(half, tile_mask, block_map, leaf_mass, constraint_modes, more, after):
    rows, size = constraint_modes.shape[1], constraint_modes.shape[2] // 2
    outs = [jax.ShapeDtypeStruct((size // 2, size), F32)] * 2
    scratch = [
        pltpu.VMEM((rows, rows), BF16),
        pltpu.VMEM((rows, size), BF16),
        pltpu.VMEM((size, size), F32),
        pltpu.VMEM((size, size), F32),
        pltpu.SemaphoreType.DMA((2 + MASS_PARTS,)),
    ]
    if half == 0:
        outs.append(jax.ShapeDtypeStruct((rows, size), BF16))
        specs = []
    else:
        modes = more[0].shape[2]
        outs.append(jax.ShapeDtypeStruct((2, modes, size), F32))
        scratch += [pltpu.VMEM((rows, modes), BF16), pltpu.VMEM((rows, size), BF16)]
        specs = [HBM, VMEM]
    return pl.pallas_call(
        functools.partial(leaf_kernel, half),
        in_specs=[SMEM] * 2 + [HBM] * 2 + specs + [pl.BlockSpec(memory_space=pl.ANY)],
        out_specs=[VMEM] * len(outs),
        out_shape=outs,
        scratch_shapes=scratch,
        compiler_params=params(LEAF_MEGABYTES),
        cost_estimate=pl.CostEstimate(
            flops=2 * rows * size * (rows + size),
            bytes_accessed=2 * rows * (rows + size) + 8 * size * size,
            transcendentals=0,
        ),
        name="leaf_group" if half == 0 else "leaf_top",
    )(tile_mask, block_map, leaf_mass, constraint_modes, *more, after)


def split(value):
    high = value.astype(BF16)
    return high, (value - high.astype(F32)).astype(BF16)


def three_pass(left, right, turn=False):
    (left_high, left_low), (right_high, right_low) = left, right
    multiply = rows_first if turn else functools.partial(jnp.dot, preferred_element_type=F32)
    width = right_high.shape[1]
    both = multiply(left_high, jnp.concatenate([right_high, right_low], axis=1))
    return both[:, :width] + both[:, width:] + multiply(left_low, right_high)


def halve(step, keep_ref, other_ref, next_ref, send_ref):
    axis, bit = step
    height = next_ref.shape[0]
    mine = lax.rem(lax.axis_index(axis) // bit, 2) == 1
    low = keep_ref[:height, :] + other_ref[:height, :]
    high = keep_ref[height:, :] + other_ref[height:, :]
    next_ref[...] = jnp.where(mine, high, low)
    send_ref[...] = jnp.where(mine, low, high)


def prepare_kernel(
    count, keep_in, send_ref, other_ref, top_keep_in, top_send_ref, moved_ref, group_own_ref,
    top_own_ref, *refs,
):
    pieces = refs[:count]
    (
        packed_ref, terms_ref, next_ref, next_send_ref, top_keep_ref, top_next_ref, bases_ref, keep_ref
    ) = refs[count:]
    modes = terms_ref.shape[2]
    size = bases_ref.shape[0]
    row, col = lax.axis_index("row"), lax.axis_index("col")
    row_count, col_count = lax.axis_size("row"), lax.axis_size("col")
    group_steps = exchanges(0, row_count, col_count)
    top_steps = exchanges(1, row_count, col_count)
    keep_ref[...] = keep_in[...]
    add_own(keep_ref, group_own_ref[0], share_place(group_steps[1:]))
    halve(group_steps[1], keep_ref, other_ref, next_ref, next_send_ref)
    top_keep_ref[...] = top_keep_in[...]
    add_own(top_keep_ref, top_own_ref[...], share_place(top_steps[1:]))
    top_next_ref[...] = top_send_ref[...]
    line = size // row_count
    for k, piece in enumerate(pieces):
        pair = lax.bitwise_xor(row // 2, k)
        for i in range(2):
            at = (2 * pair + lax.rem(row + i, 2)) * line
            bases_ref[pl.ds(pl.multiple_of(at, line), line), :] = piece[i * line : (i + 1) * line, :]
    grams = []
    for half in range(2):
        lanes = slice(half * modes, (half + 1) * modes)
        basis = split(bases_ref[:, lanes])
        order = cut_order(half, row_count, col_count)
        share = size // len(order)
        lower = jnp.concatenate(
            [bases_ref[at * share : (at + 1) * share, lanes] for at in order[: len(order) // 2]], axis=0
        )
        upper = jnp.concatenate(
            [bases_ref[at * share : (at + 1) * share, lanes] for at in order[len(order) // 2 :]], axis=0
        )
        swap = lax.rem((row, col)[half], 2) == 1
        ordered = jnp.concatenate(
            [jnp.where(swap, upper, lower), jnp.where(swap, lower, upper)], axis=0
        )
        parts = ((keep_ref, send_ref), (top_keep_ref, top_send_ref))[half]
        matrix = jnp.concatenate([part[...] for part in parts], axis=0)
        applied = three_pass(split(matrix), basis)
        gram = three_pass(split(ordered), split(applied), turn=True)
        grams.append(0.5 * (gram + gram.T))
        terms_ref[half] = three_pass(split(moved_ref[half]), basis)
    down = lax.broadcasted_iota(jnp.int32, (modes, modes), 0)
    across = lax.broadcasted_iota(jnp.int32, (modes, modes), 1)
    packed_ref[:modes, :] = jnp.where(down >= across, grams[0], grams[1])
    diagonal = jnp.sum(jnp.where(down == across, grams[1], 0.0), axis=0, keepdims=True)
    packed_ref[modes:, :] = jnp.broadcast_to(diagonal, (SUBLANES, modes))


def prepare(keep, send, other, top_keep, top_send, moved, group_own, top_own, pieces):
    _, modes, size = moved.shape
    part = jax.ShapeDtypeStruct((keep.shape[0] // 2, size), F32)
    half = jax.ShapeDtypeStruct(keep.shape, F32)
    return pl.pallas_call(
        functools.partial(prepare_kernel, len(pieces)),
        in_specs=[VMEM] * (8 + len(pieces)),
        out_specs=[VMEM] * 6,
        out_shape=[
            jax.ShapeDtypeStruct((modes + SUBLANES, modes), F32),
            jax.ShapeDtypeStruct((2, modes, modes), F32),
            part,
            part,
            half,
            half,
        ],
        scratch_shapes=[pltpu.VMEM((size, 2 * modes), F32), pltpu.VMEM(keep.shape, F32)],
        compiler_params=params(32),
        cost_estimate=pl.CostEstimate(
            flops=12 * size * size * modes, bytes_accessed=12 * size * size, transcendentals=0
        ),
        name="prepare",
    )(keep, send, other, top_keep, top_send, moved, group_own, top_own, *pieces)


def fold_kernel(step, after_count, keep_ref, other_ref, *refs):
    halve(step, keep_ref, other_ref, *refs[after_count:])


def fold(step, keep, other, *after):
    part = jax.ShapeDtypeStruct((keep.shape[0] // 2, keep.shape[1]), F32)
    return pl.pallas_call(
        functools.partial(fold_kernel, step, len(after)),
        in_specs=[VMEM] * 2 + [pl.BlockSpec(memory_space=pl.ANY)] * len(after),
        out_specs=[VMEM] * 2,
        out_shape=[part, part],
        compiler_params=params(16),
        cost_estimate=pl.CostEstimate(flops=1, bytes_accessed=1, transcendentals=0),
        name="fold",
    )(keep, other, *after)


def add_kernel(left_ref, right_ref, *refs):
    refs[-1][...] = left_ref[...] + right_ref[...]


def add(left, right, *after):
    return pl.pallas_call(
        add_kernel,
        in_specs=[VMEM] * 2 + [pl.BlockSpec(memory_space=pl.ANY)] * len(after),
        out_specs=VMEM,
        out_shape=jax.ShapeDtypeStruct(left.shape, F32),
        compiler_params=params(16),
        cost_estimate=pl.CostEstimate(flops=1, bytes_accessed=1, transcendentals=0),
        name="add",
    )(left, right, *after)


def last_kernel(keep_ref, other_ref, top_keep_ref, top_other_ref, after_ref, group_ref, top_ref):
    size = group_ref.shape[2]
    group_ref[0] = size * (keep_ref[...] + other_ref[...])
    top_ref[...] = size * (top_keep_ref[...] + top_other_ref[...])


def last(keep, other, top_keep, top_other, after):
    return pl.pallas_call(
        last_kernel,
        in_specs=[VMEM] * 4 + [pl.BlockSpec(memory_space=pl.ANY)],
        out_specs=[VMEM] * 2,
        out_shape=[
            jax.ShapeDtypeStruct((1,) + keep.shape, F32),
            jax.ShapeDtypeStruct(top_keep.shape, F32),
        ],
        compiler_params=params(16),
        cost_estimate=pl.CostEstimate(flops=1, bytes_accessed=1, transcendentals=0),
        name="last",
    )(keep, other, top_keep, top_other, after)


def factor(matrices):
    size = matrices[0].shape[0]
    width = SUBLANES
    down = lax.broadcasted_iota(jnp.int32, (size, size), 0)
    across = lax.broadcasted_iota(jnp.int32, (size, size), 1)
    line = lax.broadcasted_iota(jnp.int32, (width, size), 0)
    lane = lax.broadcasted_iota(jnp.int32, (width, size), 1)
    states = list(matrices)
    diagonals = [[] for _ in matrices]
    for start in range(0, size, width):
        stop = start + width
        for m, state in enumerate(states):
            spread = [
                jnp.broadcast_to(state[:, start + q : start + q + 1], (size, size))
                for q in range(width)
            ]
            strip = state[start:stop, :]
            small = [s[start:stop, :] for s in spread]
            scaled = []
            rest = strip
            for q in range(width):
                scale = lax.rsqrt(small[q][q : q + 1, :])
                tail = [small[t][q : q + 1, :] * scale for t in range(q + 1, width)]
                level = rest[q : q + 1, :] * scale
                rest = rest - small[q] * (scale * level)
                small[q] = jnp.where(line == q, 1.0, small[q]) * scale
                for t in range(q + 1, width):
                    small[t] = jnp.where(line == q, 0.0, small[t]) - small[q] * tail[t - q - 1]
                scaled.append(level)
            small = [jnp.where(line <= q, s, 0.0) for q, s in enumerate(small)]
            solved = small[0] * scaled[0]
            for q in range(1, width):
                solved = solved + small[q] * scaled[q]
            solved = jnp.where(lane >= stop, solved, 0.0)
            update = spread[0] * solved[0:1, :]
            for q in range(1, width):
                update = update + spread[q] * solved[q : q + 1, :]
            block = jnp.where(lane == line + start, 1.0, 0.0)
            kept = jnp.where(lane < start, strip, block) - solved
            parts = []
            if start > 0:
                parts.append(state[:start] - update[:start])
            parts.append(kept)
            if stop < size:
                parts.append(state[stop:] - update[stop:])
            states[m] = jnp.concatenate(parts, axis=0)
            diagonal = jnp.zeros((width, size), F32)
            for q in range(width):
                diagonal = jnp.where(lane == start + q, small[q], diagonal)
            diagonals[m].append(diagonal)
    uppers = [jnp.where(across >= down, state, 0.0) for state in states]
    return uppers, [jnp.concatenate(d, axis=0) for d in diagonals]


def finish_kernel(
    near_ref, far_ref, terms_ref, group_basis_ref, top_basis_ref, coupling_ref, group_ref, top_ref,
):
    modes = near_ref.shape[1]
    down = lax.broadcasted_iota(jnp.int32, (modes, modes), 0)
    across = lax.broadcasted_iota(jnp.int32, (modes, modes), 1)
    near, far = near_ref[:modes, :], far_ref[:modes, :]
    group = jnp.where(down >= across, near, near.T)
    top = jnp.where(down > across, far.T, far)
    diagonal = jnp.broadcast_to(far_ref[modes : modes + 1, :], top.shape)
    top = jnp.where(down == across, diagonal, top)
    uppers, diagonals = factor([group, top])
    for half in range(2):
        inverse = split(three_pass(split(uppers[half]), split(diagonals[half])))
        basis = (group_basis_ref[0], top_basis_ref[...])[half]
        left = jnp.concatenate([terms_ref[half], basis], axis=0)
        result = three_pass(split(left), inverse)
        coupling_ref[0, :, half, :] = result[:modes]
        if half == 0:
            group_ref[0] = result[modes:]
        else:
            top_ref[...] = result[modes:]


def finish(near, far, terms, group_basis, top_basis):
    modes = near.shape[1]
    return pl.pallas_call(
        finish_kernel,
        in_specs=[VMEM] * 5,
        out_specs=[VMEM] * 3,
        out_shape=[
            jax.ShapeDtypeStruct((1, modes, 2, modes), F32),
            jax.ShapeDtypeStruct(group_basis.shape, F32),
            jax.ShapeDtypeStruct(top_basis.shape, F32),
        ],
        compiler_params=params(32),
        cost_estimate=pl.CostEstimate(
            flops=20 * modes**3, bytes_accessed=24 * modes * modes, transcendentals=2 * modes
        ),
        name="finish",
    )(near, far, terms, group_basis, top_basis)


def body(
    leaf_mass, tile_mask, constraint_modes, leaf_fixed_modes, block_map, group_mass, top_mass,
    group_basis, top_basis,
):
    row_count, col_count = lax.axis_size("row"), lax.axis_size("col")
    sizes = {"row": row_count, "col": col_count}

    def swap(value, axis, bit):
        return lax.ppermute(value, axis, crossed(sizes[axis], bit))

    def half_of(half, more, after):
        return leaf_half(half, tile_mask, block_map, leaf_mass, constraint_modes, more, after)

    group_steps = exchanges(0, row_count, col_count)
    basis = jnp.concatenate([group_basis[0], top_basis], axis=1)
    beside = swap(basis, "row", 1)
    keep, send, loaded = half_of(0, [], basis)
    pair = jnp.concatenate([basis, beside], axis=0)
    pieces = [pair] + [swap(pair, "row", 2 * k) for k in range(1, row_count // 2)]
    other = swap(send, *group_steps[0])
    top_keep, top_send, moved = half_of(1, [leaf_fixed_modes, loaded], pair)
    packed, terms, keep, send, top_keep, top_send = prepare(
        keep, send, other, top_keep, top_send, moved, group_mass, top_mass, pieces
    )
    group_left = group_steps[1:]
    top_left = exchanges(1, row_count, col_count)
    sums = [("row", 1 << b) for b in range(bits_of(row_count))]
    sums += [("col", 1 << b) for b in range(bits_of(col_count))]
    value = near = packed
    group_other, top_other = None, swap(top_send, *top_left[0])
    for i, step in enumerate(sums):
        other = swap(value, *step)
        after = []
        if i == 0:
            group_other = swap(send, *group_left[0])
        if len(top_left) > 1 and i != 1:
            top_keep, top_send = fold(top_left[1], top_keep, top_other, value)
            top_left = top_left[1:]
            top_other = swap(top_send, *top_left[0])
            after.append(top_send)
        if len(group_left) > 1 and i >= len(sums) - len(group_left) + 1:
            keep, send = fold(group_left[1], keep, group_other, value)
            group_left = group_left[1:]
            group_other = swap(send, *group_left[0])
            after.append(send)
        value = add(value, other, *after)
        if i == bits_of(row_count) - 1:
            near = value
    while len(top_left) > 1:
        top_keep, top_send = fold(top_left[1], top_keep, top_other, value)
        top_left = top_left[1:]
        top_other = swap(top_send, *top_left[0])
    coupling, group_modes, top_modes = finish(near, value, terms, group_basis, top_basis)
    assembled, top_assembled = last(keep, group_other, top_keep, top_other, top_modes)
    return coupling, group_modes, top_modes, assembled, top_assembled


def solution(mesh):
    leaf = P(("row", "col"), None, None)
    group = P("col", "row", None)
    in_specs = (
        leaf, leaf, leaf, leaf, leaf, group, P(("row", "col"), None), group, P("row", None),
    )
    out_specs = (
        P(("row", "col"), None, None, None), group, P("row", None), group, P(("row", "col"), None),
    )
    return jax.shard_map(body, mesh=mesh, in_specs=in_specs, out_specs=out_specs, check_vma=False)
```

```python
import functools

import jax
import jax.numpy as jnp
from jax import lax
from jax.experimental import pallas as pl
from jax.experimental.pallas import tpu as pltpu
from jax.sharding import PartitionSpec as P

TILE = 128
SUBLANES = 8
F32 = jnp.float32
BF16 = jnp.bfloat16
VMEM = pl.BlockSpec(memory_space=pltpu.VMEM)
SMEM = pl.BlockSpec(memory_space=pltpu.SMEM)
HBM = pl.BlockSpec(memory_space=pltpu.HBM)
MASS_PARTS = 2
LEAF_MEGABYTES = 48


def params(megabytes):
    return pltpu.CompilerParams(vmem_limit_bytes=int(megabytes * 2**20))


def crossed(count, bit):
    return [(i, i ^ bit) for i in range(count)]


def rows_first(left, right):
    return lax.dot_general(left, right, (((0,), (0,)), ((), ())), preferred_element_type=F32)


def add_own(ref, own, place):
    share = own.shape[0]
    if share % SUBLANES == 0:
        window = pl.ds(pl.multiple_of(place * share, SUBLANES), share)
        ref[window, :] += own
        return
    fold = SUBLANES // share
    wide = jnp.concatenate([own] * fold, axis=0)
    line = lax.broadcasted_iota(jnp.int32, wide.shape, 0) // share
    window = pl.ds(pl.multiple_of(place // fold * SUBLANES, SUBLANES), SUBLANES)
    ref[window, :] += jnp.where(line == place % fold, wide, 0.0)


def copy_rows(target_ref, start, source_ref, place, share):
    if share % SUBLANES == 0:
        window = pl.ds(pl.multiple_of(place * share, SUBLANES), share)
        target_ref[start : start + share, :] = source_ref[window, :]
        return
    for i in range(share):
        target_ref[start + i : start + i + 1, :] = source_ref[pl.ds(place * share + i, 1), :]


def bits_of(count):
    return count.bit_length() - 1


def exchanges(half, row_count, col_count):
    row = [("row", 1)] + [("row", 1 << b) for b in range(bits_of(row_count) - 1, 0, -1)]
    col = [("col", 1 << b) for b in range(bits_of(col_count))]
    return row if half == 0 else col + row


def cut_order(half, row_count, col_count):
    steps = exchanges(half, row_count, col_count)
    order = [0]
    for axis, bit in reversed(steps):
        stride = 1 if half == 0 or axis == "col" else col_count
        order = order + [place + bit * stride for place in order]
    return order


def share_place(steps):
    place = 0
    for axis, bit in steps:
        place = 2 * place + lax.rem(lax.axis_index(axis) // bit, 2)
    return place


def leaf_kernel(half, mask_ref, map_ref, mass_hbm, modes_hbm, *refs):
    if half == 0:
        after_ref, keep_ref, send_ref, loaded_ref = refs[:4]
    else:
        fixed_hbm, first_ref, after_ref, keep_ref, send_ref, moved_ref = refs[:6]
        fixed_ref, loaded_ref = refs[-2:]
        refs = refs[:-2]
    mass_ref, modes_ref, whole_ref, partial_ref, sems = refs[-5:]
    row, col = lax.axis_index("row"), lax.axis_index("col")
    row_count, col_count = lax.axis_size("row"), lax.axis_size("col")
    rows, size = modes_ref.shape
    tiles = rows // TILE
    height = rows // MASS_PARTS

    def mass_copy(i):
        window = pl.ds(pl.multiple_of(i * height, height), height)
        return pltpu.make_async_copy(
            mass_hbm.at[0, window], mass_ref.at[window], sems.at[2 + i]
        )

    half_modes = modes_hbm.at[0, :, pl.ds(half * size, size)]
    modes_copy = pltpu.make_async_copy(half_modes, modes_ref, sems.at[0])
    modes_copy.start()
    for i in range(MASS_PARTS):
        mass_copy(i).start()
    if half == 1:
        fixed_copy = pltpu.make_async_copy(fixed_hbm.at[0], fixed_ref, sems.at[1])
        fixed_copy.start()
    modes_copy.wait()

    def part(i, first):
        mass_copy(i).wait()
        lines = []
        for a in range(height // TILE):
            pieces = []
            for b in range(tiles):
                kept = mask_ref[0, i * (height // TILE) + a, b]
                window = pl.ds(pl.multiple_of(i * height + a * TILE, TILE), TILE)
                piece = mass_ref[window, b * TILE : (b + 1) * TILE]
                pieces.append(jnp.where(kept != 0, piece, jnp.zeros_like(piece)))
            lines.append(jnp.concatenate(pieces, axis=1))
        masked = jnp.concatenate(lines, axis=0)
        loaded = jnp.dot(masked, modes_ref[...], preferred_element_type=F32).astype(BF16)
        window = pl.ds(pl.multiple_of(i * height, height), height)
        loaded_ref[window, :] = loaded
        partial = rows_first(modes_ref[window, :], loaded)
        if first:
            partial_ref[...] = partial
        else:
            partial_ref[...] += partial

    part(0, True)
    lax.fori_loop(1, MASS_PARTS, lambda i, _: part(i, False), None)

    blocks = size // TILE
    to = [pl.multiple_of(map_ref[0, half, a] * TILE, TILE) for a in range(blocks)]
    for b in range(blocks):
        for a in range(blocks):
            whole_ref[pl.ds(to[a], TILE), pl.ds(to[b], TILE)] = partial_ref[
                a * TILE : (a + 1) * TILE, b * TILE : (b + 1) * TILE
            ]
    order = cut_order(half, row_count, col_count)
    share = size // len(order)
    bit = lax.rem(row if half == 0 else col, 2)
    for k, chunk in enumerate((keep_ref, send_ref)):
        for i in range(len(order) // 2):
            step = order[i + len(order) // 2] - order[i]
            copy_rows(chunk, i * share, whole_ref, order[i] + step * lax.rem(bit + k, 2), share)
    if half == 1:
        fixed_copy.wait()
        for k, ref in enumerate((first_ref, loaded_ref)):
            projected = rows_first(fixed_ref[...], ref[...])
            for b in range(blocks):
                at = pl.multiple_of(map_ref[0, k, b] * TILE, TILE)
                moved_ref[k, :, pl.ds(at, TILE)] = projected[:, b * TILE : (b + 1) * TILE]


def leaf_half(half, tile_mask, block_map, leaf_mass, constraint_modes, more, after):
    rows, size = constraint_modes.shape[1], constraint_modes.shape[2] // 2
    outs = [jax.ShapeDtypeStruct((size // 2, size), F32)] * 2
    scratch = [
        pltpu.VMEM((rows, rows), BF16),
        pltpu.VMEM((rows, size), BF16),
        pltpu.VMEM((size, size), F32),
        pltpu.VMEM((size, size), F32),
        pltpu.SemaphoreType.DMA((2 + MASS_PARTS,)),
    ]
    if half == 0:
        outs.append(jax.ShapeDtypeStruct((rows, size), BF16))
        specs = []
    else:
        modes = more[0].shape[2]
        outs.append(jax.ShapeDtypeStruct((2, modes, size), F32))
        scratch += [pltpu.VMEM((rows, modes), BF16), pltpu.VMEM((rows, size), BF16)]
        specs = [HBM, VMEM]
    return pl.pallas_call(
        functools.partial(leaf_kernel, half),
        in_specs=[SMEM] * 2 + [HBM] * 2 + specs + [pl.BlockSpec(memory_space=pl.ANY)],
        out_specs=[VMEM] * len(outs),
        out_shape=outs,
        scratch_shapes=scratch,
        compiler_params=params(LEAF_MEGABYTES),
        cost_estimate=pl.CostEstimate(
            flops=2 * rows * size * (rows + size),
            bytes_accessed=2 * rows * (rows + size) + 8 * size * size,
            transcendentals=0,
        ),
        name="leaf_group" if half == 0 else "leaf_top",
    )(tile_mask, block_map, leaf_mass, constraint_modes, *more, after)


def split(value):
    high = value.astype(BF16)
    return high, (value - high.astype(F32)).astype(BF16)


def three_pass(left, right, turn=False):
    (left_high, left_low), (right_high, right_low) = left, right
    multiply = rows_first if turn else functools.partial(jnp.dot, preferred_element_type=F32)
    width = right_high.shape[1]
    both = multiply(left_high, jnp.concatenate([right_high, right_low], axis=1))
    return both[:, :width] + both[:, width:] + multiply(left_low, right_high)


def halve(step, keep_ref, other_ref, next_ref, send_ref):
    axis, bit = step
    height = next_ref.shape[0]
    mine = lax.rem(lax.axis_index(axis) // bit, 2) == 1
    low = keep_ref[:height, :] + other_ref[:height, :]
    high = keep_ref[height:, :] + other_ref[height:, :]
    next_ref[...] = jnp.where(mine, high, low)
    send_ref[...] = jnp.where(mine, low, high)


def prepare_kernel(
    count, keep_in, send_ref, top_keep_in, top_send_ref, moved_ref, group_own_ref,
    top_own_ref, *refs,
):
    pieces = refs[1 : count + 1]
    (
        packed_ref, terms_ref, keep_ref, top_keep_ref, top_next_ref, bases_ref
    ) = refs[count + 1 :]
    modes = terms_ref.shape[2]
    size = bases_ref.shape[0]
    row, col = lax.axis_index("row"), lax.axis_index("col")
    row_count, col_count = lax.axis_size("row"), lax.axis_size("col")
    group_steps = exchanges(0, row_count, col_count)
    top_steps = exchanges(1, row_count, col_count)
    keep_ref[...] = keep_in[...]
    add_own(keep_ref, group_own_ref[0], share_place(group_steps[1:]))
    top_keep_ref[...] = top_keep_in[...]
    add_own(top_keep_ref, top_own_ref[...], share_place(top_steps[1:]))
    top_next_ref[...] = top_send_ref[...]
    line = size // row_count
    for k, piece in enumerate(pieces):
        pair = lax.bitwise_xor(row // 2, k)
        for i in range(2):
            at = (2 * pair + lax.rem(row + i, 2)) * line
            bases_ref[pl.ds(pl.multiple_of(at, line), line), :] = piece[i * line : (i + 1) * line, :]
    grams = []
    for half in range(2):
        lanes = slice(half * modes, (half + 1) * modes)
        basis = split(bases_ref[:, lanes])
        order = cut_order(half, row_count, col_count)
        share = size // len(order)
        lower = jnp.concatenate(
            [bases_ref[at * share : (at + 1) * share, lanes] for at in order[: len(order) // 2]], axis=0
        )
        upper = jnp.concatenate(
            [bases_ref[at * share : (at + 1) * share, lanes] for at in order[len(order) // 2 :]], axis=0
        )
        swap = lax.rem((row, col)[half], 2) == 1
        ordered = jnp.concatenate(
            [jnp.where(swap, upper, lower), jnp.where(swap, lower, upper)], axis=0
        )
        parts = ((keep_ref, send_ref), (top_keep_ref, top_send_ref))[half]
        matrix = jnp.concatenate([part[...] for part in parts], axis=0)
        applied = three_pass(split(matrix), basis)
        gram = three_pass(split(ordered), split(applied), turn=True)
        grams.append(0.5 * (gram + gram.T))
        terms_ref[half] = three_pass(split(moved_ref[half]), basis)
    down = lax.broadcasted_iota(jnp.int32, (modes, modes), 0)
    across = lax.broadcasted_iota(jnp.int32, (modes, modes), 1)
    packed_ref[:modes, :] = jnp.where(down >= across, grams[0], grams[1])
    diagonal = jnp.sum(jnp.where(down == across, grams[1], 0.0), axis=0, keepdims=True)
    packed_ref[modes:, :] = jnp.broadcast_to(diagonal, (SUBLANES, modes))


def prepare(keep, send, top_keep, top_send, moved, group_own, top_own, after, pieces):
    _, modes, size = moved.shape
    half = jax.ShapeDtypeStruct(keep.shape, F32)
    return pl.pallas_call(
        functools.partial(prepare_kernel, len(pieces)),
        in_specs=[VMEM] * 7 + [pl.BlockSpec(memory_space=pl.ANY)] + [VMEM] * len(pieces),
        out_specs=[VMEM] * 5,
        out_shape=[
            jax.ShapeDtypeStruct((modes + SUBLANES, modes), F32),
            jax.ShapeDtypeStruct((2, modes, modes), F32),
            half,
            half,
            half,
        ],
        scratch_shapes=[pltpu.VMEM((size, 2 * modes), F32)],
        compiler_params=params(32),
        cost_estimate=pl.CostEstimate(
            flops=12 * size * size * modes, bytes_accessed=12 * size * size, transcendentals=0
        ),
        name="prepare",
    )(keep, send, top_keep, top_send, moved, group_own, top_own, after, *pieces)


def fold_kernel(step, after_count, keep_ref, other_ref, *refs):
    halve(step, keep_ref, other_ref, *refs[after_count:])


def fold(step, keep, other, *after):
    part = jax.ShapeDtypeStruct((keep.shape[0] // 2, keep.shape[1]), F32)
    return pl.pallas_call(
        functools.partial(fold_kernel, step, len(after)),
        in_specs=[VMEM] * 2 + [pl.BlockSpec(memory_space=pl.ANY)] * len(after),
        out_specs=[VMEM] * 2,
        out_shape=[part, part],
        compiler_params=params(16),
        cost_estimate=pl.CostEstimate(flops=1, bytes_accessed=1, transcendentals=0),
        name="fold",
    )(keep, other, *after)


def add_kernel(left_ref, right_ref, *refs):
    refs[-1][...] = left_ref[...] + right_ref[...]


def add(left, right, *after):
    return pl.pallas_call(
        add_kernel,
        in_specs=[VMEM] * 2 + [pl.BlockSpec(memory_space=pl.ANY)] * len(after),
        out_specs=VMEM,
        out_shape=jax.ShapeDtypeStruct(left.shape, F32),
        compiler_params=params(16),
        cost_estimate=pl.CostEstimate(flops=1, bytes_accessed=1, transcendentals=0),
        name="add",
    )(left, right, *after)


def last_kernel(keep_ref, other_ref, top_keep_ref, top_other_ref, after_ref, group_ref, top_ref):
    size = group_ref.shape[2]
    group_ref[0] = size * (keep_ref[...] + other_ref[...])
    top_ref[...] = size * (top_keep_ref[...] + top_other_ref[...])


def last(keep, other, top_keep, top_other, after):
    return pl.pallas_call(
        last_kernel,
        in_specs=[VMEM] * 4 + [pl.BlockSpec(memory_space=pl.ANY)],
        out_specs=[VMEM] * 2,
        out_shape=[
            jax.ShapeDtypeStruct((1,) + keep.shape, F32),
            jax.ShapeDtypeStruct(top_keep.shape, F32),
        ],
        compiler_params=params(16),
        cost_estimate=pl.CostEstimate(flops=1, bytes_accessed=1, transcendentals=0),
        name="last",
    )(keep, other, top_keep, top_other, after)


def factor(matrices):
    size = matrices[0].shape[0]
    width = SUBLANES
    down = lax.broadcasted_iota(jnp.int32, (size, size), 0)
    across = lax.broadcasted_iota(jnp.int32, (size, size), 1)
    line = lax.broadcasted_iota(jnp.int32, (width, size), 0)
    lane = lax.broadcasted_iota(jnp.int32, (width, size), 1)
    states = list(matrices)
    diagonals = [[] for _ in matrices]
    for start in range(0, size, width):
        stop = start + width
        for m, state in enumerate(states):
            spread = [
                jnp.broadcast_to(state[:, start + q : start + q + 1], (size, size))
                for q in range(width)
            ]
            strip = state[start:stop, :]
            small = [s[start:stop, :] for s in spread]
            units, levels, scales = [], [], []
            rest = strip
            for q in range(width):
                scale = lax.rsqrt(small[q][q : q + 1, :])
                inverse = scale * scale
                level = rest[q : q + 1, :]
                rest = rest - (small[q] * level) * inverse
                unit = jnp.where(line == q, 1.0, small[q])
                for t in range(q + 1, width):
                    product = unit * small[t][q : q + 1, :]
                    small[t] = jnp.where(line == q, 0.0, small[t]) - product * inverse
                units.append(jnp.where(line <= q, unit, 0.0))
                levels.append(level * inverse)
                scales.append(scale)
            solved = units[0] * levels[0]
            for q in range(1, width):
                solved = solved + units[q] * levels[q]
            solved = jnp.where(lane >= stop, solved, 0.0)
            update = spread[0] * solved[0:1, :]
            for q in range(1, width):
                update = update + spread[q] * solved[q : q + 1, :]
            block = jnp.where(lane == line + start, 1.0, 0.0)
            kept = jnp.where(lane < start, strip, block) - solved
            parts = []
            if start > 0:
                parts.append(state[:start] - update[:start])
            parts.append(kept)
            if stop < size:
                parts.append(state[stop:] - update[stop:])
            states[m] = jnp.concatenate(parts, axis=0)
            diagonal = jnp.zeros((width, size), F32)
            for q in range(width):
                diagonal = jnp.where(lane == start + q, units[q] * scales[q], diagonal)
            diagonals[m].append(diagonal)
    uppers = [jnp.where(across >= down, state, 0.0) for state in states]
    return uppers, [jnp.concatenate(d, axis=0) for d in diagonals]


def finish_kernel(
    near_ref, far_ref, terms_ref, group_basis_ref, top_basis_ref, coupling_ref, group_ref, top_ref,
    token_ref,
):
    modes = near_ref.shape[1]
    down = lax.broadcasted_iota(jnp.int32, (modes, modes), 0)
    across = lax.broadcasted_iota(jnp.int32, (modes, modes), 1)
    near, far = near_ref[:modes, :], far_ref[:modes, :]
    group = jnp.where(down >= across, near, near.T)
    top = jnp.where(down > across, far.T, far)
    diagonal = jnp.broadcast_to(far_ref[modes : modes + 1, :], top.shape)
    top = jnp.where(down == across, diagonal, top)
    uppers, diagonals = factor([group, top])
    for half in range(2):
        inverse = split(three_pass(split(uppers[half]), split(diagonals[half])))
        basis = (group_basis_ref[0], top_basis_ref[...])[half]
        left = jnp.concatenate([terms_ref[half], basis], axis=0)
        result = three_pass(split(left), inverse)
        coupling_ref[0, :, half, :] = result[:modes]
        if half == 0:
            group_ref[0] = result[modes:]
        else:
            top_ref[...] = result[modes:]
            token_ref[...] = result[:SUBLANES]


def finish(near, far, terms, group_basis, top_basis):
    modes = near.shape[1]
    return pl.pallas_call(
        finish_kernel,
        in_specs=[VMEM] * 5,
        out_specs=[VMEM] * 4,
        out_shape=[
            jax.ShapeDtypeStruct((1, modes, 2, modes), F32),
            jax.ShapeDtypeStruct(group_basis.shape, F32),
            jax.ShapeDtypeStruct(top_basis.shape, F32),
            jax.ShapeDtypeStruct((SUBLANES, modes), F32),
        ],
        compiler_params=params(32),
        cost_estimate=pl.CostEstimate(
            flops=20 * modes**3, bytes_accessed=24 * modes * modes, transcendentals=2 * modes
        ),
        name="finish",
    )(near, far, terms, group_basis, top_basis)


def body(
    leaf_mass, tile_mask, constraint_modes, leaf_fixed_modes, block_map, group_mass, top_mass,
    group_basis, top_basis,
):
    row_count, col_count = lax.axis_size("row"), lax.axis_size("col")
    sizes = {"row": row_count, "col": col_count}

    def swap(value, axis, bit):
        return lax.ppermute(value, axis, crossed(sizes[axis], bit))

    def half_of(half, more, after):
        return leaf_half(half, tile_mask, block_map, leaf_mass, constraint_modes, more, after)

    group_steps = exchanges(0, row_count, col_count)
    basis = jnp.concatenate([group_basis[0], top_basis], axis=1)
    beside = swap(basis, "row", 1)
    keep, send, loaded = half_of(0, [], basis)
    pair = jnp.concatenate([basis, beside], axis=0)
    pieces = [pair] + [swap(pair, "row", 2 * k) for k in range(1, row_count // 2)]
    other = swap(send, *group_steps[0])
    top_keep, top_send, moved = half_of(1, [leaf_fixed_modes, loaded], pair)
    packed, terms, keep, top_keep, top_send = prepare(
        keep, send, top_keep, top_send, moved, group_mass, top_mass, other, pieces
    )
    top_left = exchanges(1, row_count, col_count)
    sums = [("row", 1 << b) for b in range(1, bits_of(row_count))] + [("row", 1)]
    row_steps = len(sums)
    sums += [("col", 1 << b) for b in range(bits_of(col_count))]
    value = near = packed
    top_other = swap(top_send, *top_left[0])
    after = []
    for i, step in enumerate(sums):
        value = add(value, swap(value, *step), *after)
        after = []
        if i == row_steps - 1:
            near = value
        if len(top_left) > 1:
            top_keep, top_send = fold(top_left[1], top_keep, top_other, value)
            top_left = top_left[1:]
            top_other = swap(top_send, *top_left[0])
            after.append(top_send)
        behind = i - (row_steps - 2)
        if behind == 0 or (behind >= 3 and len(group_steps) > 1):
            keep, send = fold(group_steps[1], keep, other, value)
            group_steps = group_steps[1:]
            other = swap(send, *group_steps[0])
            after.append(send)
    while len(group_steps) > 1:
        keep, send = fold(group_steps[1], keep, other, value)
        group_steps = group_steps[1:]
        other = swap(send, *group_steps[0])
    while len(top_left) > 1:
        top_keep, top_send = fold(top_left[1], top_keep, top_other, value)
        top_left = top_left[1:]
        top_other = swap(top_send, *top_left[0])
    coupling, group_modes, top_modes, token = finish(near, value, terms, group_basis, top_basis)
    assembled, top_assembled = last(keep, other, top_keep, top_other, token)
    return coupling, group_modes, top_modes, assembled, top_assembled


def solution(mesh):
    leaf = P(("row", "col"), None, None)
    group = P("col", "row", None)
    in_specs = (
        leaf, leaf, leaf, leaf, leaf, group, P(("row", "col"), None), group, P("row", None),
    )
    out_specs = (
        P(("row", "col"), None, None, None), group, P("row", None), group, P(("row", "col"), None),
    )
    return jax.shard_map(body, mesh=mesh, in_specs=in_specs, out_specs=out_specs, check_vma=False)
```

```python
import functools

import jax
import jax.numpy as jnp
from jax import lax
from jax.experimental import pallas as pl
from jax.experimental.pallas import tpu as pltpu
from jax.sharding import PartitionSpec as P

TILE = 128
SUBLANES = 8
F32 = jnp.float32
BF16 = jnp.bfloat16
VMEM = pl.BlockSpec(memory_space=pltpu.VMEM)
SMEM = pl.BlockSpec(memory_space=pltpu.SMEM)
HBM = pl.BlockSpec(memory_space=pltpu.HBM)
MASS_PARTS = 4


def params(megabytes):
    return pltpu.CompilerParams(vmem_limit_bytes=int(megabytes * 2**20))


def crossed(count, bit):
    return [(i, i ^ bit) for i in range(count)]


def rows_first(left, right):
    return lax.dot_general(left, right, (((0,), (0,)), ((), ())), preferred_element_type=F32)


def add_own(ref, own, place):
    share = own.shape[0]
    if share % SUBLANES == 0:
        window = pl.ds(pl.multiple_of(place * share, SUBLANES), share)
        ref[window, :] += own
        return
    fold = SUBLANES // share
    wide = jnp.concatenate([own] * fold, axis=0)
    line = lax.broadcasted_iota(jnp.int32, wide.shape, 0) // share
    window = pl.ds(pl.multiple_of(place // fold * SUBLANES, SUBLANES), SUBLANES)
    ref[window, :] += jnp.where(line == place % fold, wide, 0.0)


def copy_rows(target_ref, start, source_ref, place, share):
    if share % SUBLANES == 0:
        window = pl.ds(pl.multiple_of(place * share, SUBLANES), share)
        target_ref[start : start + share, :] = source_ref[window, :]
        return
    for i in range(share):
        target_ref[start + i : start + i + 1, :] = source_ref[pl.ds(place * share + i, 1), :]


def bits_of(count):
    return count.bit_length() - 1


def exchanges(half, row_count, col_count):
    row = [("row", 1)] + [("row", 1 << b) for b in range(bits_of(row_count) - 1, 0, -1)]
    col = [("col", 1 << b) for b in range(bits_of(col_count))]
    return row if half == 0 else col + row


def cut_order(half, row_count, col_count):
    steps = exchanges(half, row_count, col_count)
    order = [0]
    for axis, bit in reversed(steps):
        stride = 1 if half == 0 or axis == "col" else col_count
        order = order + [place + bit * stride for place in order]
    return order


def share_place(steps):
    place = 0
    for axis, bit in steps:
        place = 2 * place + lax.rem(lax.axis_index(axis) // bit, 2)
    return place


def cut_matrix(half, map_ref, partial_ref, whole_ref, keep_ref, send_ref):
    size = partial_ref.shape[0]
    blocks = size // TILE
    to = [pl.multiple_of(map_ref[0, half, a] * TILE, TILE) for a in range(blocks)]
    for b in range(blocks):
        for a in range(blocks):
            whole_ref[pl.ds(to[a], TILE), pl.ds(to[b], TILE)] = partial_ref[
                a * TILE : (a + 1) * TILE, b * TILE : (b + 1) * TILE
            ]
    order = cut_order(half, lax.axis_size("row"), lax.axis_size("col"))
    share = size // len(order)
    bit = lax.rem(lax.axis_index(("row", "col")[half]), 2)
    for k, chunk in enumerate((keep_ref, send_ref)):
        for i in range(len(order) // 2):
            step = order[i + len(order) // 2] - order[i]
            copy_rows(chunk, i * share, whole_ref, order[i] + step * lax.rem(bit + k, 2), share)


def group_kernel(
    mask_ref, map_ref, mass_hbm, modes_ref, after_ref, keep_ref, send_ref, loaded_ref, mass_ref,
    whole_ref, partial_ref, sems,
):
    rows, size = loaded_ref.shape
    tiles = rows // TILE
    height = rows // MASS_PARTS
    mass_copies = [
        pltpu.make_async_copy(
            mass_hbm.at[0, pl.ds(i * height, height)],
            mass_ref.at[pl.ds(i * height, height)],
            sems.at[i],
        )
        for i in range(MASS_PARTS)
    ]
    for copy in mass_copies:
        copy.start()
    for start, stop in ((0, 1), (1, MASS_PARTS)):
        for i in range(start, stop):
            mass_copies[i].wait()
        lines = []
        for a in range(start * height // TILE, stop * height // TILE):
            pieces = []
            for b in range(tiles):
                piece = mass_ref[a * TILE : (a + 1) * TILE, b * TILE : (b + 1) * TILE]
                pieces.append(jnp.where(mask_ref[0, a, b] != 0, piece, jnp.zeros_like(piece)))
            lines.append(jnp.concatenate(pieces, axis=1))
        masked = jnp.concatenate(lines, axis=0)
        window = slice(start * height, stop * height)
        mass_ref[window, :] = masked
        loaded = jnp.dot(masked, modes_ref[0, :, :size], preferred_element_type=F32).astype(BF16)
        loaded_ref[window, :] = loaded
        partial = rows_first(modes_ref[0, window, :size], loaded)
        if start == 0:
            partial_ref[...] = partial
        else:
            partial_ref[...] += partial
    cut_matrix(0, map_ref, partial_ref, whole_ref, keep_ref, send_ref)


def leaf_group(tile_mask, block_map, leaf_mass, constraint_modes, after):
    rows, size = constraint_modes.shape[1], constraint_modes.shape[2] // 2
    part = jax.ShapeDtypeStruct((size // 2, size), F32)
    half = jax.ShapeDtypeStruct((rows, size), BF16)
    return pl.pallas_call(
        group_kernel,
        in_specs=[SMEM] * 2 + [HBM, VMEM, pl.BlockSpec(memory_space=pl.ANY)],
        out_specs=[VMEM] * 4,
        out_shape=[part, part, half, jax.ShapeDtypeStruct((rows, rows), BF16)],
        scratch_shapes=[
            pltpu.VMEM((size, size), F32),
            pltpu.VMEM((size, size), F32),
            pltpu.SemaphoreType.DMA((MASS_PARTS,)),
        ],
        compiler_params=params(32),
        cost_estimate=pl.CostEstimate(
            flops=2 * rows * size * (rows + size),
            bytes_accessed=2 * rows * (rows + size) + 8 * size * size,
            transcendentals=0,
        ),
        name="leaf_group",
    )(tile_mask, block_map, leaf_mass, constraint_modes, after)


def top_kernel(
    map_ref, mass_ref, modes_ref, fixed_ref, first_ref, after_ref, keep_ref, send_ref, moved_ref,
    whole_ref, partial_ref, loaded_ref,
):
    rows, size = loaded_ref.shape
    height = rows // 2
    for i in range(2):
        window = slice(i * height, (i + 1) * height)
        loaded = jnp.dot(mass_ref[window, :], modes_ref[0, :, size:], preferred_element_type=F32)
        loaded = loaded.astype(BF16)
        loaded_ref[window, :] = loaded
        partial = rows_first(modes_ref[0, window, size:], loaded)
        if i == 0:
            partial_ref[...] = partial
        else:
            partial_ref[...] += partial
    for k, ref in enumerate((first_ref, loaded_ref)):
        projected = rows_first(fixed_ref[0], ref[...])
        for b in range(size // TILE):
            at = pl.multiple_of(map_ref[0, k, b] * TILE, TILE)
            moved_ref[k, :, pl.ds(at, TILE)] = projected[:, b * TILE : (b + 1) * TILE]
    cut_matrix(1, map_ref, partial_ref, whole_ref, keep_ref, send_ref)


def leaf_top(block_map, mass, modes, fixed, first, after):
    rows, size = modes.shape[1], modes.shape[2] // 2
    part = jax.ShapeDtypeStruct((size // 2, size), F32)
    return pl.pallas_call(
        top_kernel,
        in_specs=[SMEM] + [VMEM] * 4 + [pl.BlockSpec(memory_space=pl.ANY)],
        out_specs=[VMEM] * 3,
        out_shape=[part, part, jax.ShapeDtypeStruct((2, fixed.shape[2], size), F32)],
        scratch_shapes=[
            pltpu.VMEM((size, size), F32),
            pltpu.VMEM((size, size), F32),
            pltpu.VMEM((rows, size), BF16),
        ],
        compiler_params=params(32),
        cost_estimate=pl.CostEstimate(
            flops=2 * rows * size * (rows + size),
            bytes_accessed=2 * rows * (rows + size) + 8 * size * size,
            transcendentals=0,
        ),
        name="leaf_top",
    )(block_map, mass, modes, fixed, first, after)


def split(value):
    high = value.astype(BF16)
    return high, (value - high.astype(F32)).astype(BF16)


def three_pass(left, right, turn=False):
    (left_high, left_low), (right_high, right_low) = left, right
    multiply = rows_first if turn else functools.partial(jnp.dot, preferred_element_type=F32)
    width = right_high.shape[1]
    both = multiply(left_high, jnp.concatenate([right_high, right_low], axis=1))
    return both[:, :width] + both[:, width:] + multiply(left_low, right_high)


def halve(step, keep_ref, other_ref, next_ref, send_ref):
    axis, bit = step
    height = next_ref.shape[0]
    mine = lax.rem(lax.axis_index(axis) // bit, 2) == 1
    low = keep_ref[:height, :] + other_ref[:height, :]
    high = keep_ref[height:, :] + other_ref[height:, :]
    next_ref[...] = jnp.where(mine, high, low)
    send_ref[...] = jnp.where(mine, low, high)


def prepare_kernel(
    count, keep_in, send_ref, top_keep_in, top_send_ref, moved_ref, group_own_ref,
    top_own_ref, *refs,
):
    pieces = refs[1 : count + 1]
    (
        packed_ref, terms_ref, keep_ref, top_keep_ref, top_next_ref, bases_ref
    ) = refs[count + 1 :]
    modes = terms_ref.shape[2]
    size = bases_ref.shape[0]
    row, col = lax.axis_index("row"), lax.axis_index("col")
    row_count, col_count = lax.axis_size("row"), lax.axis_size("col")
    group_steps = exchanges(0, row_count, col_count)
    top_steps = exchanges(1, row_count, col_count)
    keep_ref[...] = keep_in[...]
    add_own(keep_ref, group_own_ref[0], share_place(group_steps[1:]))
    top_keep_ref[...] = top_keep_in[...]
    add_own(top_keep_ref, top_own_ref[...], share_place(top_steps[1:]))
    top_next_ref[...] = top_send_ref[...]
    line = size // row_count
    for k, piece in enumerate(pieces):
        pair = lax.bitwise_xor(row // 2, k)
        for i in range(2):
            at = (2 * pair + lax.rem(row + i, 2)) * line
            bases_ref[pl.ds(pl.multiple_of(at, line), line), :] = piece[i * line : (i + 1) * line, :]
    grams = []
    for half in range(2):
        lanes = slice(half * modes, (half + 1) * modes)
        basis = split(bases_ref[:, lanes])
        order = cut_order(half, row_count, col_count)
        share = size // len(order)
        lower = jnp.concatenate(
            [bases_ref[at * share : (at + 1) * share, lanes] for at in order[: len(order) // 2]], axis=0
        )
        upper = jnp.concatenate(
            [bases_ref[at * share : (at + 1) * share, lanes] for at in order[len(order) // 2 :]], axis=0
        )
        swap = lax.rem((row, col)[half], 2) == 1
        ordered = jnp.concatenate(
            [jnp.where(swap, upper, lower), jnp.where(swap, lower, upper)], axis=0
        )
        parts = ((keep_ref, send_ref), (top_keep_ref, top_send_ref))[half]
        matrix = jnp.concatenate([part[...] for part in parts], axis=0)
        applied = three_pass(split(matrix), basis)
        gram = three_pass(split(ordered), split(applied), turn=True)
        grams.append(0.5 * (gram + gram.T))
        terms_ref[half] = three_pass(split(moved_ref[half]), basis)
    down = lax.broadcasted_iota(jnp.int32, (modes, modes), 0)
    across = lax.broadcasted_iota(jnp.int32, (modes, modes), 1)
    packed_ref[:modes, :] = jnp.where(down >= across, grams[0], grams[1])
    diagonal = jnp.sum(jnp.where(down == across, grams[1], 0.0), axis=0, keepdims=True)
    packed_ref[modes:, :] = jnp.broadcast_to(diagonal, (SUBLANES, modes))


def prepare(keep, send, top_keep, top_send, moved, group_own, top_own, after, pieces):
    _, modes, size = moved.shape
    half = jax.ShapeDtypeStruct(keep.shape, F32)
    return pl.pallas_call(
        functools.partial(prepare_kernel, len(pieces)),
        in_specs=[VMEM] * 7 + [pl.BlockSpec(memory_space=pl.ANY)] + [VMEM] * len(pieces),
        out_specs=[VMEM] * 5,
        out_shape=[
            jax.ShapeDtypeStruct((modes + SUBLANES, modes), F32),
            jax.ShapeDtypeStruct((2, modes, modes), F32),
            half,
            half,
            half,
        ],
        scratch_shapes=[pltpu.VMEM((size, 2 * modes), F32)],
        compiler_params=params(32),
        cost_estimate=pl.CostEstimate(
            flops=12 * size * size * modes, bytes_accessed=12 * size * size, transcendentals=0
        ),
        name="prepare",
    )(keep, send, top_keep, top_send, moved, group_own, top_own, after, *pieces)


def fold_kernel(step, after_count, keep_ref, other_ref, *refs):
    halve(step, keep_ref, other_ref, *refs[after_count:])


def fold(step, keep, other, *after):
    part = jax.ShapeDtypeStruct((keep.shape[0] // 2, keep.shape[1]), F32)
    return pl.pallas_call(
        functools.partial(fold_kernel, step, len(after)),
        in_specs=[VMEM] * 2 + [pl.BlockSpec(memory_space=pl.ANY)] * len(after),
        out_specs=[VMEM] * 2,
        out_shape=[part, part],
        compiler_params=params(16),
        cost_estimate=pl.CostEstimate(flops=1, bytes_accessed=1, transcendentals=0),
        name="fold",
    )(keep, other, *after)


def add_kernel(left_ref, right_ref, *refs):
    refs[-1][...] = left_ref[...] + right_ref[...]


def add(left, right, *after):
    return pl.pallas_call(
        add_kernel,
        in_specs=[VMEM] * 2 + [pl.BlockSpec(memory_space=pl.ANY)] * len(after),
        out_specs=VMEM,
        out_shape=jax.ShapeDtypeStruct(left.shape, F32),
        compiler_params=params(16),
        cost_estimate=pl.CostEstimate(flops=1, bytes_accessed=1, transcendentals=0),
        name="add",
    )(left, right, *after)


def last_kernel(keep_ref, other_ref, top_keep_ref, top_other_ref, after_ref, group_ref, top_ref):
    size = group_ref.shape[2]
    group_ref[0] = size * (keep_ref[...] + other_ref[...])
    top_ref[...] = size * (top_keep_ref[...] + top_other_ref[...])


def last(keep, other, top_keep, top_other, after):
    return pl.pallas_call(
        last_kernel,
        in_specs=[VMEM] * 4 + [pl.BlockSpec(memory_space=pl.ANY)],
        out_specs=[VMEM] * 2,
        out_shape=[
            jax.ShapeDtypeStruct((1,) + keep.shape, F32),
            jax.ShapeDtypeStruct(top_keep.shape, F32),
        ],
        compiler_params=params(16),
        cost_estimate=pl.CostEstimate(flops=1, bytes_accessed=1, transcendentals=0),
        name="last",
    )(keep, other, top_keep, top_other, after)


def factor(matrices):
    size = matrices[0].shape[0]
    width = SUBLANES
    down = lax.broadcasted_iota(jnp.int32, (size, size), 0)
    across = lax.broadcasted_iota(jnp.int32, (size, size), 1)
    line = lax.broadcasted_iota(jnp.int32, (width, size), 0)
    lane = lax.broadcasted_iota(jnp.int32, (width, size), 1)
    states = list(matrices)
    diagonals = [[] for _ in matrices]
    for start in range(0, size, width):
        stop = start + width
        for m, state in enumerate(states):
            spread = [
                jnp.broadcast_to(state[:, start + q : start + q + 1], (size, size))
                for q in range(width)
            ]
            strip = state[start:stop, :]
            small = [s[start:stop, :] for s in spread]
            scaled = []
            rest = strip
            for q in range(width):
                scale = lax.rsqrt(small[q][q : q + 1, :])
                tail = [small[t][q : q + 1, :] * scale for t in range(q + 1, width)]
                level = rest[q : q + 1, :] * scale
                rest = rest - small[q] * (scale * level)
                small[q] = jnp.where(line == q, 1.0, small[q]) * scale
                for t in range(q + 1, width):
                    small[t] = jnp.where(line == q, 0.0, small[t]) - small[q] * tail[t - q - 1]
                scaled.append(level)
            small = [jnp.where(line <= q, s, 0.0) for q, s in enumerate(small)]
            solved = small[0] * scaled[0]
            for q in range(1, width):
                solved = solved + small[q] * scaled[q]
            solved = jnp.where(lane >= stop, solved, 0.0)
            update = spread[0] * solved[0:1, :]
            for q in range(1, width):
                update = update + spread[q] * solved[q : q + 1, :]
            block = jnp.where(lane == line + start, 1.0, 0.0)
            kept = jnp.where(lane < start, strip, block) - solved
            parts = []
            if start > 0:
                parts.append(state[:start] - update[:start])
            parts.append(kept)
            if stop < size:
                parts.append(state[stop:] - update[stop:])
            states[m] = jnp.concatenate(parts, axis=0)
            diagonal = jnp.zeros((width, size), F32)
            for q in range(width):
                diagonal = jnp.where(lane == start + q, small[q], diagonal)
            diagonals[m].append(diagonal)
    uppers = [jnp.where(across >= down, state, 0.0) for state in states]
    return uppers, [jnp.concatenate(d, axis=0) for d in diagonals]


def finish_kernel(
    near_ref, far_ref, terms_ref, group_basis_ref, top_basis_ref, coupling_ref, group_ref, top_ref,
    token_ref,
):
    modes = near_ref.shape[1]
    down = lax.broadcasted_iota(jnp.int32, (modes, modes), 0)
    across = lax.broadcasted_iota(jnp.int32, (modes, modes), 1)
    near, far = near_ref[:modes, :], far_ref[:modes, :]
    group = jnp.where(down >= across, near, near.T)
    top = jnp.where(down > across, far.T, far)
    diagonal = jnp.broadcast_to(far_ref[modes : modes + 1, :], top.shape)
    top = jnp.where(down == across, diagonal, top)
    uppers, diagonals = factor([group, top])
    for half in range(2):
        inverse = split(three_pass(split(uppers[half]), split(diagonals[half])))
        basis = (group_basis_ref[0], top_basis_ref[...])[half]
        left = jnp.concatenate([terms_ref[half], basis], axis=0)
        result = three_pass(split(left), inverse)
        coupling_ref[0, :, half, :] = result[:modes]
        if half == 0:
            group_ref[0] = result[modes:]
        else:
            top_ref[...] = result[modes:]
            token_ref[...] = result[:SUBLANES]


def finish(near, far, terms, group_basis, top_basis):
    modes = near.shape[1]
    return pl.pallas_call(
        finish_kernel,
        in_specs=[VMEM] * 5,
        out_specs=[VMEM] * 4,
        out_shape=[
            jax.ShapeDtypeStruct((1, modes, 2, modes), F32),
            jax.ShapeDtypeStruct(group_basis.shape, F32),
            jax.ShapeDtypeStruct(top_basis.shape, F32),
            jax.ShapeDtypeStruct((SUBLANES, modes), F32),
        ],
        compiler_params=params(32),
        cost_estimate=pl.CostEstimate(
            flops=20 * modes**3, bytes_accessed=24 * modes * modes, transcendentals=2 * modes
        ),
        name="finish",
    )(near, far, terms, group_basis, top_basis)


def body(
    leaf_mass, tile_mask, constraint_modes, leaf_fixed_modes, block_map, group_mass, top_mass,
    group_basis, top_basis,
):
    row_count, col_count = lax.axis_size("row"), lax.axis_size("col")
    sizes = {"row": row_count, "col": col_count}

    def swap(value, axis, bit):
        return lax.ppermute(value, axis, crossed(sizes[axis], bit))

    group_steps = exchanges(0, row_count, col_count)
    basis = jnp.concatenate([group_basis[0], top_basis], axis=1)
    beside = swap(basis, "row", 1)
    keep, send, loaded, mass = leaf_group(
        tile_mask, block_map, leaf_mass, constraint_modes, basis
    )
    pair = jnp.concatenate([basis, beside], axis=0)
    pieces = [pair] + [swap(pair, "row", 2 * k) for k in range(1, row_count // 2)]
    other = swap(send, *group_steps[0])
    top_keep, top_send, moved = leaf_top(
        block_map, mass, constraint_modes, leaf_fixed_modes, loaded, pair
    )
    packed, terms, keep, top_keep, top_send = prepare(
        keep, send, top_keep, top_send, moved, group_mass, top_mass, other, pieces
    )
    top_left = exchanges(1, row_count, col_count)
    sums = [("row", 1 << b) for b in range(1, bits_of(row_count))] + [("row", 1)]
    row_steps = len(sums)
    sums += [("col", 1 << b) for b in range(bits_of(col_count))]
    value = near = packed
    top_other = swap(top_send, *top_left[0])
    after = []
    for i, step in enumerate(sums):
        value = add(value, swap(value, *step), *after)
        after = []
        if i == row_steps - 1:
            near = value
        if len(top_left) > 1:
            top_keep, top_send = fold(top_left[1], top_keep, top_other, value)
            top_left = top_left[1:]
            top_other = swap(top_send, *top_left[0])
            after.append(top_send)
        behind = i - (row_steps - 2)
        if behind == 0 or (behind >= 3 and len(group_steps) > 1):
            keep, send = fold(group_steps[1], keep, other, value)
            group_steps = group_steps[1:]
            other = swap(send, *group_steps[0])
            after.append(send)
    while len(group_steps) > 1:
        keep, send = fold(group_steps[1], keep, other, value)
        group_steps = group_steps[1:]
        other = swap(send, *group_steps[0])
    while len(top_left) > 1:
        top_keep, top_send = fold(top_left[1], top_keep, top_other, value)
        top_left = top_left[1:]
        top_other = swap(top_send, *top_left[0])
    coupling, group_modes, top_modes, token = finish(near, value, terms, group_basis, top_basis)
    assembled, top_assembled = last(keep, other, top_keep, top_other, token)
    return coupling, group_modes, top_modes, assembled, top_assembled


def solution(mesh):
    leaf = P(("row", "col"), None, None)
    group = P("col", "row", None)
    in_specs = (
        leaf, leaf, leaf, leaf, leaf, group, P(("row", "col"), None), group, P("row", None),
    )
    out_specs = (
        P(("row", "col"), None, None, None), group, P("row", None), group, P(("row", "col"), None),
    )
    return jax.shard_map(body, mesh=mesh, in_specs=in_specs, out_specs=out_specs, check_vma=False)
```

```python
import functools

import jax
import jax.numpy as jnp
from jax import lax
from jax.experimental import pallas as pl
from jax.experimental.pallas import tpu as pltpu
from jax.sharding import PartitionSpec as P

TILE = 128
SUBLANES = 8
F32 = jnp.float32
BF16 = jnp.bfloat16
VMEM = pl.BlockSpec(memory_space=pltpu.VMEM)
SMEM = pl.BlockSpec(memory_space=pltpu.SMEM)
HBM = pl.BlockSpec(memory_space=pltpu.HBM)
MASS_PARTS = 4


def params(megabytes):
    return pltpu.CompilerParams(vmem_limit_bytes=int(megabytes * 2**20))


def crossed(count, bit):
    return [(i, i ^ bit) for i in range(count)]


def rows_first(left, right):
    return lax.dot_general(left, right, (((0,), (0,)), ((), ())), preferred_element_type=F32)


def add_own(ref, own, place):
    share = own.shape[0]
    if share % SUBLANES == 0:
        window = pl.ds(pl.multiple_of(place * share, SUBLANES), share)
        ref[window, :] += own
        return
    fold = SUBLANES // share
    wide = jnp.concatenate([own] * fold, axis=0)
    line = lax.broadcasted_iota(jnp.int32, wide.shape, 0) // share
    window = pl.ds(pl.multiple_of(place // fold * SUBLANES, SUBLANES), SUBLANES)
    ref[window, :] += jnp.where(line == place % fold, wide, 0.0)


def copy_rows(target_ref, start, source_ref, place, share):
    if share % SUBLANES == 0:
        window = pl.ds(pl.multiple_of(place * share, SUBLANES), share)
        target_ref[start : start + share, :] = source_ref[window, :]
        return
    for i in range(share):
        target_ref[start + i : start + i + 1, :] = source_ref[pl.ds(place * share + i, 1), :]


def bits_of(count):
    return count.bit_length() - 1


def exchanges(half, row_count, col_count):
    row = [("row", 1)] + [("row", 1 << b) for b in range(bits_of(row_count) - 1, 0, -1)]
    col = [("col", 1 << b) for b in range(bits_of(col_count))]
    return row if half == 0 else col + row


def cut_order(half, row_count, col_count):
    steps = exchanges(half, row_count, col_count)
    order = [0]
    for axis, bit in reversed(steps):
        stride = 1 if half == 0 or axis == "col" else col_count
        order = order + [place + bit * stride for place in order]
    return order


def share_place(steps):
    place = 0
    for axis, bit in steps:
        place = 2 * place + lax.rem(lax.axis_index(axis) // bit, 2)
    return place


def cut_matrix(half, map_ref, partial_ref, whole_ref, keep_ref, send_ref):
    size = partial_ref.shape[0]
    blocks = size // TILE
    to = [pl.multiple_of(map_ref[0, half, a] * TILE, TILE) for a in range(blocks)]
    for b in range(blocks):
        for a in range(blocks):
            whole_ref[pl.ds(to[a], TILE), pl.ds(to[b], TILE)] = partial_ref[
                a * TILE : (a + 1) * TILE, b * TILE : (b + 1) * TILE
            ]
    order = cut_order(half, lax.axis_size("row"), lax.axis_size("col"))
    share = size // len(order)
    bit = lax.rem(lax.axis_index(("row", "col")[half]), 2)
    for k, chunk in enumerate((keep_ref, send_ref)):
        for i in range(len(order) // 2):
            step = order[i + len(order) // 2] - order[i]
            copy_rows(chunk, i * share, whole_ref, order[i] + step * lax.rem(bit + k, 2), share)


def group_kernel(
    mask_ref, map_ref, mass_hbm, modes_ref, after_ref, keep_ref, send_ref, loaded_ref, mass_ref,
    whole_ref, partial_ref, sems,
):
    rows, size = loaded_ref.shape
    tiles = rows // TILE
    height = rows // MASS_PARTS
    mass_copies = [
        pltpu.make_async_copy(
            mass_hbm.at[0, pl.ds(i * height, height)],
            mass_ref.at[pl.ds(i * height, height)],
            sems.at[i],
        )
        for i in range(MASS_PARTS)
    ]
    for copy in mass_copies:
        copy.start()
    for start, stop in ((0, 1), (1, MASS_PARTS)):
        for i in range(start, stop):
            mass_copies[i].wait()
        lines = []
        for a in range(start * height // TILE, stop * height // TILE):
            pieces = []
            for b in range(tiles):
                piece = mass_ref[a * TILE : (a + 1) * TILE, b * TILE : (b + 1) * TILE]
                pieces.append(jnp.where(mask_ref[0, a, b] != 0, piece, jnp.zeros_like(piece)))
            lines.append(jnp.concatenate(pieces, axis=1))
        masked = jnp.concatenate(lines, axis=0)
        window = slice(start * height, stop * height)
        mass_ref[window, :] = masked
        loaded = jnp.dot(masked, modes_ref[0, :, :size], preferred_element_type=F32).astype(BF16)
        loaded_ref[window, :] = loaded
        partial = rows_first(modes_ref[0, window, :size], loaded)
        if start == 0:
            partial_ref[...] = partial
        else:
            partial_ref[...] += partial
    cut_matrix(0, map_ref, partial_ref, whole_ref, keep_ref, send_ref)


def leaf_group(tile_mask, block_map, leaf_mass, constraint_modes, after):
    rows, size = constraint_modes.shape[1], constraint_modes.shape[2] // 2
    part = jax.ShapeDtypeStruct((size // 2, size), F32)
    half = jax.ShapeDtypeStruct((rows, size), BF16)
    return pl.pallas_call(
        group_kernel,
        in_specs=[SMEM] * 2 + [HBM, VMEM, pl.BlockSpec(memory_space=pl.ANY)],
        out_specs=[VMEM] * 4,
        out_shape=[part, part, half, jax.ShapeDtypeStruct((rows, rows), BF16)],
        scratch_shapes=[
            pltpu.VMEM((size, size), F32),
            pltpu.VMEM((size, size), F32),
            pltpu.SemaphoreType.DMA((MASS_PARTS,)),
        ],
        compiler_params=params(32),
        cost_estimate=pl.CostEstimate(
            flops=2 * rows * size * (rows + size),
            bytes_accessed=2 * rows * (rows + size) + 8 * size * size,
            transcendentals=0,
        ),
        name="leaf_group",
    )(tile_mask, block_map, leaf_mass, constraint_modes, after)


def top_kernel(
    map_ref, mass_ref, modes_ref, fixed_ref, first_ref, after_ref, keep_ref, send_ref, moved_ref,
    whole_ref, partial_ref, loaded_ref,
):
    rows, size = loaded_ref.shape
    height = rows // 2
    for i in range(2):
        window = slice(i * height, (i + 1) * height)
        loaded = jnp.dot(mass_ref[window, :], modes_ref[0, :, size:], preferred_element_type=F32)
        loaded = loaded.astype(BF16)
        loaded_ref[window, :] = loaded
        partial = rows_first(modes_ref[0, window, size:], loaded)
        if i == 0:
            partial_ref[...] = partial
        else:
            partial_ref[...] += partial
    for k, ref in enumerate((first_ref, loaded_ref)):
        projected = rows_first(fixed_ref[0], ref[...])
        for b in range(size // TILE):
            at = pl.multiple_of(map_ref[0, k, b] * TILE, TILE)
            moved_ref[k, :, pl.ds(at, TILE)] = projected[:, b * TILE : (b + 1) * TILE]
    cut_matrix(1, map_ref, partial_ref, whole_ref, keep_ref, send_ref)


def leaf_top(block_map, mass, modes, fixed, first, after):
    rows, size = modes.shape[1], modes.shape[2] // 2
    part = jax.ShapeDtypeStruct((size // 2, size), F32)
    return pl.pallas_call(
        top_kernel,
        in_specs=[SMEM] + [VMEM] * 4 + [pl.BlockSpec(memory_space=pl.ANY)],
        out_specs=[VMEM] * 3,
        out_shape=[part, part, jax.ShapeDtypeStruct((2, fixed.shape[2], size), F32)],
        scratch_shapes=[
            pltpu.VMEM((size, size), F32),
            pltpu.VMEM((size, size), F32),
            pltpu.VMEM((rows, size), BF16),
        ],
        compiler_params=params(32),
        cost_estimate=pl.CostEstimate(
            flops=2 * rows * size * (rows + size),
            bytes_accessed=2 * rows * (rows + size) + 8 * size * size,
            transcendentals=0,
        ),
        name="leaf_top",
    )(block_map, mass, modes, fixed, first, after)


def split(value):
    high = value.astype(BF16)
    return high, (value - high.astype(F32)).astype(BF16)


def three_pass(left, right, turn=False):
    (left_high, left_low), (right_high, right_low) = left, right
    multiply = rows_first if turn else functools.partial(jnp.dot, preferred_element_type=F32)
    width = right_high.shape[1]
    both = multiply(left_high, jnp.concatenate([right_high, right_low], axis=1))
    return both[:, :width] + both[:, width:] + multiply(left_low, right_high)


def halve(step, keep_ref, other_ref, next_ref, send_ref):
    axis, bit = step
    height = next_ref.shape[0]
    mine = lax.rem(lax.axis_index(axis) // bit, 2) == 1
    low = keep_ref[:height, :] + other_ref[:height, :]
    high = keep_ref[height:, :] + other_ref[height:, :]
    next_ref[...] = jnp.where(mine, high, low)
    send_ref[...] = jnp.where(mine, low, high)


def prepare_kernel(
    count, keep_in, send_ref, top_keep_in, top_send_ref, moved_ref, group_own_ref,
    top_own_ref, *refs,
):
    pieces = refs[:count]
    (
        packed_ref, terms_ref, keep_ref, next_ref, top_keep_ref, top_next_ref, bases_ref
    ) = refs[count:]
    modes = terms_ref.shape[2]
    size = bases_ref.shape[0]
    row, col = lax.axis_index("row"), lax.axis_index("col")
    row_count, col_count = lax.axis_size("row"), lax.axis_size("col")
    group_steps = exchanges(0, row_count, col_count)
    top_steps = exchanges(1, row_count, col_count)
    keep_ref[...] = keep_in[...]
    add_own(keep_ref, group_own_ref[0], share_place(group_steps[1:]))
    top_keep_ref[...] = top_keep_in[...]
    add_own(top_keep_ref, top_own_ref[...], share_place(top_steps[1:]))
    next_ref[...] = send_ref[...]
    top_next_ref[...] = top_send_ref[...]
    line = size // row_count
    for i, piece in enumerate(pieces):
        for k in range(row_count // 2):
            at = (2 * lax.bitwise_xor(row // 2, k) + lax.rem(row + i, 2)) * line
            bases_ref[pl.ds(pl.multiple_of(at, line), line), :] = piece[k * line : (k + 1) * line, :]
    grams = []
    for half in range(2):
        lanes = slice(half * modes, (half + 1) * modes)
        basis = split(bases_ref[:, lanes])
        order = cut_order(half, row_count, col_count)
        share = size // len(order)
        lower = jnp.concatenate(
            [bases_ref[at * share : (at + 1) * share, lanes] for at in order[: len(order) // 2]], axis=0
        )
        upper = jnp.concatenate(
            [bases_ref[at * share : (at + 1) * share, lanes] for at in order[len(order) // 2 :]], axis=0
        )
        swap = lax.rem((row, col)[half], 2) == 1
        ordered = jnp.concatenate(
            [jnp.where(swap, upper, lower), jnp.where(swap, lower, upper)], axis=0
        )
        parts = ((keep_ref, send_ref), (top_keep_ref, top_send_ref))[half]
        matrix = jnp.concatenate([part[...] for part in parts], axis=0)
        applied = three_pass(split(matrix), basis)
        gram = three_pass(split(ordered), split(applied), turn=True)
        grams.append(0.5 * (gram + gram.T))
        terms_ref[half] = three_pass(split(moved_ref[half]), basis)
    down = lax.broadcasted_iota(jnp.int32, (modes, modes), 0)
    across = lax.broadcasted_iota(jnp.int32, (modes, modes), 1)
    packed_ref[:modes, :] = jnp.where(down >= across, grams[0], grams[1])
    diagonal = jnp.sum(jnp.where(down == across, grams[1], 0.0), axis=0, keepdims=True)
    packed_ref[modes:, :] = jnp.broadcast_to(diagonal, (SUBLANES, modes))


def prepare(keep, send, top_keep, top_send, moved, group_own, top_own, pieces):
    _, modes, size = moved.shape
    half = jax.ShapeDtypeStruct(keep.shape, F32)
    return pl.pallas_call(
        functools.partial(prepare_kernel, len(pieces)),
        in_specs=[VMEM] * (7 + len(pieces)),
        out_specs=[VMEM] * 6,
        out_shape=[
            jax.ShapeDtypeStruct((modes + SUBLANES, modes), F32),
            jax.ShapeDtypeStruct((2, modes, modes), F32),
            half,
            half,
            half,
            half,
        ],
        scratch_shapes=[pltpu.VMEM((size, 2 * modes), F32)],
        compiler_params=params(32),
        cost_estimate=pl.CostEstimate(
            flops=12 * size * size * modes, bytes_accessed=12 * size * size, transcendentals=0
        ),
        name="prepare",
    )(keep, send, top_keep, top_send, moved, group_own, top_own, *pieces)


def fold_kernel(step, after_count, keep_ref, other_ref, *refs):
    halve(step, keep_ref, other_ref, *refs[after_count:])


def fold(step, keep, other, *after):
    part = jax.ShapeDtypeStruct((keep.shape[0] // 2, keep.shape[1]), F32)
    return pl.pallas_call(
        functools.partial(fold_kernel, step, len(after)),
        in_specs=[VMEM] * 2 + [pl.BlockSpec(memory_space=pl.ANY)] * len(after),
        out_specs=[VMEM] * 2,
        out_shape=[part, part],
        compiler_params=params(16),
        cost_estimate=pl.CostEstimate(flops=1, bytes_accessed=1, transcendentals=0),
        name="fold",
    )(keep, other, *after)


def add_kernel(left_ref, right_ref, *refs):
    refs[-1][...] = left_ref[...] + right_ref[...]


def add(left, right, *after):
    return pl.pallas_call(
        add_kernel,
        in_specs=[VMEM] * 2 + [pl.BlockSpec(memory_space=pl.ANY)] * len(after),
        out_specs=VMEM,
        out_shape=jax.ShapeDtypeStruct(left.shape, F32),
        compiler_params=params(16),
        cost_estimate=pl.CostEstimate(flops=1, bytes_accessed=1, transcendentals=0),
        name="add",
    )(left, right, *after)


def last_kernel(keep_ref, other_ref, top_keep_ref, top_other_ref, after_ref, group_ref, top_ref):
    size = group_ref.shape[2]
    group_ref[0] = size * (keep_ref[...] + other_ref[...])
    top_ref[...] = size * (top_keep_ref[...] + top_other_ref[...])


def last(keep, other, top_keep, top_other, after):
    return pl.pallas_call(
        last_kernel,
        in_specs=[VMEM] * 4 + [pl.BlockSpec(memory_space=pl.ANY)],
        out_specs=[VMEM] * 2,
        out_shape=[
            jax.ShapeDtypeStruct((1,) + keep.shape, F32),
            jax.ShapeDtypeStruct(top_keep.shape, F32),
        ],
        compiler_params=params(16),
        cost_estimate=pl.CostEstimate(flops=1, bytes_accessed=1, transcendentals=0),
        name="last",
    )(keep, other, top_keep, top_other, after)


def factor(matrices):
    size = matrices[0].shape[0]
    width = SUBLANES
    down = lax.broadcasted_iota(jnp.int32, (size, size), 0)
    across = lax.broadcasted_iota(jnp.int32, (size, size), 1)
    line = lax.broadcasted_iota(jnp.int32, (width, size), 0)
    lane = lax.broadcasted_iota(jnp.int32, (width, size), 1)
    states = list(matrices)
    diagonals = [[] for _ in matrices]
    for start in range(0, size, width):
        stop = start + width
        for m, state in enumerate(states):
            spread = [
                jnp.broadcast_to(state[:, start + q : start + q + 1], (size, size))
                for q in range(width)
            ]
            strip = state[start:stop, :]
            small = [s[start:stop, :] for s in spread]
            scaled = []
            rest = strip
            for q in range(width):
                scale = lax.rsqrt(small[q][q : q + 1, :])
                tail = [small[t][q : q + 1, :] * scale for t in range(q + 1, width)]
                level = rest[q : q + 1, :] * scale
                rest = rest - small[q] * (scale * level)
                small[q] = jnp.where(line == q, 1.0, small[q]) * scale
                for t in range(q + 1, width):
                    small[t] = jnp.where(line == q, 0.0, small[t]) - small[q] * tail[t - q - 1]
                scaled.append(level)
            small = [jnp.where(line <= q, s, 0.0) for q, s in enumerate(small)]
            solved = small[0] * scaled[0]
            for q in range(1, width):
                solved = solved + small[q] * scaled[q]
            solved = jnp.where(lane >= stop, solved, 0.0)
            update = spread[0] * solved[0:1, :]
            for q in range(1, width):
                update = update + spread[q] * solved[q : q + 1, :]
            block = jnp.where(lane == line + start, 1.0, 0.0)
            kept = jnp.where(lane < start, strip, block) - solved
            parts = []
            if start > 0:
                parts.append(state[:start] - update[:start])
            parts.append(kept)
            if stop < size:
                parts.append(state[stop:] - update[stop:])
            states[m] = jnp.concatenate(parts, axis=0)
            diagonal = jnp.zeros((width, size), F32)
            for q in range(width):
                diagonal = jnp.where(lane == start + q, small[q], diagonal)
            diagonals[m].append(diagonal)
    uppers = [jnp.where(across >= down, state, 0.0) for state in states]
    return uppers, [jnp.concatenate(d, axis=0) for d in diagonals]


def finish_kernel(
    near_ref, far_ref, terms_ref, group_basis_ref, top_basis_ref, coupling_ref, group_ref, top_ref,
    token_ref,
):
    modes = near_ref.shape[1]
    down = lax.broadcasted_iota(jnp.int32, (modes, modes), 0)
    across = lax.broadcasted_iota(jnp.int32, (modes, modes), 1)
    near, far = near_ref[:modes, :], far_ref[:modes, :]
    group = jnp.where(down >= across, near, near.T)
    top = jnp.where(down > across, far.T, far)
    diagonal = jnp.broadcast_to(far_ref[modes : modes + 1, :], top.shape)
    top = jnp.where(down == across, diagonal, top)
    uppers, diagonals = factor([group, top])
    for half in range(2):
        inverse = split(three_pass(split(uppers[half]), split(diagonals[half])))
        basis = (group_basis_ref[0], top_basis_ref[...])[half]
        left = jnp.concatenate([terms_ref[half], basis], axis=0)
        result = three_pass(split(left), inverse)
        coupling_ref[0, :, half, :] = result[:modes]
        if half == 0:
            group_ref[0] = result[modes:]
        else:
            top_ref[...] = result[modes:]
            token_ref[...] = result[:SUBLANES]


def finish(near, far, terms, group_basis, top_basis):
    modes = near.shape[1]
    return pl.pallas_call(
        finish_kernel,
        in_specs=[VMEM] * 5,
        out_specs=[VMEM] * 4,
        out_shape=[
            jax.ShapeDtypeStruct((1, modes, 2, modes), F32),
            jax.ShapeDtypeStruct(group_basis.shape, F32),
            jax.ShapeDtypeStruct(top_basis.shape, F32),
            jax.ShapeDtypeStruct((SUBLANES, modes), F32),
        ],
        compiler_params=params(32),
        cost_estimate=pl.CostEstimate(
            flops=20 * modes**3, bytes_accessed=24 * modes * modes, transcendentals=2 * modes
        ),
        name="finish",
    )(near, far, terms, group_basis, top_basis)


def body(
    leaf_mass, tile_mask, constraint_modes, leaf_fixed_modes, block_map, group_mass, top_mass,
    group_basis, top_basis,
):
    row_count, col_count = lax.axis_size("row"), lax.axis_size("col")
    sizes = {"row": row_count, "col": col_count}

    def swap(value, axis, bit):
        return lax.ppermute(value, axis, crossed(sizes[axis], bit))

    group_steps = exchanges(0, row_count, col_count)
    basis = jnp.concatenate([group_basis[0], top_basis], axis=1)
    lines = [basis] + [swap(basis, "row", 2 * k) for k in range(1, row_count // 2)]
    keep, send, loaded, mass = leaf_group(
        tile_mask, block_map, leaf_mass, constraint_modes, basis
    )
    near_lines = jnp.concatenate(lines, axis=0)
    pieces = [near_lines, swap(near_lines, "row", 1)]
    top_keep, top_send, moved = leaf_top(
        block_map, mass, constraint_modes, leaf_fixed_modes, loaded, near_lines
    )
    packed, terms, keep, send, top_keep, top_send = prepare(
        keep, send, top_keep, top_send, moved, group_mass, top_mass, pieces
    )
    top_left = exchanges(1, row_count, col_count)
    sums = [("row", 1 << b) for b in range(1, bits_of(row_count))] + [("row", 1)]
    row_steps = len(sums)
    sums += [("col", 1 << b) for b in range(bits_of(col_count))]
    value = near = packed
    other = swap(send, *group_steps[0])
    top_other = swap(top_send, *top_left[0])
    after = []
    for i, step in enumerate(sums):
        value = add(value, swap(value, *step), *after)
        after = []
        if i == row_steps - 1:
            near = value
        if len(top_left) > 1:
            top_keep, top_send = fold(top_left[1], top_keep, top_other, value)
            top_left = top_left[1:]
            top_other = swap(top_send, *top_left[0])
            after.append(top_send)
        behind = i - (row_steps - 2)
        if behind == 0 or (behind >= 3 and len(group_steps) > 1):
            keep, send = fold(group_steps[1], keep, other, value)
            group_steps = group_steps[1:]
            other = swap(send, *group_steps[0])
            after.append(send)
    while len(group_steps) > 1:
        keep, send = fold(group_steps[1], keep, other, value)
        group_steps = group_steps[1:]
        other = swap(send, *group_steps[0])
    while len(top_left) > 1:
        top_keep, top_send = fold(top_left[1], top_keep, top_other, value)
        top_left = top_left[1:]
        top_other = swap(top_send, *top_left[0])
    coupling, group_modes, top_modes, token = finish(near, value, terms, group_basis, top_basis)
    assembled, top_assembled = last(keep, other, top_keep, top_other, token)
    return coupling, group_modes, top_modes, assembled, top_assembled


def solution(mesh):
    leaf = P(("row", "col"), None, None)
    group = P("col", "row", None)
    in_specs = (
        leaf, leaf, leaf, leaf, leaf, group, P(("row", "col"), None), group, P("row", None),
    )
    out_specs = (
        P(("row", "col"), None, None, None), group, P("row", None), group, P(("row", "col"), None),
    )
    return jax.shard_map(body, mesh=mesh, in_specs=in_specs, out_specs=out_specs, check_vma=False)
```

```python
import functools

import jax
import jax.numpy as jnp
from jax import lax
from jax.experimental import pallas as pl
from jax.experimental.pallas import tpu as pltpu
from jax.sharding import PartitionSpec as P

TILE = 128
SUBLANES = 8
F32 = jnp.float32
BF16 = jnp.bfloat16
VMEM = pl.BlockSpec(memory_space=pltpu.VMEM)
SMEM = pl.BlockSpec(memory_space=pltpu.SMEM)
HBM = pl.BlockSpec(memory_space=pltpu.HBM)
MASS_PARTS = 2
LEAF_MEGABYTES = 48


def params(megabytes):
    return pltpu.CompilerParams(vmem_limit_bytes=int(megabytes * 2**20))


def crossed(count, bit):
    return [(i, i ^ bit) for i in range(count)]


def rows_first(left, right):
    return lax.dot_general(left, right, (((0,), (0,)), ((), ())), preferred_element_type=F32)


def add_own(ref, own, place):
    share = own.shape[0]
    if share % SUBLANES == 0:
        window = pl.ds(pl.multiple_of(place * share, SUBLANES), share)
        ref[window, :] += own
        return
    fold = SUBLANES // share
    wide = jnp.concatenate([own] * fold, axis=0)
    line = lax.broadcasted_iota(jnp.int32, wide.shape, 0) // share
    window = pl.ds(pl.multiple_of(place // fold * SUBLANES, SUBLANES), SUBLANES)
    ref[window, :] += jnp.where(line == place % fold, wide, 0.0)


def copy_rows(target_ref, start, source_ref, place, share):
    if share % SUBLANES == 0:
        window = pl.ds(pl.multiple_of(place * share, SUBLANES), share)
        target_ref[start : start + share, :] = source_ref[window, :]
        return
    for i in range(share):
        target_ref[start + i : start + i + 1, :] = source_ref[pl.ds(place * share + i, 1), :]


def bits_of(count):
    return count.bit_length() - 1


def exchanges(half, row_count, col_count):
    row = [("row", 1)] + [("row", 1 << b) for b in range(bits_of(row_count) - 1, 0, -1)]
    col = [("col", 1 << b) for b in range(bits_of(col_count))]
    return row if half == 0 else col + row


def cut_order(half, row_count, col_count):
    steps = exchanges(half, row_count, col_count)
    order = [0]
    for axis, bit in reversed(steps):
        stride = 1 if half == 0 or axis == "col" else col_count
        order = order + [place + bit * stride for place in order]
    return order


def share_place(steps):
    place = 0
    for axis, bit in steps:
        place = 2 * place + lax.rem(lax.axis_index(axis) // bit, 2)
    return place


def leaf_kernel(half, mask_ref, map_ref, mass_hbm, modes_hbm, *refs):
    if half == 0:
        after_ref, keep_ref, send_ref, loaded_ref = refs[:4]
    else:
        fixed_hbm, first_ref, after_ref, keep_ref, send_ref, moved_ref = refs[:6]
        fixed_ref, loaded_ref = refs[-2:]
        refs = refs[:-2]
    mass_ref, modes_ref, whole_ref, partial_ref, sems = refs[-5:]
    row, col = lax.axis_index("row"), lax.axis_index("col")
    row_count, col_count = lax.axis_size("row"), lax.axis_size("col")
    rows, size = modes_ref.shape
    tiles = rows // TILE
    height = rows // MASS_PARTS

    def mass_copy(i):
        window = pl.ds(pl.multiple_of(i * height, height), height)
        return pltpu.make_async_copy(
            mass_hbm.at[0, window], mass_ref.at[window], sems.at[2 + i]
        )

    half_modes = modes_hbm.at[0, :, pl.ds(half * size, size)]
    modes_copy = pltpu.make_async_copy(half_modes, modes_ref, sems.at[0])
    modes_copy.start()
    for i in range(MASS_PARTS):
        mass_copy(i).start()
    if half == 1:
        fixed_copy = pltpu.make_async_copy(fixed_hbm.at[0], fixed_ref, sems.at[1])
        fixed_copy.start()
    modes_copy.wait()

    def part(i, first):
        mass_copy(i).wait()
        lines = []
        for a in range(height // TILE):
            pieces = []
            for b in range(tiles):
                kept = mask_ref[0, i * (height // TILE) + a, b]
                window = pl.ds(pl.multiple_of(i * height + a * TILE, TILE), TILE)
                piece = mass_ref[window, b * TILE : (b + 1) * TILE]
                pieces.append(jnp.where(kept != 0, piece, jnp.zeros_like(piece)))
            lines.append(jnp.concatenate(pieces, axis=1))
        masked = jnp.concatenate(lines, axis=0)
        loaded = jnp.dot(masked, modes_ref[...], preferred_element_type=F32).astype(BF16)
        window = pl.ds(pl.multiple_of(i * height, height), height)
        loaded_ref[window, :] = loaded
        partial = rows_first(modes_ref[window, :], loaded)
        if first:
            partial_ref[...] = partial
        else:
            partial_ref[...] += partial

    part(0, True)
    lax.fori_loop(1, MASS_PARTS, lambda i, _: part(i, False), None)

    blocks = size // TILE
    to = [pl.multiple_of(map_ref[0, half, a] * TILE, TILE) for a in range(blocks)]
    for b in range(blocks):
        for a in range(blocks):
            whole_ref[pl.ds(to[a], TILE), pl.ds(to[b], TILE)] = partial_ref[
                a * TILE : (a + 1) * TILE, b * TILE : (b + 1) * TILE
            ]
    order = cut_order(half, row_count, col_count)
    share = size // len(order)
    bit = lax.rem(row if half == 0 else col, 2)
    for k, chunk in enumerate((keep_ref, send_ref)):
        for i in range(len(order) // 2):
            step = order[i + len(order) // 2] - order[i]
            copy_rows(chunk, i * share, whole_ref, order[i] + step * lax.rem(bit + k, 2), share)
    if half == 1:
        fixed_copy.wait()
        for k, ref in enumerate((first_ref, loaded_ref)):
            projected = rows_first(fixed_ref[...], ref[...])
            for b in range(blocks):
                at = pl.multiple_of(map_ref[0, k, b] * TILE, TILE)
                moved_ref[k, :, pl.ds(at, TILE)] = projected[:, b * TILE : (b + 1) * TILE]


def leaf_half(half, tile_mask, block_map, leaf_mass, constraint_modes, more, after):
    rows, size = constraint_modes.shape[1], constraint_modes.shape[2] // 2
    outs = [jax.ShapeDtypeStruct((size // 2, size), F32)] * 2
    scratch = [
        pltpu.VMEM((rows, rows), BF16),
        pltpu.VMEM((rows, size), BF16),
        pltpu.VMEM((size, size), F32),
        pltpu.VMEM((size, size), F32),
        pltpu.SemaphoreType.DMA((2 + MASS_PARTS,)),
    ]
    if half == 0:
        outs.append(jax.ShapeDtypeStruct((rows, size), BF16))
        specs = []
    else:
        modes = more[0].shape[2]
        outs.append(jax.ShapeDtypeStruct((2, modes, size), F32))
        scratch += [pltpu.VMEM((rows, modes), BF16), pltpu.VMEM((rows, size), BF16)]
        specs = [HBM, VMEM]
    return pl.pallas_call(
        functools.partial(leaf_kernel, half),
        in_specs=[SMEM] * 2 + [HBM] * 2 + specs + [pl.BlockSpec(memory_space=pl.ANY)],
        out_specs=[VMEM] * len(outs),
        out_shape=outs,
        scratch_shapes=scratch,
        compiler_params=params(LEAF_MEGABYTES),
        cost_estimate=pl.CostEstimate(
            flops=2 * rows * size * (rows + size),
            bytes_accessed=2 * rows * (rows + size) + 8 * size * size,
            transcendentals=0,
        ),
        name="leaf_group" if half == 0 else "leaf_top",
    )(tile_mask, block_map, leaf_mass, constraint_modes, *more, after)


def split(value):
    high = value.astype(BF16)
    return high, (value - high.astype(F32)).astype(BF16)


def three_pass(left, right, turn=False):
    (left_high, left_low), (right_high, right_low) = left, right
    multiply = rows_first if turn else functools.partial(jnp.dot, preferred_element_type=F32)
    width = right_high.shape[1]
    both = multiply(left_high, jnp.concatenate([right_high, right_low], axis=1))
    return both[:, :width] + both[:, width:] + multiply(left_low, right_high)


def halve(step, keep_ref, other_ref, next_ref, send_ref):
    axis, bit = step
    height = next_ref.shape[0]
    mine = lax.rem(lax.axis_index(axis) // bit, 2) == 1
    low = keep_ref[:height, :] + other_ref[:height, :]
    high = keep_ref[height:, :] + other_ref[height:, :]
    next_ref[...] = jnp.where(mine, high, low)
    send_ref[...] = jnp.where(mine, low, high)


def prepare_kernel(
    count, keep_in, send_ref, top_keep_in, top_send_ref, moved_ref, group_own_ref,
    top_own_ref, *refs,
):
    pieces = refs[1 : count + 1]
    (
        packed_ref, terms_ref, keep_ref, top_keep_ref, top_next_ref, bases_ref
    ) = refs[count + 1 :]
    modes = terms_ref.shape[2]
    size = bases_ref.shape[0]
    row, col = lax.axis_index("row"), lax.axis_index("col")
    row_count, col_count = lax.axis_size("row"), lax.axis_size("col")
    group_steps = exchanges(0, row_count, col_count)
    top_steps = exchanges(1, row_count, col_count)
    keep_ref[...] = keep_in[...]
    add_own(keep_ref, group_own_ref[0], share_place(group_steps[1:]))
    top_keep_ref[...] = top_keep_in[...]
    add_own(top_keep_ref, top_own_ref[...], share_place(top_steps[1:]))
    top_next_ref[...] = top_send_ref[...]
    line = size // row_count
    for k, piece in enumerate(pieces):
        pair = lax.bitwise_xor(row // 2, k)
        for i in range(2):
            at = (2 * pair + lax.rem(row + i, 2)) * line
            bases_ref[pl.ds(pl.multiple_of(at, line), line), :] = piece[i * line : (i + 1) * line, :]
    grams = []
    for half in range(2):
        lanes = slice(half * modes, (half + 1) * modes)
        basis = split(bases_ref[:, lanes])
        order = cut_order(half, row_count, col_count)
        share = size // len(order)
        lower = jnp.concatenate(
            [bases_ref[at * share : (at + 1) * share, lanes] for at in order[: len(order) // 2]], axis=0
        )
        upper = jnp.concatenate(
            [bases_ref[at * share : (at + 1) * share, lanes] for at in order[len(order) // 2 :]], axis=0
        )
        swap = lax.rem((row, col)[half], 2) == 1
        ordered = jnp.concatenate(
            [jnp.where(swap, upper, lower), jnp.where(swap, lower, upper)], axis=0
        )
        parts = ((keep_ref, send_ref), (top_keep_ref, top_send_ref))[half]
        matrix = jnp.concatenate([part[...] for part in parts], axis=0)
        applied = three_pass(split(matrix), basis)
        gram = three_pass(split(ordered), split(applied), turn=True)
        grams.append(0.5 * (gram + gram.T))
        terms_ref[half] = three_pass(split(moved_ref[half]), basis)
    down = lax.broadcasted_iota(jnp.int32, (modes, modes), 0)
    across = lax.broadcasted_iota(jnp.int32, (modes, modes), 1)
    packed_ref[:modes, :] = jnp.where(down >= across, grams[0], grams[1])
    diagonal = jnp.sum(jnp.where(down == across, grams[1], 0.0), axis=0, keepdims=True)
    packed_ref[modes:, :] = jnp.broadcast_to(diagonal, (SUBLANES, modes))


def prepare(keep, send, top_keep, top_send, moved, group_own, top_own, after, pieces):
    _, modes, size = moved.shape
    half = jax.ShapeDtypeStruct(keep.shape, F32)
    return pl.pallas_call(
        functools.partial(prepare_kernel, len(pieces)),
        in_specs=[VMEM] * 7 + [pl.BlockSpec(memory_space=pl.ANY)] + [VMEM] * len(pieces),
        out_specs=[VMEM] * 5,
        out_shape=[
            jax.ShapeDtypeStruct((modes + SUBLANES, modes), F32),
            jax.ShapeDtypeStruct((2, modes, modes), F32),
            half,
            half,
            half,
        ],
        scratch_shapes=[pltpu.VMEM((size, 2 * modes), F32)],
        compiler_params=params(32),
        cost_estimate=pl.CostEstimate(
            flops=12 * size * size * modes, bytes_accessed=12 * size * size, transcendentals=0
        ),
        name="prepare",
    )(keep, send, top_keep, top_send, moved, group_own, top_own, after, *pieces)


def fold_kernel(step, after_count, keep_ref, other_ref, *refs):
    halve(step, keep_ref, other_ref, *refs[after_count:])


def fold(step, keep, other, *after):
    part = jax.ShapeDtypeStruct((keep.shape[0] // 2, keep.shape[1]), F32)
    return pl.pallas_call(
        functools.partial(fold_kernel, step, len(after)),
        in_specs=[VMEM] * 2 + [pl.BlockSpec(memory_space=pl.ANY)] * len(after),
        out_specs=[VMEM] * 2,
        out_shape=[part, part],
        compiler_params=params(16),
        cost_estimate=pl.CostEstimate(flops=1, bytes_accessed=1, transcendentals=0),
        name="fold",
    )(keep, other, *after)


def add_kernel(left_ref, right_ref, *refs):
    refs[-1][...] = left_ref[...] + right_ref[...]


def add(left, right, *after):
    return pl.pallas_call(
        add_kernel,
        in_specs=[VMEM] * 2 + [pl.BlockSpec(memory_space=pl.ANY)] * len(after),
        out_specs=VMEM,
        out_shape=jax.ShapeDtypeStruct(left.shape, F32),
        compiler_params=params(16),
        cost_estimate=pl.CostEstimate(flops=1, bytes_accessed=1, transcendentals=0),
        name="add",
    )(left, right, *after)


def last_kernel(keep_ref, other_ref, top_keep_ref, top_other_ref, after_ref, group_ref, top_ref):
    size = group_ref.shape[2]
    group_ref[0] = size * (keep_ref[...] + other_ref[...])
    top_ref[...] = size * (top_keep_ref[...] + top_other_ref[...])


def last(keep, other, top_keep, top_other, after):
    return pl.pallas_call(
        last_kernel,
        in_specs=[VMEM] * 4 + [pl.BlockSpec(memory_space=pl.ANY)],
        out_specs=[VMEM] * 2,
        out_shape=[
            jax.ShapeDtypeStruct((1,) + keep.shape, F32),
            jax.ShapeDtypeStruct(top_keep.shape, F32),
        ],
        compiler_params=params(16),
        cost_estimate=pl.CostEstimate(flops=1, bytes_accessed=1, transcendentals=0),
        name="last",
    )(keep, other, top_keep, top_other, after)


def factor(matrices):
    size = matrices[0].shape[0]
    width = SUBLANES
    down = lax.broadcasted_iota(jnp.int32, (size, size), 0)
    across = lax.broadcasted_iota(jnp.int32, (size, size), 1)
    line = lax.broadcasted_iota(jnp.int32, (width, size), 0)
    lane = lax.broadcasted_iota(jnp.int32, (width, size), 1)
    states = list(matrices)
    diagonals = [[] for _ in matrices]
    for start in range(0, size, width):
        stop = start + width
        for m, state in enumerate(states):
            spread = [
                jnp.broadcast_to(state[:, start + q : start + q + 1], (size, size))
                for q in range(width)
            ]
            strip = state[start:stop, :]
            small = [s[start:stop, :] for s in spread]
            scaled = []
            rest = strip
            for q in range(width):
                scale = lax.rsqrt(small[q][q : q + 1, :])
                tail = [small[t][q : q + 1, :] * scale for t in range(q + 1, width)]
                level = rest[q : q + 1, :] * scale
                rest = rest - small[q] * (scale * level)
                small[q] = jnp.where(line == q, 1.0, small[q]) * scale
                for t in range(q + 1, width):
                    small[t] = jnp.where(line == q, 0.0, small[t]) - small[q] * tail[t - q - 1]
                scaled.append(level)
            small = [jnp.where(line <= q, s, 0.0) for q, s in enumerate(small)]
            solved = small[0] * scaled[0]
            for q in range(1, width):
                solved = solved + small[q] * scaled[q]
            solved = jnp.where(lane >= stop, solved, 0.0)
            update = spread[0] * solved[0:1, :]
            for q in range(1, width):
                update = update + spread[q] * solved[q : q + 1, :]
            block = jnp.where(lane == line + start, 1.0, 0.0)
            kept = jnp.where(lane < start, strip, block) - solved
            parts = []
            if start > 0:
                parts.append(state[:start] - update[:start])
            parts.append(kept)
            if stop < size:
                parts.append(state[stop:] - update[stop:])
            states[m] = jnp.concatenate(parts, axis=0)
            diagonal = jnp.zeros((width, size), F32)
            for q in range(width):
                diagonal = jnp.where(lane == start + q, small[q], diagonal)
            diagonals[m].append(diagonal)
    uppers = [jnp.where(across >= down, state, 0.0) for state in states]
    return uppers, [jnp.concatenate(d, axis=0) for d in diagonals]


def finish_kernel(
    near_ref, far_ref, terms_ref, group_basis_ref, top_basis_ref, coupling_ref, group_ref, top_ref,
    token_ref,
):
    modes = near_ref.shape[1]
    down = lax.broadcasted_iota(jnp.int32, (modes, modes), 0)
    across = lax.broadcasted_iota(jnp.int32, (modes, modes), 1)
    near, far = near_ref[:modes, :], far_ref[:modes, :]
    group = jnp.where(down >= across, near, near.T)
    top = jnp.where(down > across, far.T, far)
    diagonal = jnp.broadcast_to(far_ref[modes : modes + 1, :], top.shape)
    top = jnp.where(down == across, diagonal, top)
    uppers, diagonals = factor([group, top])
    for half in range(2):
        inverse = split(three_pass(split(uppers[half]), split(diagonals[half])))
        basis = (group_basis_ref[0], top_basis_ref[...])[half]
        left = jnp.concatenate([terms_ref[half], basis], axis=0)
        result = three_pass(split(left), inverse)
        coupling_ref[0, :, half, :] = result[:modes]
        if half == 0:
            group_ref[0] = result[modes:]
        else:
            top_ref[...] = result[modes:]
            token_ref[...] = result[:SUBLANES]


def finish(near, far, terms, group_basis, top_basis):
    modes = near.shape[1]
    return pl.pallas_call(
        finish_kernel,
        in_specs=[VMEM] * 5,
        out_specs=[VMEM] * 4,
        out_shape=[
            jax.ShapeDtypeStruct((1, modes, 2, modes), F32),
            jax.ShapeDtypeStruct(group_basis.shape, F32),
            jax.ShapeDtypeStruct(top_basis.shape, F32),
            jax.ShapeDtypeStruct((SUBLANES, modes), F32),
        ],
        compiler_params=params(32),
        cost_estimate=pl.CostEstimate(
            flops=20 * modes**3, bytes_accessed=24 * modes * modes, transcendentals=2 * modes
        ),
        name="finish",
    )(near, far, terms, group_basis, top_basis)


def body(
    leaf_mass, tile_mask, constraint_modes, leaf_fixed_modes, block_map, group_mass, top_mass,
    group_basis, top_basis,
):
    row_count, col_count = lax.axis_size("row"), lax.axis_size("col")
    sizes = {"row": row_count, "col": col_count}

    def swap(value, axis, bit):
        return lax.ppermute(value, axis, crossed(sizes[axis], bit))

    def half_of(half, more, after):
        return leaf_half(half, tile_mask, block_map, leaf_mass, constraint_modes, more, after)

    group_steps = exchanges(0, row_count, col_count)
    basis = jnp.concatenate([group_basis[0], top_basis], axis=1)
    beside = swap(basis, "row", 1)
    keep, send, loaded = half_of(0, [], basis)
    pair = jnp.concatenate([basis, beside], axis=0)
    pieces = [pair] + [swap(pair, "row", 2 * k) for k in range(1, row_count // 2)]
    other = swap(send, *group_steps[0])
    top_keep, top_send, moved = half_of(1, [leaf_fixed_modes, loaded], pair)
    packed, terms, keep, top_keep, top_send = prepare(
        keep, send, top_keep, top_send, moved, group_mass, top_mass, other, pieces
    )
    top_left = exchanges(1, row_count, col_count)
    sums = [("row", 1 << b) for b in range(1, bits_of(row_count))] + [("row", 1)]
    row_steps = len(sums)
    sums += [("col", 1 << b) for b in range(bits_of(col_count))]
    value = near = packed
    top_other = swap(top_send, *top_left[0])
    after = []
    for i, step in enumerate(sums):
        value = add(value, swap(value, *step), *after)
        after = []
        if i == row_steps - 1:
            near = value
        if len(top_left) > 2:
            top_keep, top_send = fold(top_left[1], top_keep, top_other, value)
            top_left = top_left[1:]
            top_other = swap(top_send, *top_left[0])
            after.append(top_send)
        if i == row_steps - 2:
            keep, send = fold(group_steps[1], keep, other, value)
            group_steps = group_steps[1:]
            other = swap(send, *group_steps[0])
            after.append(send)
    coupling, group_modes, top_modes, token = finish(near, value, terms, group_basis, top_basis)
    while len(group_steps) > 1:
        keep, send = fold(group_steps[1], keep, other, token)
        group_steps = group_steps[1:]
        other = swap(send, *group_steps[0])
    while len(top_left) > 1:
        top_keep, top_send = fold(top_left[1], top_keep, top_other, token)
        top_left = top_left[1:]
        top_other = swap(top_send, *top_left[0])
    assembled, top_assembled = last(keep, other, top_keep, top_other, token)
    return coupling, group_modes, top_modes, assembled, top_assembled


def solution(mesh):
    leaf = P(("row", "col"), None, None)
    group = P("col", "row", None)
    in_specs = (
        leaf, leaf, leaf, leaf, leaf, group, P(("row", "col"), None), group, P("row", None),
    )
    out_specs = (
        P(("row", "col"), None, None, None), group, P("row", None), group, P(("row", "col"), None),
    )
    return jax.shard_map(body, mesh=mesh, in_specs=in_specs, out_specs=out_specs, check_vma=False)
```

```python
import functools

import jax
import jax.numpy as jnp
from jax import lax
from jax.experimental import pallas as pl
from jax.experimental.pallas import tpu as pltpu
from jax.sharding import PartitionSpec as P

TILE = 128
SUBLANES = 8
F32 = jnp.float32
BF16 = jnp.bfloat16
VMEM = pl.BlockSpec(memory_space=pltpu.VMEM)
SMEM = pl.BlockSpec(memory_space=pltpu.SMEM)
HBM = pl.BlockSpec(memory_space=pltpu.HBM)
MASS_PARTS = 2
LEAF_MEGABYTES = 48


def params(megabytes):
    return pltpu.CompilerParams(vmem_limit_bytes=int(megabytes * 2**20))


def crossed(count, bit):
    return [(i, i ^ bit) for i in range(count)]


def rows_first(left, right):
    return lax.dot_general(left, right, (((0,), (0,)), ((), ())), preferred_element_type=F32)


def add_own(ref, own, place):
    share = own.shape[0]
    if share % SUBLANES == 0:
        window = pl.ds(pl.multiple_of(place * share, SUBLANES), share)
        ref[window, :] += own
        return
    fold = SUBLANES // share
    wide = jnp.concatenate([own] * fold, axis=0)
    line = lax.broadcasted_iota(jnp.int32, wide.shape, 0) // share
    window = pl.ds(pl.multiple_of(place // fold * SUBLANES, SUBLANES), SUBLANES)
    ref[window, :] += jnp.where(line == place % fold, wide, 0.0)


def copy_rows(target_ref, start, source_ref, place, share):
    if share % SUBLANES == 0:
        window = pl.ds(pl.multiple_of(place * share, SUBLANES), share)
        target_ref[start : start + share, :] = source_ref[window, :]
        return
    for i in range(share):
        target_ref[start + i : start + i + 1, :] = source_ref[pl.ds(place * share + i, 1), :]


def bits_of(count):
    return count.bit_length() - 1


def exchanges(half, row_count, col_count):
    row = [("row", 1)] + [("row", 1 << b) for b in range(bits_of(row_count) - 1, 0, -1)]
    col = [("col", 1 << b) for b in range(bits_of(col_count))]
    return row if half == 0 else col + row


def cut_order(half, row_count, col_count):
    steps = exchanges(half, row_count, col_count)
    order = [0]
    for axis, bit in reversed(steps):
        stride = 1 if half == 0 or axis == "col" else col_count
        order = order + [place + bit * stride for place in order]
    return order


def share_place(steps):
    place = 0
    for axis, bit in steps:
        place = 2 * place + lax.rem(lax.axis_index(axis) // bit, 2)
    return place


def leaf_kernel(half, mask_ref, map_ref, mass_hbm, modes_hbm, *refs):
    if half == 0:
        after_ref, keep_ref, send_ref, loaded_ref = refs[:4]
    else:
        fixed_hbm, first_ref, after_ref, keep_ref, send_ref, moved_ref = refs[:6]
        fixed_ref, loaded_ref = refs[-2:]
        refs = refs[:-2]
    mass_ref, modes_ref, whole_ref, partial_ref, sems = refs[-5:]
    row, col = lax.axis_index("row"), lax.axis_index("col")
    row_count, col_count = lax.axis_size("row"), lax.axis_size("col")
    rows, size = modes_ref.shape
    tiles = rows // TILE
    height = rows // MASS_PARTS

    def mass_copy(i):
        window = pl.ds(pl.multiple_of(i * height, height), height)
        return pltpu.make_async_copy(
            mass_hbm.at[0, window], mass_ref.at[window], sems.at[2 + i]
        )

    half_modes = modes_hbm.at[0, :, pl.ds(half * size, size)]
    modes_copy = pltpu.make_async_copy(half_modes, modes_ref, sems.at[0])
    modes_copy.start()
    for i in range(MASS_PARTS):
        mass_copy(i).start()
    if half == 1:
        fixed_copy = pltpu.make_async_copy(fixed_hbm.at[0], fixed_ref, sems.at[1])
        fixed_copy.start()
    modes_copy.wait()

    def part(i, first):
        mass_copy(i).wait()
        lines = []
        for a in range(height // TILE):
            pieces = []
            for b in range(tiles):
                kept = mask_ref[0, i * (height // TILE) + a, b]
                window = pl.ds(pl.multiple_of(i * height + a * TILE, TILE), TILE)
                piece = mass_ref[window, b * TILE : (b + 1) * TILE]
                pieces.append(jnp.where(kept != 0, piece, jnp.zeros_like(piece)))
            lines.append(jnp.concatenate(pieces, axis=1))
        masked = jnp.concatenate(lines, axis=0)
        loaded = jnp.dot(masked, modes_ref[...], preferred_element_type=F32).astype(BF16)
        window = pl.ds(pl.multiple_of(i * height, height), height)
        loaded_ref[window, :] = loaded
        partial = rows_first(modes_ref[window, :], loaded)
        if first:
            partial_ref[...] = partial
        else:
            partial_ref[...] += partial

    part(0, True)
    lax.fori_loop(1, MASS_PARTS, lambda i, _: part(i, False), None)

    blocks = size // TILE
    to = [pl.multiple_of(map_ref[0, half, a] * TILE, TILE) for a in range(blocks)]
    for b in range(blocks):
        for a in range(blocks):
            whole_ref[pl.ds(to[a], TILE), pl.ds(to[b], TILE)] = partial_ref[
                a * TILE : (a + 1) * TILE, b * TILE : (b + 1) * TILE
            ]
    order = cut_order(half, row_count, col_count)
    share = size // len(order)
    bit = lax.rem(row if half == 0 else col, 2)
    for k, chunk in enumerate((keep_ref, send_ref)):
        for i in range(len(order) // 2):
            step = order[i + len(order) // 2] - order[i]
            copy_rows(chunk, i * share, whole_ref, order[i] + step * lax.rem(bit + k, 2), share)
    if half == 1:
        fixed_copy.wait()
        for k, ref in enumerate((first_ref, loaded_ref)):
            projected = rows_first(fixed_ref[...], ref[...])
            for b in range(blocks):
                at = pl.multiple_of(map_ref[0, k, b] * TILE, TILE)
                moved_ref[k, :, pl.ds(at, TILE)] = projected[:, b * TILE : (b + 1) * TILE]


def leaf_half(half, tile_mask, block_map, leaf_mass, constraint_modes, more, after):
    rows, size = constraint_modes.shape[1], constraint_modes.shape[2] // 2
    outs = [jax.ShapeDtypeStruct((size // 2, size), F32)] * 2
    scratch = [
        pltpu.VMEM((rows, rows), BF16),
        pltpu.VMEM((rows, size), BF16),
        pltpu.VMEM((size, size), F32),
        pltpu.VMEM((size, size), F32),
        pltpu.SemaphoreType.DMA((2 + MASS_PARTS,)),
    ]
    if half == 0:
        outs.append(jax.ShapeDtypeStruct((rows, size), BF16))
        specs = []
    else:
        modes = more[0].shape[2]
        outs.append(jax.ShapeDtypeStruct((2, modes, size), F32))
        scratch += [pltpu.VMEM((rows, modes), BF16), pltpu.VMEM((rows, size), BF16)]
        specs = [HBM, VMEM]
    return pl.pallas_call(
        functools.partial(leaf_kernel, half),
        in_specs=[SMEM] * 2 + [HBM] * 2 + specs + [pl.BlockSpec(memory_space=pl.ANY)],
        out_specs=[VMEM] * len(outs),
        out_shape=outs,
        scratch_shapes=scratch,
        compiler_params=params(LEAF_MEGABYTES),
        cost_estimate=pl.CostEstimate(
            flops=2 * rows * size * (rows + size),
            bytes_accessed=2 * rows * (rows + size) + 8 * size * size,
            transcendentals=0,
        ),
        name="leaf_group" if half == 0 else "leaf_top",
    )(tile_mask, block_map, leaf_mass, constraint_modes, *more, after)


def split(value):
    high = value.astype(BF16)
    return high, (value - high.astype(F32)).astype(BF16)


def three_pass(left, right, turn=False):
    (left_high, left_low), (right_high, right_low) = left, right
    multiply = rows_first if turn else functools.partial(jnp.dot, preferred_element_type=F32)
    width = right_high.shape[1]
    both = multiply(left_high, jnp.concatenate([right_high, right_low], axis=1))
    return both[:, :width] + both[:, width:] + multiply(left_low, right_high)


def halve(step, keep_ref, other_ref, next_ref, send_ref):
    axis, bit = step
    height = next_ref.shape[0]
    mine = lax.rem(lax.axis_index(axis) // bit, 2) == 1
    low = keep_ref[:height, :] + other_ref[:height, :]
    high = keep_ref[height:, :] + other_ref[height:, :]
    next_ref[...] = jnp.where(mine, high, low)
    send_ref[...] = jnp.where(mine, low, high)


def prepare_kernel(
    count, keep_in, send_ref, top_keep_in, top_send_ref, moved_ref, group_own_ref,
    top_own_ref, *refs,
):
    pieces = refs[1 : count + 1]
    (
        packed_ref, terms_ref, keep_ref, top_keep_ref, top_next_ref, bases_ref
    ) = refs[count + 1 :]
    modes = terms_ref.shape[2]
    size = bases_ref.shape[0]
    row, col = lax.axis_index("row"), lax.axis_index("col")
    row_count, col_count = lax.axis_size("row"), lax.axis_size("col")
    group_steps = exchanges(0, row_count, col_count)
    top_steps = exchanges(1, row_count, col_count)
    keep_ref[...] = keep_in[...]
    add_own(keep_ref, group_own_ref[0], share_place(group_steps[1:]))
    top_keep_ref[...] = top_keep_in[...]
    add_own(top_keep_ref, top_own_ref[...], share_place(top_steps[1:]))
    top_next_ref[...] = top_send_ref[...]
    line = size // row_count
    for k, piece in enumerate(pieces):
        pair = lax.bitwise_xor(row // 2, k)
        for i in range(2):
            at = (2 * pair + lax.rem(row + i, 2)) * line
            bases_ref[pl.ds(pl.multiple_of(at, line), line), :] = piece[i * line : (i + 1) * line, :]
    grams = []
    for half in range(2):
        lanes = slice(half * modes, (half + 1) * modes)
        basis = split(bases_ref[:, lanes])
        order = cut_order(half, row_count, col_count)
        share = size // len(order)
        lower = jnp.concatenate(
            [bases_ref[at * share : (at + 1) * share, lanes] for at in order[: len(order) // 2]], axis=0
        )
        upper = jnp.concatenate(
            [bases_ref[at * share : (at + 1) * share, lanes] for at in order[len(order) // 2 :]], axis=0
        )
        swap = lax.rem((row, col)[half], 2) == 1
        ordered = jnp.concatenate(
            [jnp.where(swap, upper, lower), jnp.where(swap, lower, upper)], axis=0
        )
        parts = ((keep_ref, send_ref), (top_keep_ref, top_send_ref))[half]
        matrix = jnp.concatenate([part[...] for part in parts], axis=0)
        applied = three_pass(split(matrix), basis)
        gram = three_pass(split(ordered), split(applied), turn=True)
        grams.append(0.5 * (gram + gram.T))
        terms_ref[half] = three_pass(split(moved_ref[half]), basis)
    down = lax.broadcasted_iota(jnp.int32, (modes, modes), 0)
    across = lax.broadcasted_iota(jnp.int32, (modes, modes), 1)
    packed_ref[:modes, :] = jnp.where(down >= across, grams[0], grams[1])
    diagonal = jnp.sum(jnp.where(down == across, grams[1], 0.0), axis=0, keepdims=True)
    packed_ref[modes:, :] = jnp.broadcast_to(diagonal, (SUBLANES, modes))


def prepare(keep, send, top_keep, top_send, moved, group_own, top_own, after, pieces):
    _, modes, size = moved.shape
    half = jax.ShapeDtypeStruct(keep.shape, F32)
    return pl.pallas_call(
        functools.partial(prepare_kernel, len(pieces)),
        in_specs=[VMEM] * 7 + [pl.BlockSpec(memory_space=pl.ANY)] + [VMEM] * len(pieces),
        out_specs=[VMEM] * 5,
        out_shape=[
            jax.ShapeDtypeStruct((modes + SUBLANES, modes), F32),
            jax.ShapeDtypeStruct((2, modes, modes), F32),
            half,
            half,
            half,
        ],
        scratch_shapes=[pltpu.VMEM((size, 2 * modes), F32)],
        compiler_params=params(32),
        cost_estimate=pl.CostEstimate(
            flops=12 * size * size * modes, bytes_accessed=12 * size * size, transcendentals=0
        ),
        name="prepare",
    )(keep, send, top_keep, top_send, moved, group_own, top_own, after, *pieces)


def fold_kernel(step, after_count, keep_ref, other_ref, *refs):
    halve(step, keep_ref, other_ref, *refs[after_count:])


def fold(step, keep, other, *after):
    part = jax.ShapeDtypeStruct((keep.shape[0] // 2, keep.shape[1]), F32)
    return pl.pallas_call(
        functools.partial(fold_kernel, step, len(after)),
        in_specs=[VMEM] * 2 + [pl.BlockSpec(memory_space=pl.ANY)] * len(after),
        out_specs=[VMEM] * 2,
        out_shape=[part, part],
        compiler_params=params(16),
        cost_estimate=pl.CostEstimate(flops=1, bytes_accessed=1, transcendentals=0),
        name="fold",
    )(keep, other, *after)


def add_kernel(left_ref, right_ref, *refs):
    refs[-1][...] = left_ref[...] + right_ref[...]


def add(left, right, *after):
    return pl.pallas_call(
        add_kernel,
        in_specs=[VMEM] * 2 + [pl.BlockSpec(memory_space=pl.ANY)] * len(after),
        out_specs=VMEM,
        out_shape=jax.ShapeDtypeStruct(left.shape, F32),
        compiler_params=params(16),
        cost_estimate=pl.CostEstimate(flops=1, bytes_accessed=1, transcendentals=0),
        name="add",
    )(left, right, *after)


def last_kernel(keep_ref, other_ref, top_keep_ref, top_other_ref, after_ref, group_ref, top_ref):
    size = group_ref.shape[2]
    group_ref[0] = size * (keep_ref[...] + other_ref[...])
    top_ref[...] = size * (top_keep_ref[...] + top_other_ref[...])


def last(keep, other, top_keep, top_other, after):
    return pl.pallas_call(
        last_kernel,
        in_specs=[VMEM] * 4 + [pl.BlockSpec(memory_space=pl.ANY)],
        out_specs=[VMEM] * 2,
        out_shape=[
            jax.ShapeDtypeStruct((1,) + keep.shape, F32),
            jax.ShapeDtypeStruct(top_keep.shape, F32),
        ],
        compiler_params=params(16),
        cost_estimate=pl.CostEstimate(flops=1, bytes_accessed=1, transcendentals=0),
        name="last",
    )(keep, other, top_keep, top_other, after)


def factor(matrices):
    size = matrices[0].shape[0]
    width = SUBLANES
    down = lax.broadcasted_iota(jnp.int32, (size, size), 0)
    across = lax.broadcasted_iota(jnp.int32, (size, size), 1)
    line = lax.broadcasted_iota(jnp.int32, (width, size), 0)
    lane = lax.broadcasted_iota(jnp.int32, (width, size), 1)
    states = list(matrices)
    diagonals = [[] for _ in matrices]
    for start in range(0, size, width):
        stop = start + width
        for m, state in enumerate(states):
            spread = [
                jnp.broadcast_to(state[:, start + q : start + q + 1], (size, size))
                for q in range(width)
            ]
            strip = state[start:stop, :]
            small = [s[start:stop, :] for s in spread]
            scaled = []
            rest = strip
            for q in range(width):
                scale = lax.rsqrt(small[q][q : q + 1, :])
                tail = [small[t][q : q + 1, :] * scale for t in range(q + 1, width)]
                level = rest[q : q + 1, :] * scale
                rest = rest - small[q] * (scale * level)
                small[q] = jnp.where(line == q, 1.0, small[q]) * scale
                for t in range(q + 1, width):
                    small[t] = jnp.where(line == q, 0.0, small[t]) - small[q] * tail[t - q - 1]
                scaled.append(level)
            small = [jnp.where(line <= q, s, 0.0) for q, s in enumerate(small)]
            solved = small[0] * scaled[0]
            for q in range(1, width):
                solved = solved + small[q] * scaled[q]
            solved = jnp.where(lane >= stop, solved, 0.0)
            update = spread[0] * solved[0:1, :]
            for q in range(1, width):
                update = update + spread[q] * solved[q : q + 1, :]
            block = jnp.where(lane == line + start, 1.0, 0.0)
            kept = jnp.where(lane < start, strip, block) - solved
            parts = []
            if start > 0:
                parts.append(state[:start] - update[:start])
            parts.append(kept)
            if stop < size:
                parts.append(state[stop:] - update[stop:])
            states[m] = jnp.concatenate(parts, axis=0)
            diagonal = jnp.zeros((width, size), F32)
            for q in range(width):
                diagonal = jnp.where(lane == start + q, small[q], diagonal)
            diagonals[m].append(diagonal)
    uppers = [jnp.where(across >= down, state, 0.0) for state in states]
    return uppers, [jnp.concatenate(d, axis=0) for d in diagonals]


def finish_kernel(
    near_ref, far_ref, terms_ref, group_basis_ref, top_basis_ref, coupling_ref, group_ref, top_ref,
    token_ref,
):
    modes = near_ref.shape[1]
    down = lax.broadcasted_iota(jnp.int32, (modes, modes), 0)
    across = lax.broadcasted_iota(jnp.int32, (modes, modes), 1)
    near, far = near_ref[:modes, :], far_ref[:modes, :]
    group = jnp.where(down >= across, near, near.T)
    top = jnp.where(down > across, far.T, far)
    diagonal = jnp.broadcast_to(far_ref[modes : modes + 1, :], top.shape)
    top = jnp.where(down == across, diagonal, top)
    uppers, diagonals = factor([group, top])
    for half in range(2):
        inverse = split(three_pass(split(uppers[half]), split(diagonals[half])))
        basis = (group_basis_ref[0], top_basis_ref[...])[half]
        left = jnp.concatenate([terms_ref[half], basis], axis=0)
        result = three_pass(split(left), inverse)
        coupling_ref[0, :, half, :] = result[:modes]
        if half == 0:
            group_ref[0] = result[modes:]
        else:
            top_ref[...] = result[modes:]
            token_ref[...] = result[:SUBLANES]


def finish(near, far, terms, group_basis, top_basis):
    modes = near.shape[1]
    return pl.pallas_call(
        finish_kernel,
        in_specs=[VMEM] * 5,
        out_specs=[VMEM] * 4,
        out_shape=[
            jax.ShapeDtypeStruct((1, modes, 2, modes), F32),
            jax.ShapeDtypeStruct(group_basis.shape, F32),
            jax.ShapeDtypeStruct(top_basis.shape, F32),
            jax.ShapeDtypeStruct((SUBLANES, modes), F32),
        ],
        compiler_params=params(32),
        cost_estimate=pl.CostEstimate(
            flops=20 * modes**3, bytes_accessed=24 * modes * modes, transcendentals=2 * modes
        ),
        name="finish",
    )(near, far, terms, group_basis, top_basis)


def body(
    leaf_mass, tile_mask, constraint_modes, leaf_fixed_modes, block_map, group_mass, top_mass,
    group_basis, top_basis,
):
    row_count, col_count = lax.axis_size("row"), lax.axis_size("col")
    sizes = {"row": row_count, "col": col_count}

    def swap(value, axis, bit):
        return lax.ppermute(value, axis, crossed(sizes[axis], bit))

    def half_of(half, more, after):
        return leaf_half(half, tile_mask, block_map, leaf_mass, constraint_modes, more, after)

    group_steps = exchanges(0, row_count, col_count)
    basis = jnp.concatenate([group_basis[0], top_basis], axis=1)
    beside = swap(basis, "row", 1)
    keep, send, loaded = half_of(0, [], basis)
    pair = jnp.concatenate([basis, beside], axis=0)
    pieces = [pair] + [swap(pair, "row", 2 * k) for k in range(1, row_count // 2)]
    other = swap(send, *group_steps[0])
    top_keep, top_send, moved = half_of(1, [leaf_fixed_modes, loaded], pair)
    packed, terms, keep, top_keep, top_send = prepare(
        keep, send, top_keep, top_send, moved, group_mass, top_mass, other, pieces
    )
    top_left = exchanges(1, row_count, col_count)
    sums = [("row", 1 << b) for b in range(1, bits_of(row_count))] + [("row", 1)]
    row_steps = len(sums)
    sums += [("col", 1 << b) for b in range(bits_of(col_count))]
    value = near = packed
    top_other = swap(top_send, *top_left[0])
    after = []
    for i, step in enumerate(sums):
        value = add(value, swap(value, *step), *after)
        after = []
        if i == row_steps - 1:
            near = value
        if len(top_left) > 1:
            top_keep, top_send = fold(top_left[1], top_keep, top_other, value)
            top_left = top_left[1:]
            top_other = swap(top_send, *top_left[0])
            after.append(top_send)
        behind = i - (row_steps - 2)
        if behind == 0 or (behind >= 3 and len(group_steps) > 1):
            keep, send = fold(group_steps[1], keep, other, value)
            group_steps = group_steps[1:]
            other = swap(send, *group_steps[0])
            after.append(send)
    while len(group_steps) > 1:
        keep, send = fold(group_steps[1], keep, other, value)
        group_steps = group_steps[1:]
        other = swap(send, *group_steps[0])
    while len(top_left) > 1:
        top_keep, top_send = fold(top_left[1], top_keep, top_other, value)
        top_left = top_left[1:]
        top_other = swap(top_send, *top_left[0])
    coupling, group_modes, top_modes, token = finish(near, value, terms, group_basis, top_basis)
    assembled, top_assembled = last(keep, other, top_keep, top_other, token)
    return coupling, group_modes, top_modes, assembled, top_assembled


def solution(mesh):
    leaf = P(("row", "col"), None, None)
    group = P("col", "row", None)
    in_specs = (
        leaf, leaf, leaf, leaf, leaf, group, P(("row", "col"), None), group, P("row", None),
    )
    out_specs = (
        P(("row", "col"), None, None, None), group, P("row", None), group, P(("row", "col"), None),
    )
    return jax.shard_map(body, mesh=mesh, in_specs=in_specs, out_specs=out_specs, check_vma=False)
```
